32 devices in a mesh: dp: 16 (over z, x, core), mp: 2 (over y).
Axes of the slice: x: 2, y: 2, z: 4, core: 2. Of those that a mesh axis runs over, the one named last changes fastest.
Arguments:
- tokens: float32 [16384, 768], P('dp'), may hold values from -6 to 6
- conditioning: float32 [64, 768], P('dp'), may hold values from -5 to 5
- sigmas: float32 [64], P('dp'), may hold values from 0.07 to 3.3
- positions: int32 [64, 2, 256], P('dp'), may hold values from 0 to 15, as said below
- cotangent: bfloat16 [16384, 768], P('dp'), may hold values from -6 to 6
- owners: int32 [2, 180], P('mp'), may hold values from 0 to 15, as said below
- master: float32 [2, 192, 32, 768], P('mp', 'dp'), may hold values from -0.57735027 to 0.57735027, as said below
- moment_one: float32 [2, 192, 32, 768], P('mp', 'dp'), may hold values from -256 to 256, as said below
- moment_two: float32 [2, 192, 32, 768], P('mp', 'dp'), may hold values from 0 to 16384, as said below
- scale_state: float32 [3, 12], P(None, 'mp'), may hold values from -153.6 to 5898.24, as said below
Outputs:
- output: float32 [16384, 768], P('dp')
- input_grad: float32 [16384, 768], P('dp')
- weight_grads: float32 [2, 180, 24576], P('mp', None, 'dp')
- new_master: float32 [2, 192, 32, 768], P('mp', 'dp')
- new_moment_one: float32 [2, 192, 32, 768], P('mp', 'dp')
- new_moment_two: float32 [2, 192, 32, 768], P('mp', 'dp')
- scale_update: float32 [2, 12], P(None, 'mp')
- scale_moment_two: float32 [12], P('mp')
The draws below stay inside these ranges and needn't reach their ends.
Inputs may be any that keep to these rules, and one draw needn't show every extreme that they name: owners[h, u] is the index of dp whose slots hold unit u of half h; no index holds more than 12 units of one half, and in each half some index holds exactly 12. `positions`: each image's (row, column) pairs visit every cell of the 16 x 16 grid once. `master`: slots that no unit fills are zero. `moment_one`: slots that no unit fills are zero. `moment_two`: slots that no unit fills are zero; the others are positive. `scale_state`: row 0 lies between 6 and 14, row 2 is positive.
All inputs are finite; a program needn't handle non-finite values.
Results may differ from the reference program's by a relative error of at most 0.024.
Values may be sent and summed in bfloat16 or wider, within the bound.
No kernel may reach another device: no remote copies, remote signals or barrier semaphores. Data moves between devices by JAX's collectives and lax.ppermute only.
A program may use at most 192 MiB of HBM per device.

```python
import math
import jax
import jax.numpy as jnp
from jax import lax

D = 768
HEADS = 12
HD = 64
FF = 2304
C = 768
SIDE = 16
R = 32
STEP = 10
SEQ = 256
IMAGES = 64
TOKENS = 16384
HALF_ROWS = 5760
UNITS_MP = 180
SLOTS = 12
N_DP = 16
N_MP = 2


def slot_places_drawn(owner_list, slots):
    unit_count = owner_list.shape[0]
    same_owner = owner_list[:, None] == owner_list[None, :]
    row_ids = lax.broadcasted_iota(jnp.int32, (unit_count, unit_count), 0)
    col_ids = lax.broadcasted_iota(jnp.int32, (unit_count, unit_count), 1)
    before = jnp.sum(jnp.where(same_owner & (col_ids < row_ids), 1, 0), axis=1).astype(jnp.int32)
    return (owner_list * slots + before).astype(jnp.int32)


def owner_table(key):
    tables = []
    for half_index in range(N_MP):
        half_key = jax.random.fold_in(key, 500 + half_index)
        key_list = jax.random.split(half_key, 3)
        spare = jax.random.permutation(key_list[0], N_DP * SLOTS - SLOTS).astype(jnp.int32) + SLOTS
        chosen = jnp.concatenate([jnp.arange(SLOTS, dtype=jnp.int32), spare])[:UNITS_MP]
        chosen = jax.random.permutation(key_list[1], chosen)
        relabel = jax.random.permutation(key_list[2], N_DP).astype(jnp.int32)
        tables.append(relabel[chosen // SLOTS])
    return jnp.stack(tables).astype(jnp.int32)


def pack_units(units, table):
    packed = jnp.zeros((N_MP, N_DP * SLOTS, R, D), jnp.float32)
    for half_index in range(N_MP):
        packed = packed.at[half_index, slot_places_drawn(table[half_index], SLOTS)].set(units[half_index])
    return packed


def row_factor(factors):
    cond_rows = C // N_MP
    feat_rows = D // N_MP
    hidden_rows = FF // N_MP
    row_counts = [cond_rows, 3 * feat_rows, feat_rows, cond_rows, 2 * hidden_rows, hidden_rows]
    return jnp.concatenate([jnp.full((span_rows,), factor, jnp.float32) for span_rows, factor in zip(row_counts, factors)])


def grad_factor():
    return row_factor([0.5, 0.2, 0.1, 0.5, 0.3, 0.4]) * math.sqrt(TOKENS)


def draw_owners(key, part):
    return owner_table(key)


def draw_master(key, part):
    table = owner_table(key)
    key = jax.random.fold_in(key, 21)
    spread = row_factor([0.3 / math.sqrt(C), 1.0 / math.sqrt(D), 4.0 / math.sqrt(D), 0.3 / math.sqrt(C), 1.0 / math.sqrt(D), math.sqrt(2.0 / FF)])
    noise = jax.random.truncated_normal(key, -4.0, 4.0, (N_MP, HALF_ROWS, D), jnp.float32)
    units = (noise * spread[None, :, None]).reshape(N_MP, UNITS_MP, R, D)
    return pack_units(units, table)


def draw_moment_one(key, part):
    table = owner_table(key)
    key = jax.random.fold_in(key, 22)
    noise = jax.random.truncated_normal(key, -4.0, 4.0, (N_MP, HALF_ROWS, D), jnp.float32)
    units = (noise * grad_factor()[None, :, None]).reshape(N_MP, UNITS_MP, R, D)
    return pack_units(units, table)


def draw_moment_two(key, part):
    table = owner_table(key)
    key = jax.random.fold_in(key, 23)
    factor = jnp.exp(jax.random.uniform(key, (N_MP, HALF_ROWS, D), jnp.float32, 0.0, math.log(4.0)))
    level = grad_factor()
    units = (factor * (level * level)[None, :, None]).reshape(N_MP, UNITS_MP, R, D)
    return pack_units(units, table)


def draw_scale_state(key, part):
    key = jax.random.fold_in(key, 24)
    key_list = jax.random.split(key, 3)
    level = 0.3 * math.sqrt(TOKENS)
    values_row = jax.random.uniform(key_list[0], (HEADS,), jnp.float32, 6.0, 14.0)
    first_row = jax.random.truncated_normal(key_list[1], -4.0, 4.0, (HEADS,), jnp.float32) * level
    second_row = jnp.exp(jax.random.uniform(key_list[2], (HEADS,), jnp.float32, 0.0, math.log(4.0))) * level * level
    return jnp.stack([values_row, first_row, second_row]).astype(jnp.float32)


def draw_sigmas(key, part):
    key = jax.random.fold_in(key, 11)
    key_list = jax.random.split(key, 2)
    rank_share = jnp.arange(IMAGES, dtype=jnp.float32) / IMAGES
    reach = 1.2
    depth = reach * (1.0 - rank_share) * jax.random.uniform(key_list[0], (IMAGES,), jnp.float32, 0.75, 1.25)
    signs = jnp.where(jax.random.bernoulli(key_list[1], 0.5, (IMAGES,)), 1.0, -1.0)
    return (0.5 * jnp.exp(signs * depth)).astype(jnp.float32)


def draw_positions(key, part):
    key = jax.random.fold_in(key, 7)
    key_list = jax.random.split(key, IMAGES)
    order = jax.vmap(lambda single: jax.random.permutation(single, SEQ))(key_list).astype(jnp.int32)
    return jnp.stack([order // SIDE, order % SIDE], axis=1).astype(jnp.int32)


def block_scale(rng, shape, shards, smallest, high):
    level, own = 1.0, jax.random.fold_in(rng, 6)
    for dim, shards_of in shards:
        steps = jnp.exp(jax.random.uniform(jax.random.fold_in(own, dim), (shards_of,), jnp.float32, smallest / len(shards), high / len(shards)))
        level = level * jnp.repeat(steps, shape[dim] // shards_of).reshape([-1 if axis == dim else 1 for axis in range(len(shape))])
    return level


def scatter_about(rng, shape, width, bound, shards=(), kind=jnp.bfloat16):
    loudness = block_scale(rng, shape, shards, -0.22, 0.18) if shards else 1.0
    entries = jax.random.normal(rng, shape, jnp.float32) * width * loudness
    return jnp.minimum(jnp.maximum(entries, -bound), bound).astype(kind)


def setup_inputs(seed: int = 0) -> dict:
    key_of = jax.random.split(jax.random.key(seed), 11)
    return {
        "tokens": scatter_about(key_of[0], (TOKENS, D), 1.0, 6.0, ((0, 16),), jnp.float32),
        "conditioning": scatter_about(key_of[1], (IMAGES, C), 1.0, 5.0, ((0, 16),), jnp.float32),
        "sigmas": draw_sigmas(jax.random.fold_in(key_of[10], 71), 0),
        "positions": draw_positions(jax.random.fold_in(key_of[10], 71), 0),
        "cotangent": scatter_about(key_of[4], (TOKENS, D), 1.0, 6.0, ((0, 16),)),
        "owners": draw_owners(jax.random.fold_in(key_of[10], 71), 0),
        "master": draw_master(jax.random.fold_in(key_of[10], 71), 0),
        "moment_one": draw_moment_one(jax.random.fold_in(key_of[10], 71), 0),
        "moment_two": draw_moment_two(jax.random.fold_in(key_of[10], 71), 0),
        "scale_state": draw_scale_state(jax.random.fold_in(key_of[10], 71), 0),
    }


@jax.custom_vjp
def low(v):
    return lax.optimization_barrier(v.astype(jnp.bfloat16)).astype(jnp.float32)

@jax.custom_vjp
def low_back(v):
    return v

def low_keep(v):
    return (low(v), None)

def low_pass(kept, grad):
    return (grad,)

def back_keep(v):
    return (v, None)

def back_low(kept, grad):
    return (low(grad),)
low.defvjp(low_keep, low_pass)
low_back.defvjp(back_keep, back_low)
NORM_EPS = 1e-06
COS_EPS = 1e-06
SIGMA_DATA = 0.5
BETA_ONE = 0.5
BETA_TWO = 0.5
ADAM_EPS = 1e-08
WEIGHT_DECAY = 0.01
LEARN_RATE = 0.04
SCALE_RATE = 1.0

def dot_high(left, right):
    return jnp.dot(left, right, precision=lax.Precision.HIGHEST, preferred_element_type=jnp.float32)

def dot_rows(left, right):
    return lax.dot_general(left, right, (((1,), (1,)), ((), ())), precision=lax.Precision.HIGHEST, preferred_element_type=jnp.float32)

def slot_places(owner_list, slots):
    unit_count = owner_list.shape[0]
    same_owner = owner_list[:, None] == owner_list[None, :]
    row_ids = lax.broadcasted_iota(jnp.int32, (unit_count, unit_count), 0)
    col_ids = lax.broadcasted_iota(jnp.int32, (unit_count, unit_count), 1)
    before = lax.optimization_barrier(jnp.sum(jnp.where(same_owner & (col_ids < row_ids), 1, 0), axis=1)).astype(jnp.int32)
    return (owner_list * slots + before).astype(jnp.int32)

def rope_tables(positions, first_head, heads_here):
    quarter = HD // 8
    head_ids = lax.broadcasted_iota(jnp.int32, (heads_here, quarter), 0) + first_head
    column = lax.broadcasted_iota(jnp.int32, (heads_here, quarter), 1)
    flat_index = (column * HEADS + head_ids).astype(jnp.float32)
    low_log = math.log(math.pi)
    high_log = math.log(10.0 * math.pi)
    frequency = jnp.exp(low_log + (high_log - low_log) * flat_index / (HEADS * quarter))
    placed = (2.0 * positions.astype(jnp.float32) + 1.0) / SIDE - 1.0
    along_rows = placed[:, 0, :, None, None] * frequency[None, None]
    along_cols = placed[:, 1, :, None, None] * frequency[None, None]
    angles = jnp.concatenate([along_rows, along_cols], axis=-1)
    return (jnp.cos(angles), jnp.sin(angles))

def rotate(field, cosine, sine_table):
    span_width = cosine.shape[-1]
    first_part = field[..., :span_width]
    second = field[..., span_width:2 * span_width]
    return jnp.concatenate([first_part * cosine - second * sine_table, second * cosine + first_part * sine_table, field[..., 2 * span_width:]], axis=-1)

def ada_norm(x_block, gain_rows):
    inverse = lax.rsqrt(lax.optimization_barrier(jnp.mean(x_block * x_block, axis=-1, keepdims=True)) + NORM_EPS)
    return x_block * inverse * gain_rows[:, None, :]

def split_weights(stacked):
    cond_rows = C // N_MP
    feat_rows = D // N_MP
    hidden_rows = FF // N_MP
    row_counts = [cond_rows, feat_rows, feat_rows, feat_rows, feat_rows, cond_rows, hidden_rows, hidden_rows, hidden_rows]
    pieces = []
    row_start = 0
    for span_rows in row_counts:
        pieces.append(stacked[:, row_start:row_start + span_rows].reshape(N_MP * span_rows, D))
        row_start += span_rows
    return pieces

def block_layer(x_block, cond_low, positions, weights, scales):
    ada_first, w_query, w_key, w_value, out_proj, ada_second, w_gate, w_up, down_proj = weights
    images = x_block.shape[0]
    row_count = images * SEQ
    normed_first = low(ada_norm(x_block, 1.0 + dot_high(cond_low, ada_first))).reshape(row_count, D)
    head_shape = (images, SEQ, HEADS, HD)
    query_raw = low_back(dot_rows(normed_first, w_query)).reshape(head_shape)
    key_raw = low_back(dot_rows(normed_first, w_key)).reshape(head_shape)
    value_raw = low_back(dot_rows(normed_first, w_value)).reshape(head_shape)
    scale_root = jnp.sqrt(scales)[None, None, :, None]
    cosine, sine_table = rope_tables(positions, 0, HEADS)
    query_inverse = lax.rsqrt(lax.optimization_barrier(jnp.sum(query_raw * query_raw, axis=-1, keepdims=True)) + COS_EPS)
    key_inverse = lax.rsqrt(lax.optimization_barrier(jnp.sum(key_raw * key_raw, axis=-1, keepdims=True)) + COS_EPS)
    query_low = low(rotate(query_raw * scale_root * query_inverse, cosine, sine_table))
    key_low = low(rotate(key_raw * scale_root * key_inverse, cosine, sine_table))
    value_low = low(value_raw)
    scores = low_back(jnp.einsum('ishd,ithd->ihst', query_low, key_low, precision=lax.Precision.HIGHEST))
    top_score = lax.optimization_barrier(jnp.max(scores, axis=-1, keepdims=True))
    exp_scores = jnp.exp(scores - top_score)
    probs_low = low(exp_scores / lax.optimization_barrier(jnp.sum(exp_scores, axis=-1, keepdims=True)))
    mixed_out = jnp.einsum('ihst,ithd->ishd', probs_low, value_low, precision=lax.Precision.HIGHEST).reshape(row_count, D)
    mixed_out = low(low_back(mixed_out))
    x_mid = x_block.reshape(row_count, D) + low_back(dot_high(mixed_out, out_proj))
    normed_second = low(ada_norm(x_mid.reshape(images, SEQ, D), 1.0 + dot_high(cond_low, ada_second))).reshape(row_count, D)
    gate_part = low_back(dot_rows(normed_second, w_gate))
    up_part = low_back(dot_rows(normed_second, w_up))
    hidden = low(jax.nn.gelu(gate_part, approximate=False) * up_part)
    return (x_mid + low_back(dot_high(hidden, down_proj))).reshape(images, SEQ, D)

def adam_step(weights, first_new, second_new, rate):
    fix_one = 1.0 - math.pow(BETA_ONE, STEP)
    fix_two = 1.0 - math.pow(BETA_TWO, STEP)
    return weights * (1.0 - rate * WEIGHT_DECAY) - rate * (first_new / fix_one) / (jnp.sqrt(second_new / fix_two) + ADAM_EPS)

def reference(tokens, conditioning, sigmas, positions, cotangent, owners, master, moment_one, moment_two, scale_state):
    places = jnp.stack([slot_places(owners[half_index], SLOTS) for half_index in range(N_MP)])

    def units_of(table):
        return jnp.stack([table[half_index][places[half_index]] for half_index in range(N_MP)])

    def packed_of(units):
        packed = jnp.zeros((N_MP, N_DP * SLOTS, R, D), jnp.float32)
        for half_index in range(N_MP):
            packed = packed.at[half_index, places[half_index]].set(units[half_index])
        return packed
    master_units = units_of(master)
    stacked = master_units.reshape(N_MP, HALF_ROWS, D)
    square = sigmas * sigmas
    data_square = SIGMA_DATA * SIGMA_DATA
    loss_weight = 4.0 * square * data_square / ((square + data_square) * (square + data_square))
    grad_out = (cotangent.astype(jnp.float32).reshape(IMAGES, SEQ, D) * loss_weight[:, None, None]).reshape(TOKENS, D)
    group = math.gcd(IMAGES, 16)
    cond_groups = low(conditioning).reshape(-1, group, C)
    pos_groups = positions.reshape(-1, group, 2, SEQ)

    def forward(x_flat, stacked_rows, scales):
        weights = split_weights(low(stacked_rows))

        def run_group(pieces):
            return block_layer(pieces[0], pieces[1], pieces[2], weights, scales)
        results = lax.map(jax.checkpoint(run_group), (x_flat.reshape(-1, group, SEQ, D), cond_groups, pos_groups))
        return results.reshape(TOKENS, D)
    result, pullback = jax.vjp(forward, tokens.astype(jnp.float32), stacked, scale_state[0])
    input_grad, grad_rows, scale_grad = pullback(grad_out)
    grad_units = grad_rows.reshape(N_MP, UNITS_MP, R, D)
    first_new = BETA_ONE * units_of(moment_one) + (1.0 - BETA_ONE) * grad_units
    second_new = BETA_TWO * units_of(moment_two) + (1.0 - BETA_TWO) * grad_units * grad_units
    master_new = adam_step(master_units, first_new, second_new, LEARN_RATE)
    scale_first = BETA_ONE * scale_state[1] + (1.0 - BETA_ONE) * scale_grad
    scale_second = BETA_TWO * scale_state[2] + (1.0 - BETA_TWO) * scale_grad * scale_grad
    scale_new = adam_step(scale_state[0], scale_first, scale_second, SCALE_RATE)
    return (result, input_grad, grad_units.reshape(N_MP, UNITS_MP, R * D), packed_of(master_new), packed_of(first_new), packed_of(second_new), jnp.stack([scale_first, scale_new]), scale_second)
```

```python
import math

import jax
import jax.numpy as jnp
from jax import lax
from jax.experimental import pallas as pl
from jax.experimental.pallas import tpu as pltpu
from jax.sharding import PartitionSpec as P

D = 768
HEADS = 12
HD = 64
FF = 2304
SIDE = 16
STEP = 10
SEQ = 256
UNIT = 32
SPAN = 12
CHUNK = SPAN * UNIT
HALF_CHUNK = CHUNK // 2

NORM_EPS = 1e-06
COS_EPS = 1e-06
SIGMA_DATA = 0.5
BETA_ONE = 0.5
BETA_TWO = 0.5
ADAM_EPS = 1e-08
WEIGHT_DECAY = 0.01
LEARN_RATE = 0.04
SCALE_RATE = 1.0
ROOT_HALF = 0.7071067811865476
INV_ROOT_TWO_PI = 0.3989422804014327

F32 = jnp.float32
BF16 = jnp.bfloat16
VMEM_BYTES = 60 * 1024 * 1024

STACK_ORDER = ("A1", "Q", "K", "V", "O", "A2", "G", "G", "G", "U", "U", "U", "F", "F", "F")
ROW_A1, ROW_A2, ROW_Q, ROW_K, ROW_V, ROW_O = (D * place for place in range(6))
ROW_G = 6 * D
ROW_U = ROW_G + FF
ROW_F = ROW_U + FF
ROWS_ALL = ROW_F + FF


def dot_nn(left, right):
    return jnp.dot(left, right, preferred_element_type=F32)


def dot_nt(left, right):
    return lax.dot_general(left, right, (((1,), (1,)), ((), ())), preferred_element_type=F32)


def slots_before(owner_list):
    unit_count = owner_list.shape[0]
    same_owner = owner_list[:, None] == owner_list[None, :]
    row_ids = lax.broadcasted_iota(jnp.int32, (unit_count, unit_count), 0)
    col_ids = lax.broadcasted_iota(jnp.int32, (unit_count, unit_count), 1)
    return jnp.sum(jnp.where(same_owner & (col_ids < row_ids), 1, 0), axis=1).astype(jnp.int32)


def rope_tables(positions):
    quarter = HD // 8
    head_ids = lax.broadcasted_iota(jnp.int32, (HEADS, quarter), 0)
    column = lax.broadcasted_iota(jnp.int32, (HEADS, quarter), 1)
    flat_index = (column * HEADS + head_ids).astype(F32)
    low_log = math.log(math.pi)
    high_log = math.log(10.0 * math.pi)
    frequency = jnp.exp(low_log + (high_log - low_log) * flat_index / (HEADS * quarter))
    placed = (2.0 * positions.astype(F32) + 1.0) / SIDE - 1.0
    along_rows = placed[:, 0].reshape(1, 1, -1) * frequency[:, :, None]
    along_cols = placed[:, 1].reshape(1, 1, -1) * frequency[:, :, None]
    angles = jnp.concatenate([along_rows, along_cols], axis=1).reshape(HEADS * 2 * quarter, -1)
    return jnp.cos(angles), jnp.sin(angles)


def deal_matrix(core):
    target = lax.broadcasted_iota(jnp.int32, (CHUNK, CHUNK), 0)
    source = lax.broadcasted_iota(jnp.int32, (CHUNK, CHUNK), 1)
    parity = (target // HALF_CHUNK + core) % 2
    inner = target % HALF_CHUNK
    piece = inner // (2 * SPAN)
    row = inner // SPAN % 2
    unit = inner % SPAN
    return (source == unit * UNIT + 4 * piece + 2 * parity + row).astype(BF16)


def layer_kernel(
    images,
    src_ref,
    scal_ref,
    x_ref,
    cot_ref,
    cond_ref,
    cos_ref,
    sin_ref,
    deal_ref,
    slots_ref,
    out_hbm,
    grad_hbm,
    hid_keep,
    hid_send,
    gu_keep,
    gu_send,
    at_keep,
    at_send,
    n1_hbm,
    n2_hbm,
    gb_hbm,
    ga_hbm,
    gain_hbm,
    ds_hbm,
    w,
    unit_s,
    coef_s,
    qtok_s,
    qk_s,
    v_s,
    o_s,
    x2_s,
    n1_s,
    n2_s,
    gb_s,
    ga_s,
    do_s,
    dot_s,
    ff_s,
    dn2_s,
    dqkv_s,
    hid_s,
    gu_s,
    at_s,
    out_s,
    gin_s,
    gain_s,
    ds_s,
    dsout_s,
    w_sem,
    o_sem,
):
    toks = images * SEQ
    sends = []

    def send(src, dst):
        copy = pltpu.make_async_copy(src, dst, o_sem.at[len(sends)])
        copy.start()
        sends.append(copy)

    groups = ((0, ROW_Q), (ROW_Q, ROW_O), (ROW_O, ROW_G), (ROW_G, ROWS_ALL))
    for index, (low, high) in enumerate(groups):

        @pl.loop(low // UNIT, high // UNIT)
        def _(unit):
            pltpu.make_async_copy(
                slots_ref.at[src_ref[unit]],
                w.at[pl.ds(pl.multiple_of(unit * UNIT, UNIT), UNIT)],
                w_sem.at[index],
            ).start()

    def weights_here(index):
        low, high = groups[index]
        region = w.at[pl.ds(low, high - low)]
        pltpu.make_async_copy(region, region, w_sem.at[index]).wait()

    def image_rows(image):
        return pl.ds(image * SEQ, SEQ)

    weights_here(0)
    gain_one = 1.0 + dot_nn(cond_ref[...], w[ROW_A1 : ROW_A1 + D])
    gain_two = 1.0 + dot_nn(cond_ref[...], w[ROW_A2 : ROW_A2 + D])
    for image in range(images):
        x = x_ref[image_rows(image)]
        inverse = lax.rsqrt(jnp.mean(x * x, axis=-1, keepdims=True) + NORM_EPS)
        n1_s[image_rows(image)] = (x * inverse * gain_one[image : image + 1]).astype(BF16)
        weight = scal_ref[2 * HEADS + image]
        gb_s[image_rows(image)] = (cot_ref[image_rows(image)].astype(F32) * weight).astype(BF16)
    send(n1_s, n1_hbm)
    send(gb_s, gb_hbm)
    weights_here(1)
    unit_s[:D] = dot_nt(w[ROW_Q : ROW_Q + D], n1_s[...])
    unit_s[D:] = dot_nt(w[ROW_K : ROW_K + D], n1_s[...])
    v_s[...] = dot_nt(w[ROW_V : ROW_V + D], n1_s[...]).astype(BF16)

    @pl.loop(0, 2 * HEADS)
    def _(index):
        head = lax.rem(index, HEADS)
        rows = pl.ds(pl.multiple_of(index * HD, HD), HD)
        angle_rows = pl.ds(pl.multiple_of(head * 16, 16), 16)
        raw = unit_s[rows]
        inverse = lax.rsqrt(jnp.sum(raw * raw, axis=0, keepdims=True) + COS_EPS)
        unit = raw * inverse
        root = scal_ref[HEADS + head]
        unit_s[rows] = unit
        coef_s[pl.ds(index, 1)] = root * inverse
        scaled = unit * root
        first, second = scaled[:16], scaled[16:32]
        cosine, sine = cos_ref[angle_rows], sin_ref[angle_rows]
        turned = jnp.concatenate(
            [first * cosine - second * sine, second * cosine + first * sine, scaled[32:]], axis=0
        )
        qk_s[rows] = turned.astype(BF16)

    qtok_s[...] = qk_s[:D].T

    def pair_parts(image, pair, half):
        head = pair * 2 + half
        rows = pl.ds(pl.multiple_of(head * HD, HD), HD)
        key_rows = pl.ds(pl.multiple_of(D + head * HD, HD), HD)
        lanes = pl.ds(pl.multiple_of(pair * 2 * HD, 2 * HD), 2 * HD)
        query = qtok_s[image_rows(image), lanes][:, half * HD : (half + 1) * HD]
        key = qk_s[key_rows, image_rows(image)]
        value = v_s[rows, image_rows(image)]
        exp_scores = jnp.exp(dot_nn(query, key) - scal_ref[head])
        probs = exp_scores * (1.0 / jnp.sum(exp_scores, axis=-1, keepdims=True))
        return head, rows, key_rows, lanes, key, value, probs

    @pl.loop(0, HEADS // 2)
    def _(pair):
        for image in range(images):
            mixed = []
            for half in range(2):
                _, _, _, lanes, _, value, probs = pair_parts(image, pair, half)
                mixed.append(dot_nt(probs.astype(BF16), value))
            o_s[image_rows(image), lanes] = jnp.concatenate(mixed, axis=1).astype(BF16)

    weights_here(2)
    x2_s[...] = x_ref[...] + dot_nn(o_s[...], w[ROW_O : ROW_O + D])
    for image in range(images):
        x2 = x2_s[image_rows(image)]
        inverse = lax.rsqrt(jnp.mean(x2 * x2, axis=-1, keepdims=True) + NORM_EPS)
        n2_s[image_rows(image)] = (x2 * inverse * gain_two[image : image + 1]).astype(BF16)
    send(n2_s, n2_hbm)

    weights_here(3)
    chunks = FF // CHUNK

    def deal(field, store, place):
        dealt = dot_nt(deal_ref[...], field).astype(BF16)
        store[0, place] = dealt[:HALF_CHUNK]
        store[1, place] = dealt[HALF_CHUNK:]

    @pl.loop(0, chunks)
    def _(chunk):
        def part(base):
            return w[pl.ds(pl.multiple_of(base + chunk * CHUNK, CHUNK), CHUNK)]

        gate = dot_nt(n2_s[...], part(ROW_G))
        up = dot_nt(n2_s[...], part(ROW_U))
        grad_hidden = dot_nt(gb_s[...], part(ROW_F))
        phi_sum = 0.5 * (1.0 + lax.erf(gate * ROOT_HALF))
        density = INV_ROOT_TWO_PI * jnp.exp(-0.5 * gate * gate)
        gelu = gate * phi_sum
        hidden = (gelu * up).astype(BF16)
        grad_gate = (grad_hidden * up * (phi_sum + gate * density)).astype(BF16)
        grad_up = (grad_hidden * gelu).astype(BF16)
        ff = dot_nn(hidden, part(ROW_F))
        dn2 = dot_nn(grad_gate, part(ROW_G)) + dot_nn(grad_up, part(ROW_U))

        @pl.when(chunk == 0)
        def _():
            ff_s[...] = ff
            dn2_s[...] = dn2

        @pl.when(chunk > 0)
        def _():
            ff_s[...] += ff
            dn2_s[...] += dn2

        deal(hidden, hid_s, chunk)
        deal(grad_gate, gu_s, chunk)
        deal(grad_up, gu_s, chunks + chunk)

    send(hid_s.at[0], hid_keep)
    send(hid_s.at[1], hid_send)
    send(gu_s.at[0], gu_keep)
    send(gu_s.at[1], gu_send)
    out_s[...] = (x2_s[...] + ff_s[...]).astype(BF16)
    send(out_s, out_hbm)

    def norm_back(x, gain, grad_normed):
        inverse = lax.rsqrt(jnp.mean(x * x, axis=-1, keepdims=True) + NORM_EPS)
        scaled = grad_normed * gain
        inner = jnp.mean(x * scaled, axis=-1, keepdims=True)
        grad_x = inverse * scaled - x * (inverse * inverse * inverse * inner)
        return grad_x, jnp.sum(grad_normed * x * inverse, axis=0, keepdims=True)

    for image in range(images):
        rows = image_rows(image)
        grad_x, grad_gain = norm_back(x2_s[rows], gain_two[image : image + 1], dn2_s[rows])
        grad = cot_ref[rows].astype(F32) * scal_ref[2 * HEADS + image] + grad_x
        x2_s[rows] = grad
        ga_s[rows] = grad.astype(BF16)
        gain_s[pl.ds(images + image, 1)] = grad_gain
    send(ga_s, ga_hbm)

    do_s[...] = dot_nt(ga_s[...], w[ROW_O : ROW_O + D]).astype(BF16)
    dot_s[...] = dot_nt(w[ROW_O : ROW_O + D], ga_s[...]).astype(BF16)
    ds_s[...] = jnp.zeros_like(ds_s)

    @pl.loop(0, HEADS // 2)
    def _(pair):
        for image in range(images):
            cols = image_rows(image)
            for half in range(2):
                head, rows, key_rows, lanes, key, value, probs = pair_parts(image, pair, half)
                grad_mixed = do_s[cols, lanes][:, half * HD : (half + 1) * HD]
                grad_probs = dot_nn(grad_mixed, value)
                inner = jnp.sum(probs * grad_probs, axis=-1, keepdims=True)
                grad_scores = (probs * (grad_probs - inner)).astype(BF16)
                grad_query = dot_nt(key, grad_scores)
                grad_key = dot_nn(qk_s[rows, cols], grad_scores)
                grad_value = dot_nn(dot_s[rows, cols], probs.astype(BF16))
                angle_rows = pl.ds(pl.multiple_of(head * 16, 16), 16)
                cosine, sine = cos_ref[angle_rows, cols], sin_ref[angle_rows, cols]
                along = jnp.zeros((1, SEQ), F32)
                for grad, own_rows, place in (
                    (grad_query, rows, head),
                    (grad_key, key_rows, HEADS + head),
                ):
                    first, second = grad[:16], grad[16:32]
                    back = jnp.concatenate(
                        [
                            first * cosine + second * sine,
                            second * cosine - first * sine,
                            grad[32:],
                        ],
                        axis=0,
                    )
                    unit = unit_s[own_rows, cols]
                    inner_unit = jnp.sum(unit * back, axis=0, keepdims=True)
                    along += inner_unit
                    dqkv_s[own_rows, cols] = (
                        coef_s[pl.ds(place, 1), cols] * (back - unit * inner_unit)
                    ).astype(BF16)
                value_rows = pl.ds(pl.multiple_of(2 * D + head * HD, HD), HD)
                dqkv_s[value_rows, cols] = grad_value.astype(BF16)
                ds_s[pl.ds(head, 1)] += along

    for place in range(2):
        deal(o_s[:, place * CHUNK : (place + 1) * CHUNK], at_s, place)
    for place in range(6):
        dealt = dot_nn(deal_ref[...], dqkv_s[place * CHUNK : (place + 1) * CHUNK]).astype(BF16)
        at_s[0, 2 + place] = dealt[:HALF_CHUNK]
        at_s[1, 2 + place] = dealt[HALF_CHUNK:]
    send(at_s.at[0], at_keep)
    send(at_s.at[1], at_send)
    dsout_s[...] = jnp.broadcast_to(jnp.sum(ds_s[...], axis=1, keepdims=True), dsout_s.shape)
    send(dsout_s, ds_hbm)

    dn1 = dot_nn(dqkv_s[:D].T, w[ROW_Q : ROW_Q + D])
    dn1 += dot_nn(dqkv_s[D : 2 * D].T, w[ROW_K : ROW_K + D])
    dn1 += dot_nn(dqkv_s[2 * D :].T, w[ROW_V : ROW_V + D])
    dn2_s[...] = dn1
    for image in range(images):
        rows = image_rows(image)
        grad_x, grad_gain = norm_back(x_ref[rows], gain_one[image : image + 1], dn2_s[rows])
        gin_s[rows] = (x2_s[rows] + grad_x).astype(BF16)
        gain_s[pl.ds(image, 1)] = grad_gain
    send(gin_s, grad_hbm)
    send(gain_s, gain_hbm)
    for copy in sends:
        copy.wait()


def run_layer(images, source, scalars, x, cotangent, cond, cosine, sine, deal, slots):
    toks = images * SEQ
    chunks = FF // CHUNK
    any_spec = pl.BlockSpec(memory_space=pl.ANY)
    vmem = pl.BlockSpec(memory_space=pltpu.VMEM)
    smem = pl.BlockSpec(memory_space=pltpu.SMEM)
    field = jax.ShapeDtypeStruct((toks, D), BF16)

    def dealt(count):
        return jax.ShapeDtypeStruct((count, HALF_CHUNK, toks), BF16)

    outs = [field, field]
    outs += [dealt(chunks)] * 2 + [dealt(2 * chunks)] * 2 + [dealt(8)] * 2
    outs += [field] * 4
    outs += [
        jax.ShapeDtypeStruct((2 * images, D), F32),
        jax.ShapeDtypeStruct((16, 128), F32),
    ]
    wide = pltpu.VMEM((toks, D), F32)
    low = pltpu.VMEM((toks, D), BF16)
    scratch = [
        pltpu.VMEM((ROWS_ALL, D), BF16),
        pltpu.VMEM((2 * D, toks), F32),
        pltpu.VMEM((2 * HEADS, toks), F32),
        low,
        pltpu.VMEM((2 * D, toks), BF16),
        pltpu.VMEM((D, toks), BF16),
        low,
        wide,
        low,
        low,
        low,
        low,
        low,
        pltpu.VMEM((D, toks), BF16),
        wide,
        wide,
        pltpu.VMEM((3 * D, toks), BF16),
        pltpu.VMEM((2, chunks, HALF_CHUNK, toks), BF16),
        pltpu.VMEM((2, 2 * chunks, HALF_CHUNK, toks), BF16),
        pltpu.VMEM((2, 8, HALF_CHUNK, toks), BF16),
        low,
        low,
        pltpu.VMEM((2 * images, D), F32),
        pltpu.VMEM((16, SEQ), F32),
        pltpu.VMEM((16, 128), F32),
        pltpu.SemaphoreType.DMA((4,)),
        pltpu.SemaphoreType.DMA((16,)),
    ]

    def body(*refs):
        layer_kernel(images, *refs)

    return pl.pallas_call(
        body,
        out_shape=outs,
        in_specs=[smem, smem] + [vmem] * 6 + [any_spec],
        out_specs=[any_spec] * len(outs),
        scratch_shapes=scratch,
        compiler_params=pltpu.CompilerParams(vmem_limit_bytes=VMEM_BYTES),
        cost_estimate=pl.CostEstimate(
            flops=2 * 3 * ROWS_ALL * D * toks, bytes_accessed=ROWS_ALL * D * 4, transcendentals=0
        ),
        name="layer",
    )(source, scalars, x, cotangent, cond, cosine, sine, deal, slots)


def weight_grads(groups, halves):
    rows, toks = groups[0][0][0].shape[1:]
    pieces = rows // (2 * SPAN)
    operands, specs, places, flops, moved = [], [], [], 0, 0
    total = 0
    for lefts, rights, first, here in groups:
        assert first % here == 0
        places.append((len(lefts), len(operands), total, here))
        total += here
        for left in lefts:
            operands.append(left)
            specs.append(
                pl.BlockSpec((here, rows, toks), lambda half, at=first // here: (at + half, 0, 0))
            )
        for right in rights:
            operands.append(right)
            specs.append(pl.BlockSpec((toks, D), lambda half: (0, 0)))
        flops += 2 * len(lefts) * here * halves * rows * toks * D
        moved += len(lefts) * 2 * (here * halves * rows * toks + toks * D)

    def body(*refs):
        out_ref = refs[-1]
        for count, start, at, here in places:
            lefts, rights = refs[start : start + count], refs[start + count : start + 2 * count]
            summed = dot_nn(lefts[0][...].reshape(here * rows, toks), rights[0][...])
            for left, right in zip(lefts[1:], rights[1:]):
                summed += dot_nn(left[...].reshape(here * rows, toks), right[...])
            for chunk in range(here):
                out_ref[0, :, at + chunk] = (
                    summed[chunk * rows : (chunk + 1) * rows]
                    .reshape(pieces, 2 * SPAN, D)
                    .astype(BF16)
                )

    return pl.pallas_call(
        body,
        out_shape=jax.ShapeDtypeStruct((halves, pieces, total, 2 * SPAN, D), BF16),
        grid=(halves,),
        in_specs=specs,
        out_specs=pl.BlockSpec(
            (1, pieces, total, 2 * SPAN, D), lambda half: (half, 0, 0, 0, 0)
        ),
        compiler_params=pltpu.CompilerParams(vmem_limit_bytes=VMEM_BYTES),
        cost_estimate=pl.CostEstimate(
            flops=flops,
            bytes_accessed=moved + halves * pieces * total * 4 * SPAN * D,
            transcendentals=0,
        ),
        name="weight_grads",
    )(*operands)


def adam_step(weights, first_new, second_new, rate):
    fix_one = 1.0 - math.pow(BETA_ONE, STEP)
    fix_two = 1.0 - math.pow(BETA_TWO, STEP)
    return weights * (1.0 - rate * WEIGHT_DECAY) - rate * (first_new / fix_one) / (
        jnp.sqrt(second_new / fix_two) + ADAM_EPS
    )


def add(*terms):
    total = terms[0].astype(F32)
    for term in terms[1:]:
        total = total + term.astype(F32)
    return total


class Ring:
    def __init__(self, dp_count):
        self.count = dp_count // 2
        pairs = []
        for place in range(self.count):
            for core in range(2):
                pairs.append(
                    (self.chip(place) * 2 + core, self.chip((place + 1) % self.count) * 2 + core)
                )
        self.onward = pairs
        self.backward = [(b, a) for a, b in pairs]
        self.twins = [(index, index ^ 1) for index in range(dp_count)]

    def chip(self, place):
        column = self.count // 2
        return 2 * place if place < column else 2 * (self.count - 1 - place) + 1

    def here(self):
        chip = lax.axis_index("dp") // 2
        return jnp.where(chip % 2 == 0, chip // 2, self.count - 1 - chip // 2)

    def chip_at(self, offset):
        place = (self.here() + offset + self.count) % self.count
        column = self.count // 2
        return jnp.where(place < column, 2 * place, 2 * (self.count - 1 - place) + 1)

    def on(self, field):
        return lax.ppermute(field, "dp", self.onward)

    def back(self, field):
        return lax.ppermute(field, "dp", self.backward)

    def twin(self, field):
        return lax.ppermute(field, "dp", self.twins)


def after(field, *others):
    return lax.optimization_barrier((field, *others))[0]


def swap_mp(field):
    return lax.ppermute(field, "mp", [(0, 1), (1, 0)])


def both_halves(own, other, half):
    return jnp.where(
        half == 0, jnp.concatenate([own, other]), jnp.concatenate([other, own])
    )


def pick(field, *places):
    for place in places:
        field = lax.dynamic_index_in_dim(field, place, 0, keepdims=False)
    return field


def reduce_ring_first(ring, field, half, beside):
    far = ring.count // 2

    def block(offset):
        return lax.dynamic_index_in_dim(field, ring.chip_at(offset), 1, keepdims=False)

    far_block = block(far)
    on = ring.on(far_block[0])
    back = ring.back(far_block[1])
    own = block(far - 1)
    on = ring.on(jnp.stack([add(own[0], on).astype(BF16), own[1]]))
    own = block(1 - far)
    back = ring.back(jnp.stack([own[0], add(own[1], back).astype(BF16)]))
    for distance in range(far - 2, 0, -1):
        if distance == 1:
            on = after(on, beside)
        on = ring.on(add(block(distance), on).astype(BF16))
        back = ring.back(add(block(-distance), back).astype(BF16))
    total = add(block(0), on, back)
    other = swap_mp(pick(total.astype(BF16), 1 - half))
    return add(pick(total, half), other)


def gather_small(field, dp_count):
    step = dp_count // 2
    while step > 1:
        other = lax.ppermute(field, "dp", [(i, i ^ step) for i in range(dp_count)])
        field = jnp.concatenate([field, other])
        step //= 2
    field = jnp.concatenate([field, swap_mp(field)])
    other = lax.ppermute(field, "dp", [(i, i ^ 1) for i in range(dp_count)])
    return jnp.concatenate([field, other])


def on_device(
    tokens,
    conditioning,
    sigmas,
    positions,
    cotangent,
    owners,
    master,
    moment_one,
    moment_two,
    scale_state,
):
    dp_count = lax.axis_size("dp")
    mp_count = lax.axis_size("mp")
    dp_index = lax.axis_index("dp")
    mp_index = lax.axis_index("mp")
    images = conditioning.shape[0] // mp_count
    toks = images * SEQ
    slots = master.shape[1]
    unit_rows = master.shape[2]
    unit_count = owners.shape[1]
    heads_here = scale_state.shape[1]
    paired = dp_count * 2 == UNIT
    core = dp_index % 2 if paired else 0

    def mine(field, rows):
        return lax.dynamic_slice_in_dim(field, mp_index * rows, rows, 0)

    rounded = master[0].astype(BF16)
    gathered = lax.all_gather(rounded, ("dp", "mp"), axis=0, tiled=True)
    halves_here = jnp.concatenate([owners[0].astype(F32), scale_state[0]])
    halves_all = both_halves(halves_here[None], swap_mp(halves_here[None]), mp_index)
    owners_all = halves_all[:, :unit_count].astype(jnp.int32)
    scales_all = halves_all[:, unit_count:].reshape(-1)
    before = jnp.stack([slots_before(owners_all[half]) for half in range(mp_count)])
    half_ids = lax.broadcasted_iota(jnp.int32, owners_all.shape, 0)
    place = (owners_all * mp_count + half_ids) * slots + before
    by_chunk = place.reshape(mp_count, -1, SPAN)
    order = {}
    for chunk, kind in enumerate(STACK_ORDER):
        order.setdefault(kind, []).append(chunk)
    source = jnp.concatenate(
        [
            by_chunk[:, order[kind][0] : order[kind][-1] + 1].reshape(-1)
            for kind in ("A1", "A2", "Q", "K", "V", "O", "G", "U", "F")
        ]
    )
    square = sigmas * sigmas
    data_square = SIGMA_DATA * SIGMA_DATA
    loss_weight = 4.0 * square * data_square / ((square + data_square) * (square + data_square))
    scalars = jnp.concatenate([scales_all, jnp.sqrt(scales_all), mine(loss_weight, images)])
    cosine, sine = rope_tables(mine(positions, images))
    cond = jnp.pad(mine(conditioning, images).astype(BF16), ((0, 16 - images), (0, 0)))

    (
        out_low,
        grad_low,
        hid_keep,
        hid_send,
        gu_keep,
        gu_send,
        at_keep,
        at_send,
        normed_one,
        normed_two,
        grad_out,
        grad_mid,
        grad_gains,
        grad_scale,
    ) = run_layer(
        images,
        source,
        scalars,
        mine(tokens, toks),
        mine(cotangent, toks),
        cond,
        cosine,
        sine,
        deal_matrix(core),
        gathered,
    )

    out_other = swap_mp(out_low)
    grad_other = swap_mp(grad_low)
    output = both_halves(out_low, out_other, mp_index).astype(F32)
    input_grad = both_halves(grad_low, grad_other, mp_index).astype(F32)

    def small_factors(*before_it):
        cond_own = mine(conditioning, images).astype(BF16).astype(F32)
        scale_row = jnp.pad(grad_scale[:, 0], (0, D - 16))[None]
        own = jnp.concatenate([cond_own, grad_gains, scale_row, jnp.zeros((1, D), F32)], axis=0)
        small = gather_small(after(own, *before_it), dp_count).reshape(-1, 3 * images + 2, D)
        scale_sum = jnp.sum(small[:, 3 * images, :HEADS], axis=0) / (2.0 * jnp.sqrt(scales_all))
        gains = [
            small[:, place * images : (place + 1) * images].reshape(-1, D) for place in (1, 2)
        ]
        return (
            small[:, :images].reshape(-1, D),
            jnp.concatenate(gains, axis=1),
            lax.dynamic_slice_in_dim(scale_sum, mp_index * heads_here, heads_here, 0),
        )

    if paired:
        ring = Ring(dp_count)
        chunks = FF // CHUNK
        here = chunks // mp_count
        hid_both = (hid_keep, ring.twin(hid_send))
        out_both = (grad_out, ring.twin(grad_out))
        gu_both = (gu_keep, ring.twin(gu_send))
        two_both = (normed_two, ring.twin(normed_two))
        at_both = (at_keep, ring.twin(at_send))
        mid_both = (grad_mid, ring.twin(grad_mid))
        one_both = (normed_one, ring.twin(normed_one))
        grad_fg = weight_grads(
            ((hid_both, out_both, 0, here), (gu_both, two_both, 0, here)), mp_count
        )
        grad_rest = weight_grads(
            (
                (gu_both, two_both, chunks, here),
                (at_both, mid_both, 0, 1),
                (at_both, one_both, mp_count, 1),
                (at_both, one_both, 2 * mp_count, 1),
                (at_both, one_both, 3 * mp_count, 1),
            ),
            mp_count,
        )
        cond_all, gains_all, scale_grad = small_factors(grad_fg, grad_rest)
        sum_fg = reduce_ring_first(ring, grad_fg, mp_index, out_other)
        sum_rest = reduce_ring_first(ring, grad_rest, mp_index, grad_other)
        wanted = lax.broadcasted_iota(jnp.int32, (2 * SPAN, D), 0)
        feature = lax.broadcasted_iota(jnp.int32, (2 * SPAN, D), 1)
        wanted = (mp_index * SPAN + wanted % SPAN) * UNIT + 2 * dp_index + wanted // SPAN
        cond_rows = dot_nt((feature == wanted).astype(F32), cond_all)
        sum_a = jnp.dot(
            cond_rows,
            gains_all,
            precision=lax.Precision.HIGHEST,
            preferred_element_type=F32,
        )
        by_kind = jnp.concatenate(
            [
                sum_a[None, :, :D],
                sum_rest[here + 1 :],
                sum_rest[here : here + 1],
                sum_a[None, :, D:],
                sum_fg[here:],
                sum_rest[:here],
                sum_fg[:here],
            ]
        )
        grad_shards = (
            by_kind.reshape(-1, 2, SPAN, D).transpose(0, 2, 1, 3).reshape(unit_count, 2 * D)
        )
    else:
        def units_of(parts, field, kinds):
            here = parts[0].shape[0] // (kinds * mp_count)
            sides = jnp.stack(
                [
                    jnp.concatenate(
                        [
                            weight_grads(
                                (((part,), (field,), kind * mp_count * here, here),), mp_count
                            )
                            for kind in range(kinds)
                        ],
                        axis=2,
                    )
                    for part in parts
                ]
            )
            sides = sides.reshape(2, mp_count, UNIT // 4, -1, 2, SPAN, D)
            return sides.transpose(1, 3, 5, 2, 0, 4, 6).reshape(mp_count, -1, unit_rows * D)

        summed = lax.psum_scatter(
            jnp.concatenate(
                [
                    units_of((at_keep[2:], at_send[2:]), normed_one, 3),
                    units_of((at_keep[:2], at_send[:2]), grad_mid, 1),
                    units_of((gu_keep, gu_send), normed_two, 2),
                    units_of((hid_keep, hid_send), grad_out, 1),
                ],
                axis=1,
            ),
            "mp",
            scatter_dimension=0,
            tiled=True,
        )[0]
        summed = lax.psum_scatter(summed, "dp", scatter_dimension=1, tiled=True).astype(F32)
        cond_all, gains_all, scale_grad = small_factors()
        cond_half = lax.dynamic_slice_in_dim(
            cond_all, mp_index * SPAN * unit_rows, SPAN * unit_rows, 1
        )
        sum_a = lax.dot_general(
            cond_half,
            gains_all,
            (((0,), (0,)), ((), ())),
            precision=lax.Precision.HIGHEST,
            preferred_element_type=F32,
        )
        width = unit_rows * D // dp_count

        def piece(field):
            return lax.dynamic_slice_in_dim(
                field.reshape(SPAN, unit_rows * D), dp_index * width, width, 1
            )

        grad_shards = jnp.concatenate(
            [
                piece(sum_a[:, :D]),
                summed[: 4 * SPAN],
                piece(sum_a[:, D:]),
                summed[4 * SPAN :],
            ]
        )

    placed = owners[0] * slots + slots_before(owners[0])
    total_slots = dp_count * slots
    slot_ids = lax.broadcasted_iota(jnp.int32, (total_slots, unit_count), 0)
    unit_ids = lax.broadcasted_iota(jnp.int32, (total_slots, unit_count), 1)
    match_table = slot_ids == placed[None, :]
    source_unit = jnp.sum(jnp.where(match_table, unit_ids, 0), axis=1)
    filled = jnp.any(match_table, axis=1)
    outgoing = jnp.where(
        filled[:, None], jnp.take(grad_shards.astype(BF16), source_unit, axis=0), 0.0
    )
    owned = lax.all_to_all(outgoing, "dp", split_axis=0, concat_axis=1, tiled=True)
    owned_grads = owned.reshape(slots, unit_rows, D).astype(F32)
    first_new = BETA_ONE * moment_one[0] + (1.0 - BETA_ONE) * owned_grads
    second_new = BETA_TWO * moment_two[0] + (1.0 - BETA_TWO) * owned_grads * owned_grads
    master_new = adam_step(master[0], first_new, second_new, LEARN_RATE)
    scale_first = BETA_ONE * scale_state[1] + (1.0 - BETA_ONE) * scale_grad
    scale_second = BETA_TWO * scale_state[2] + (1.0 - BETA_TWO) * scale_grad * scale_grad
    scale_new = adam_step(scale_state[0], scale_first, scale_second, SCALE_RATE)
    scale_update = jnp.stack([scale_first, scale_new])
    return (
        output,
        input_grad,
        grad_shards[None],
        master_new[None],
        first_new[None],
        second_new[None],
        scale_update,
        scale_second,
    )


def solution(mesh):
    in_specs = (
        P("dp", None),
        P("dp", None),
        P("dp"),
        P("dp", None, None),
        P("dp", None),
        P("mp", None),
        P("mp", "dp", None, None),
        P("mp", "dp", None, None),
        P("mp", "dp", None, None),
        P(None, "mp"),
    )
    out_specs = (
        P("dp", None),
        P("dp", None),
        P("mp", None, "dp"),
        P("mp", "dp", None, None),
        P("mp", "dp", None, None),
        P("mp", "dp", None, None),
        P(None, "mp"),
        P("mp"),
    )
    return jax.shard_map(
        on_device, mesh=mesh, in_specs=in_specs, out_specs=out_specs, check_vma=False
    )
```

```python
import math

import jax
import jax.numpy as jnp
import numpy as np
from jax import lax
from jax.experimental import pallas as pl
from jax.experimental.pallas import tpu as pltpu
from jax.sharding import PartitionSpec as P

D = 768
HEADS = 12
HD = 64
FF = 2304
SIDE = 16
STEP = 10
SEQ = 256
UNIT = 32
SPAN = 12
CHUNK = SPAN * UNIT
HALF_CHUNK = CHUNK // 2

NORM_EPS = 1e-06
COS_EPS = 1e-06
SIGMA_DATA = 0.5
BETA_ONE = 0.5
BETA_TWO = 0.5
ADAM_EPS = 1e-08
WEIGHT_DECAY = 0.01
LEARN_RATE = 0.04
SCALE_RATE = 1.0
ROOT_HALF = 0.7071067811865476
INV_ROOT_TWO_PI = 0.3989422804014327

F32 = jnp.float32
BF16 = jnp.bfloat16
VMEM_BYTES = 60 * 1024 * 1024

STACK_ORDER = ("A1", "Q", "K", "V", "O", "A2", "G", "G", "G", "U", "U", "U", "F", "F", "F")
ROW_A1, ROW_A2, ROW_Q, ROW_K, ROW_V, ROW_O = (D * place for place in range(6))
ROW_G = 6 * D
ROW_U = ROW_G + FF
ROW_F = ROW_U + FF
ROWS_ALL = ROW_F + FF


def dot_nn(left, right):
    return jnp.dot(left, right, preferred_element_type=F32)


def dot_nt(left, right):
    return lax.dot_general(left, right, (((1,), (1,)), ((), ())), preferred_element_type=F32)


def slots_before(owner_list):
    unit_count = owner_list.shape[0]
    same_owner = owner_list[:, None] == owner_list[None, :]
    row_ids = lax.broadcasted_iota(jnp.int32, (unit_count, unit_count), 0)
    col_ids = lax.broadcasted_iota(jnp.int32, (unit_count, unit_count), 1)
    return jnp.sum(jnp.where(same_owner & (col_ids < row_ids), 1, 0), axis=1).astype(jnp.int32)


def rope_tables(positions):
    quarter = HD // 8
    head_ids = lax.broadcasted_iota(jnp.int32, (HEADS, quarter), 0)
    column = lax.broadcasted_iota(jnp.int32, (HEADS, quarter), 1)
    flat_index = (column * HEADS + head_ids).astype(F32)
    low_log = math.log(math.pi)
    high_log = math.log(10.0 * math.pi)
    frequency = jnp.exp(low_log + (high_log - low_log) * flat_index / (HEADS * quarter))
    placed = (2.0 * positions.astype(F32) + 1.0) / SIDE - 1.0
    along_rows = placed[:, 0].reshape(1, 1, -1) * frequency[:, :, None]
    along_cols = placed[:, 1].reshape(1, 1, -1) * frequency[:, :, None]
    angles = jnp.concatenate([along_rows, along_cols], axis=1).reshape(HEADS * 2 * quarter, -1)
    return jnp.cos(angles), jnp.sin(angles)


def deal_matrix(core):
    target = lax.broadcasted_iota(jnp.int32, (CHUNK, CHUNK), 0)
    source = lax.broadcasted_iota(jnp.int32, (CHUNK, CHUNK), 1)
    parity = (target // HALF_CHUNK + core) % 2
    inner = target % HALF_CHUNK
    piece = inner // (2 * SPAN)
    row = inner // SPAN % 2
    unit = inner % SPAN
    return (source == unit * UNIT + 4 * piece + 2 * parity + row).astype(BF16)


def layer_kernel(
    images,
    slots_refs,
    place_ref,
    ends_ref,
    scal_ref,
    x_ref,
    cot_ref,
    gb_ref,
    cond_ref,
    cos_ref,
    sin_ref,
    deal_ref,
    outs_hbm,
    early_keep,
    early_send,
    late_keep,
    late_send,
    n2_hbm,
    mids_hbm,
    gain_hbm,
    ds_hbm,
    w,
    unit_s,
    coef_s,
    qtok_s,
    qk_s,
    v_s,
    o_s,
    x2_s,
    n1_s,
    n2_s,
    ga_s,
    do_s,
    dot_s,
    ff_s,
    dn2_s,
    dqkv_s,
    early_s,
    late_s,
    outs_s,
    gain_s,
    ds_s,
    dsout_s,
    w_sem,
    o_sem,
):
    toks = images * SEQ
    sends = []

    def send(src, dst):
        copy = pltpu.make_async_copy(src, dst, o_sem.at[len(sends)])
        copy.start()
        sends.append(copy)

    groups = (0, ROW_Q, ROW_O, ROW_G, ROWS_ALL)

    def fetch(low, high):
        first = 0
        for array, slots_ref in enumerate(slots_refs):

            @pl.loop(ends_ref[array, low // 3], ends_ref[array, low // 3 + 1])
            def _(index, slots_ref=slots_ref, first=first):
                unit = place_ref[0, first + index]
                group = jnp.int32(low)
                for bound in groups[low + 1 : high]:
                    group += jnp.where(unit >= bound // UNIT, 1, 0)
                pltpu.make_async_copy(
                    slots_ref.at[place_ref[1, first + index]],
                    w.at[pl.ds(pl.multiple_of(unit * UNIT, UNIT), UNIT)],
                    w_sem.at[group],
                ).start()

            first += slots_ref.shape[0]

    fetch(0, 3)

    def weights_here(index):
        low, high = groups[index : index + 2]
        region = w.at[pl.ds(low, high - low)]
        pltpu.make_async_copy(region, region, w_sem.at[index]).wait()

    def image_rows(image):
        return pl.ds(image * SEQ, SEQ)

    weights_here(0)
    fetch(3, 4)
    gain_one = 1.0 + dot_nn(cond_ref[...], w[ROW_A1 : ROW_A1 + D])
    gain_two = 1.0 + dot_nn(cond_ref[...], w[ROW_A2 : ROW_A2 + D])
    for image in range(images):
        x = x_ref[image_rows(image)]
        inverse = lax.rsqrt(jnp.mean(x * x, axis=-1, keepdims=True) + NORM_EPS)
        n1_s[image_rows(image)] = (x * inverse * gain_one[image : image + 1]).astype(BF16)
    send(n1_s, mids_hbm.at[1])
    weights_here(1)
    unit_s[:D] = dot_nt(w[ROW_Q : ROW_Q + D], n1_s[...])
    unit_s[D:] = dot_nt(w[ROW_K : ROW_K + D], n1_s[...])
    v_s[...] = dot_nt(w[ROW_V : ROW_V + D], n1_s[...]).astype(BF16)

    @pl.loop(0, 2 * HEADS)
    def _(index):
        head = lax.rem(index, HEADS)
        rows = pl.ds(pl.multiple_of(index * HD, HD), HD)
        angle_rows = pl.ds(pl.multiple_of(head * 16, 16), 16)
        raw = unit_s[rows]
        inverse = lax.rsqrt(jnp.sum(raw * raw, axis=0, keepdims=True) + COS_EPS)
        unit = raw * inverse
        root = scal_ref[HEADS + head]
        unit_s[rows] = unit
        coef_s[pl.ds(index, 1)] = root * inverse
        scaled = unit * root
        first, second = scaled[:16], scaled[16:32]
        cosine, sine = cos_ref[angle_rows], sin_ref[angle_rows]
        turned = jnp.concatenate(
            [first * cosine - second * sine, second * cosine + first * sine, scaled[32:]], axis=0
        )
        qk_s[rows] = turned.astype(BF16)

    qtok_s[...] = qk_s[:D].T

    def pair_parts(image, pair, half):
        head = pair * 2 + half
        rows = pl.ds(pl.multiple_of(head * HD, HD), HD)
        key_rows = pl.ds(pl.multiple_of(D + head * HD, HD), HD)
        lanes = pl.ds(pl.multiple_of(pair * 2 * HD, 2 * HD), 2 * HD)
        query = qtok_s[image_rows(image), lanes][:, half * HD : (half + 1) * HD]
        key = qk_s[key_rows, image_rows(image)]
        value = v_s[rows, image_rows(image)]
        exp_scores = jnp.exp(dot_nn(query, key) - scal_ref[head])
        probs = exp_scores * (1.0 / jnp.sum(exp_scores, axis=-1, keepdims=True))
        return head, rows, key_rows, lanes, key, value, probs

    @pl.loop(0, HEADS // 2)
    def _(pair):
        for image in range(images):
            mixed = []
            for half in range(2):
                _, _, _, lanes, _, value, probs = pair_parts(image, pair, half)
                mixed.append(dot_nt(probs.astype(BF16), value))
            o_s[image_rows(image), lanes] = jnp.concatenate(mixed, axis=1).astype(BF16)

    weights_here(2)
    x2_s[...] = x_ref[...] + dot_nn(o_s[...], w[ROW_O : ROW_O + D])
    for image in range(images):
        x2 = x2_s[image_rows(image)]
        inverse = lax.rsqrt(jnp.mean(x2 * x2, axis=-1, keepdims=True) + NORM_EPS)
        n2_s[image_rows(image)] = (x2 * inverse * gain_two[image : image + 1]).astype(BF16)
    send(n2_s, n2_hbm)

    weights_here(3)
    chunks = FF // CHUNK

    def deal(field, store, place):
        dealt = dot_nt(deal_ref[...], field).astype(BF16)
        store[0, place] = dealt[:HALF_CHUNK]
        store[1, place] = dealt[HALF_CHUNK:]

    @pl.loop(0, chunks)
    def _(chunk):
        def part(base):
            return w[pl.ds(pl.multiple_of(base + chunk * CHUNK, CHUNK), CHUNK)]

        gate = dot_nt(n2_s[...], part(ROW_G))
        up = dot_nt(n2_s[...], part(ROW_U))
        grad_hidden = dot_nt(gb_ref[...], part(ROW_F))
        phi_sum = 0.5 * (1.0 + lax.erf(gate * ROOT_HALF))
        density = INV_ROOT_TWO_PI * jnp.exp(-0.5 * gate * gate)
        gelu = gate * phi_sum
        hidden = (gelu * up).astype(BF16)
        grad_gate = (grad_hidden * up * (phi_sum + gate * density)).astype(BF16)
        grad_up = (grad_hidden * gelu).astype(BF16)
        ff = dot_nn(hidden, part(ROW_F))
        dn2 = dot_nn(grad_gate, part(ROW_G)) + dot_nn(grad_up, part(ROW_U))

        @pl.when(chunk == 0)
        def _():
            ff_s[...] = ff
            dn2_s[...] = dn2

        @pl.when(chunk > 0)
        def _():
            ff_s[...] += ff
            dn2_s[...] += dn2

        deal(hidden, early_s, chunk)
        deal(grad_gate, early_s, chunks + chunk)
        deal(grad_up, late_s, chunk)

    send(early_s.at[0], early_keep)
    send(early_s.at[1], early_send)
    outs_s[0] = (x2_s[...] + ff_s[...]).astype(BF16)
    send(outs_s.at[0], outs_hbm.at[0])

    def norm_back(x, gain, grad_normed):
        inverse = lax.rsqrt(jnp.mean(x * x, axis=-1, keepdims=True) + NORM_EPS)
        scaled = grad_normed * gain
        inner = jnp.mean(x * scaled, axis=-1, keepdims=True)
        grad_x = inverse * scaled - x * (inverse * inverse * inverse * inner)
        return grad_x, jnp.sum(grad_normed * x * inverse, axis=0, keepdims=True)

    for image in range(images):
        rows = image_rows(image)
        grad_x, grad_gain = norm_back(x2_s[rows], gain_two[image : image + 1], dn2_s[rows])
        grad = cot_ref[rows].astype(F32) * scal_ref[2 * HEADS + image] + grad_x
        x2_s[rows] = grad
        ga_s[rows] = grad.astype(BF16)
        gain_s[pl.ds(images + image, 1)] = grad_gain
    send(ga_s, mids_hbm.at[0])

    do_s[...] = dot_nt(ga_s[...], w[ROW_O : ROW_O + D]).astype(BF16)
    dot_s[...] = dot_nt(w[ROW_O : ROW_O + D], ga_s[...]).astype(BF16)
    ds_s[...] = jnp.zeros_like(ds_s)

    @pl.loop(0, HEADS // 2)
    def _(pair):
        for image in range(images):
            cols = image_rows(image)
            for half in range(2):
                head, rows, key_rows, lanes, key, value, probs = pair_parts(image, pair, half)
                grad_mixed = do_s[cols, lanes][:, half * HD : (half + 1) * HD]
                grad_probs = dot_nn(grad_mixed, value)
                inner = jnp.sum(probs * grad_probs, axis=-1, keepdims=True)
                grad_scores = (probs * (grad_probs - inner)).astype(BF16)
                grad_query = dot_nt(key, grad_scores)
                grad_key = dot_nn(qk_s[rows, cols], grad_scores)
                grad_value = dot_nn(dot_s[rows, cols], probs.astype(BF16))
                angle_rows = pl.ds(pl.multiple_of(head * 16, 16), 16)
                cosine, sine = cos_ref[angle_rows, cols], sin_ref[angle_rows, cols]
                along = jnp.zeros((1, SEQ), F32)
                for grad, own_rows, place in (
                    (grad_query, rows, head),
                    (grad_key, key_rows, HEADS + head),
                ):
                    first, second = grad[:16], grad[16:32]
                    back = jnp.concatenate(
                        [
                            first * cosine + second * sine,
                            second * cosine - first * sine,
                            grad[32:],
                        ],
                        axis=0,
                    )
                    unit = unit_s[own_rows, cols]
                    inner_unit = jnp.sum(unit * back, axis=0, keepdims=True)
                    along += inner_unit
                    dqkv_s[own_rows, cols] = (
                        coef_s[pl.ds(place, 1), cols] * (back - unit * inner_unit)
                    ).astype(BF16)
                value_rows = pl.ds(pl.multiple_of(2 * D + head * HD, HD), HD)
                dqkv_s[value_rows, cols] = grad_value.astype(BF16)
                ds_s[pl.ds(head, 1)] += along

    for place in range(2):
        deal(o_s[:, place * CHUNK : (place + 1) * CHUNK], late_s, chunks + place)
    for place in range(6):
        dealt = dot_nn(deal_ref[...], dqkv_s[place * CHUNK : (place + 1) * CHUNK]).astype(BF16)
        late_s[0, chunks + 2 + place] = dealt[:HALF_CHUNK]
        late_s[1, chunks + 2 + place] = dealt[HALF_CHUNK:]
    send(late_s.at[0], late_keep)
    send(late_s.at[1], late_send)
    dsout_s[...] = jnp.broadcast_to(jnp.sum(ds_s[...], axis=1, keepdims=True), dsout_s.shape)
    send(dsout_s, ds_hbm)

    dn1 = dot_nn(dqkv_s[:D].T, w[ROW_Q : ROW_Q + D])
    dn1 += dot_nn(dqkv_s[D : 2 * D].T, w[ROW_K : ROW_K + D])
    dn1 += dot_nn(dqkv_s[2 * D :].T, w[ROW_V : ROW_V + D])
    dn2_s[...] = dn1
    for image in range(images):
        rows = image_rows(image)
        grad_x, grad_gain = norm_back(x_ref[rows], gain_one[image : image + 1], dn2_s[rows])
        outs_s[1, rows] = (x2_s[rows] + grad_x).astype(BF16)
        gain_s[pl.ds(image, 1)] = grad_gain
    send(outs_s.at[1], outs_hbm.at[1])
    send(gain_s, gain_hbm)
    for copy in sends:
        copy.wait()


def run_layer(images, places, ends, scalars, x, cotangent, grad_out, cond, cosine, sine, deal, slots):
    toks = images * SEQ
    chunks = FF // CHUNK
    any_spec = pl.BlockSpec(memory_space=pl.ANY)
    vmem = pl.BlockSpec(memory_space=pltpu.VMEM)
    smem = pl.BlockSpec(memory_space=pltpu.SMEM)
    field = jax.ShapeDtypeStruct((toks, D), BF16)

    def dealt(count):
        return jax.ShapeDtypeStruct((count, HALF_CHUNK, toks), BF16)

    pair = jax.ShapeDtypeStruct((2, toks, D), BF16)
    late = chunks + 8
    outs = [pair, dealt(2 * chunks), dealt(2 * chunks), dealt(late), dealt(late), field, pair]
    outs += [
        jax.ShapeDtypeStruct((2 * images, D), F32),
        jax.ShapeDtypeStruct((16, 128), F32),
    ]
    wide = pltpu.VMEM((toks, D), F32)
    low = pltpu.VMEM((toks, D), BF16)
    scratch = [
        pltpu.VMEM((ROWS_ALL, D), BF16),
        pltpu.VMEM((2 * D, toks), F32),
        pltpu.VMEM((2 * HEADS, toks), F32),
        low,
        pltpu.VMEM((2 * D, toks), BF16),
        pltpu.VMEM((D, toks), BF16),
        low,
        wide,
        low,
        low,
        low,
        low,
        pltpu.VMEM((D, toks), BF16),
        wide,
        wide,
        pltpu.VMEM((3 * D, toks), BF16),
        pltpu.VMEM((2, 2 * chunks, HALF_CHUNK, toks), BF16),
        pltpu.VMEM((2, late, HALF_CHUNK, toks), BF16),
        pltpu.VMEM((2, toks, D), BF16),
        pltpu.VMEM((2 * images, D), F32),
        pltpu.VMEM((16, SEQ), F32),
        pltpu.VMEM((16, 128), F32),
        pltpu.SemaphoreType.DMA((4,)),
        pltpu.SemaphoreType.DMA((16,)),
    ]

    operands = [places, ends, scalars, x, cotangent, grad_out, cond, cosine, sine, deal]
    here = len(operands)

    def body(*refs):
        layer_kernel(
            images, refs[here : here + len(slots)], *refs[:here], *refs[here + len(slots) :]
        )

    return pl.pallas_call(
        body,
        out_shape=outs,
        in_specs=[smem] * 3 + [vmem] * 7 + [any_spec] * len(slots),
        out_specs=[any_spec] * len(outs),
        scratch_shapes=scratch,
        compiler_params=pltpu.CompilerParams(vmem_limit_bytes=VMEM_BYTES),
        cost_estimate=pl.CostEstimate(
            flops=2 * 3 * ROWS_ALL * D * toks, bytes_accessed=ROWS_ALL * D * 4, transcendentals=0
        ),
        name="layer",
    )(*operands, *slots)


def weight_grads(groups, halves):
    rows, toks = groups[0][0][0].shape[1:]
    pieces = rows // (2 * SPAN)
    operands, specs, places, flops, moved = [], [], [], 0, 0
    total = 0
    for lefts, rights, first, here in groups:
        assert first % here == 0
        places.append((len(lefts), len(operands), total, here))
        total += here
        for left in lefts:
            operands.append(left)
            specs.append(
                pl.BlockSpec((here, rows, toks), lambda half, at=first // here: (at + half, 0, 0))
            )
        for right in rights:
            field, at = right if isinstance(right, tuple) else (right[None], 0)
            operands.append(field)
            specs.append(pl.BlockSpec((None, toks, D), lambda half, at=at: (at, 0, 0)))
        flops += 2 * len(lefts) * here * halves * rows * toks * D
        moved += len(lefts) * 2 * (here * halves * rows * toks + toks * D)

    def body(*refs):
        out_ref = refs[-1]
        for count, start, at, here in places:
            lefts, rights = refs[start : start + count], refs[start + count : start + 2 * count]
            summed = dot_nn(lefts[0][...].reshape(here * rows, toks), rights[0][...])
            for left, right in zip(lefts[1:], rights[1:]):
                summed += dot_nn(left[...].reshape(here * rows, toks), right[...])
            for chunk in range(here):
                out_ref[0, :, at + chunk] = (
                    summed[chunk * rows : (chunk + 1) * rows]
                    .reshape(pieces, 2 * SPAN, D)
                    .astype(BF16)
                )

    return pl.pallas_call(
        body,
        out_shape=jax.ShapeDtypeStruct((halves, pieces, total, 2 * SPAN, D), BF16),
        grid=(halves,),
        in_specs=specs,
        out_specs=pl.BlockSpec(
            (1, pieces, total, 2 * SPAN, D), lambda half: (half, 0, 0, 0, 0)
        ),
        compiler_params=pltpu.CompilerParams(vmem_limit_bytes=VMEM_BYTES),
        cost_estimate=pl.CostEstimate(
            flops=flops,
            bytes_accessed=moved + halves * pieces * total * 4 * SPAN * D,
            transcendentals=0,
        ),
        name="weight_grads",
    )(*operands)


def adam_step(weights, first_new, second_new, rate):
    fix_one = 1.0 - math.pow(BETA_ONE, STEP)
    fix_two = 1.0 - math.pow(BETA_TWO, STEP)
    return weights * (1.0 - rate * WEIGHT_DECAY) - rate * (first_new / fix_one) / (
        jnp.sqrt(second_new / fix_two) + ADAM_EPS
    )


def add(*terms):
    total = terms[0].astype(F32)
    for term in terms[1:]:
        total = total + term.astype(F32)
    return total


class Ring:
    def __init__(self, dp_count):
        self.count = dp_count // 2
        pairs = []
        for place in range(self.count):
            for core in range(2):
                pairs.append(
                    (self.chip(place) * 2 + core, self.chip((place + 1) % self.count) * 2 + core)
                )
        self.onward = pairs
        self.backward = [(b, a) for a, b in pairs]
        self.twins = [(index, index ^ 1) for index in range(dp_count)]

    def chip(self, place):
        column = self.count // 2
        return 2 * place if place < column else 2 * (self.count - 1 - place) + 1

    def here(self):
        chip = lax.axis_index("dp") // 2
        return jnp.where(chip % 2 == 0, chip // 2, self.count - 1 - chip // 2)

    def chip_at(self, offset):
        place = (self.here() + offset + self.count) % self.count
        column = self.count // 2
        return jnp.where(place < column, 2 * place, 2 * (self.count - 1 - place) + 1)

    def on(self, field):
        return lax.ppermute(field, "dp", self.onward)

    def back(self, field):
        return lax.ppermute(field, "dp", self.backward)

    def twin(self, field):
        return lax.ppermute(field, "dp", self.twins)


def after(field, *others):
    return lax.optimization_barrier((field, others))[0]


def swap_mp(field):
    return lax.ppermute(field, "mp", [(0, 1), (1, 0)])


class Labels:
    def __init__(self, rows):
        self.rows = list(rows)

    def __getitem__(self, cut):
        return Labels(self.rows[cut])

    def moved(self, hop, mp, core):
        return Labels((h + hop, m ^ mp, c ^ core, slot) for h, m, c, slot in self.rows)


class LabelMoves:
    def on(self, field):
        return field.moved(-1, 0, 0)

    def back(self, field):
        return field.moved(1, 0, 0)

    def swap(self, field):
        return field.moved(0, 1, 0)

    def twin(self, field):
        return field.moved(0, 0, 1)

    def cat(self, *fields):
        return Labels(row for field in fields for row in field.rows)

    def together(self, *fields):
        return fields


class Moves:
    def __init__(self, ring):
        self.on, self.back, self.twin, self.swap = ring.on, ring.back, ring.twin, swap_mp

    def cat(self, *fields):
        return jnp.concatenate(fields)

    def together(self, *fields):
        return lax.optimization_barrier(fields)


def gather_slots(moves, own, slots, beside):
    cat, on, back, swap, twin = moves.cat, moves.on, moves.back, moves.swap, moves.twin
    cut = slots // 2
    rest = slots - cut
    first, second = own[:cut], own[cut:]
    hop = [on(second), back(second), swap(first), twin(own)]
    f0, b0, y0, c0, second, *soon = moves.together(*hop, second, *beside[0])
    wide = cat(first, y0)
    hop = [on(wide), back(wide), swap(second), twin(cat(y0, f0, b0))]
    f1, b1, y1, c1, f0, b0 = moves.together(*hop, f0, b0)
    hop = [on(cat(f0, f1)), back(cat(b0, b1)), swap(cat(f0, b0)), twin(cat(f1, b1, y1))]
    f2, b2, y2, c2, *later = moves.together(*hop, *beside[1](*soon))
    crossing = cat(f2[:rest], b2[:rest])
    hop = [on(f2), back(b2), swap(crossing), twin(cat(f2, b2, y2))]
    f3, b3, y3, c3 = moves.together(*hop)
    half = (slots + cut) // 2
    crossing = cat(f3[:rest], b3[:rest])
    hop = [on(f3[:half]), back(b3[half:]), swap(crossing), twin(cat(f3, b3, y3))]
    f4, b4, y4, c4 = moves.together(*hop)
    y5 = swap(cat(f4[:rest], b4[: max(0, rest - half)]))
    c5 = [twin(f4), twin(b4), twin(y4)]
    return [own, f0, b0, y0, c0, f1, b1, y1, c1, f2, b2, y2, c2, f3, b3, y3, c3, f4, b4, y4, c4, y5] + c5 + [twin(y5)], later


def both_halves(own, other, half, axis=0):
    return jnp.where(
        half == 0,
        jnp.concatenate([own, other], axis=axis),
        jnp.concatenate([other, own], axis=axis),
    )


def pick(field, *places):
    for place in places:
        field = lax.dynamic_index_in_dim(field, place, 0, keepdims=False)
    return field


class RingSum:
    def __init__(self, ring, fields, half):
        self.ring, self.fields, self.half = ring, fields, half
        self.distance = ring.count // 2
        self.on = self.back = None

    def block(self, offset):
        place = self.ring.chip_at(offset)
        parts = [
            lax.dynamic_index_in_dim(field, place, 1, keepdims=False) for field in self.fields
        ]
        return parts[0] if len(parts) == 1 else jnp.concatenate(parts, axis=1)

    def step(self, *others):
        ring, far, distance = self.ring, self.ring.count // 2, self.distance
        if distance == far:
            block = self.block(far)
            on, back = block[0], block[1]
        else:
            on, back = self.block(distance), self.block(-distance)
            if distance == far - 1:
                on = jnp.stack([add(on[0], self.on).astype(BF16), on[1]])
                back = jnp.stack([back[0], add(back[1], self.back).astype(BF16)])
            else:
                on, back = add(on, self.on).astype(BF16), add(back, self.back).astype(BF16)
        if others:
            on, back = after(on, *others), after(back, *others)
        self.on, self.back = lax.optimization_barrier((ring.on(on), ring.back(back)))
        self.distance -= 1
        return self.on, self.back

    def total(self):
        total = add(self.block(0), self.on, self.back)
        other = swap_mp(pick(total.astype(BF16), 1 - self.half))
        return add(pick(total, self.half), other)


def on_device(
    tokens,
    conditioning,
    sigmas,
    positions,
    cotangent,
    owners,
    master,
    moment_one,
    moment_two,
    scale_state,
):
    dp_count = lax.axis_size("dp")
    mp_count = lax.axis_size("mp")
    dp_index = lax.axis_index("dp")
    mp_index = lax.axis_index("mp")
    images = conditioning.shape[0] // mp_count
    toks = images * SEQ
    slots = master.shape[1]
    unit_rows = master.shape[2]
    unit_count = owners.shape[1]
    heads_here = scale_state.shape[1]
    paired = dp_count * 2 == UNIT
    core = dp_index % 2 if paired else 0

    def mine(field, rows):
        return lax.dynamic_slice_in_dim(field, mp_index * rows, rows, 0)

    rounded = master[0].astype(BF16)
    halves_here = jnp.concatenate([owners[0].astype(F32), scale_state[0]])[None]
    ring = Ring(dp_count) if paired else None
    if paired:
        own_labels = Labels((0, 0, 0, slot) for slot in range(slots))
        arrays, _ = gather_slots(LabelMoves(), own_labels, slots, ((), lambda: ()))
        labels = [row for field in arrays for row in field.rows]
        sizes = [len(field.rows) for field in arrays]
        assert len(set((h % ring.count, m, c, slot) for h, m, c, slot in labels)) == len(labels)
        hops, sides, cores, numbers = (jnp.array(column, jnp.int32) for column in zip(*labels))
        owner = ring.chip_at(hops) * 2 + (dp_index % 2 + cores) % 2
        side = (mp_index + sides) % 2
        slot_ids = (side * dp_count + owner) * slots + numbers
    else:
        sizes = [mp_count * dp_count * slots]
        slot_ids = lax.broadcasted_iota(jnp.int32, (mp_count * dp_count * slots, 1), 0)[:, 0]

    def prepare(halves_other, tokens, conditioning, sigmas, positions, cotangent):
        halves_all = both_halves(halves_here, halves_other, mp_index)
        owners_all = halves_all[:, :unit_count].astype(jnp.int32)
        scales_all = halves_all[:, unit_count:].reshape(-1)
        before = jnp.stack([slots_before(owners_all[half]) for half in range(mp_count)])
        half_ids = lax.broadcasted_iota(jnp.int32, owners_all.shape, 0)
        unit_slots = ((half_ids * dp_count + owners_all) * slots + before).reshape(-1)
        held_first = {"A1": 0, "A2": 1, "Q": 2, "K": 3, "V": 4, "O": 5, "G": 6, "U": 9, "F": 12}
        chunk_starts, seen = [], {}
        for kind in STACK_ORDER:
            per_half = STACK_ORDER.count(kind)
            base = held_first[kind] * mp_count + seen.get(kind, 0)
            chunk_starts.append([(base + half * per_half) * SPAN for half in range(mp_count)])
            seen[kind] = seen.get(kind, 0) + 1
        belongs = jnp.array(chunk_starts, jnp.int32).T[:, :, None]
        belongs = (belongs + lax.broadcasted_iota(jnp.int32, (1, 1, SPAN), 2)).reshape(-1)
        match = slot_ids[:, None] == unit_slots[None, :]
        places = jnp.where(
            jnp.any(match, axis=1),
            jnp.sum(jnp.where(match, belongs[None, :], 0), axis=1),
            belongs.shape[0],
        )
        starts = np.cumsum([0] + sizes)
        array_ids = jnp.array(np.repeat(np.arange(len(sizes)), sizes), jnp.int32)
        slot_numbers = jnp.array(np.concatenate([np.arange(size) for size in sizes]), jnp.int32)
        key = places * starts[-1] + slot_numbers
        ahead = (array_ids[:, None] == array_ids[None, :]) & (key[None, :] < key[:, None])
        rank = jnp.sum(jnp.where(ahead, 1, 0), axis=1) + jnp.array(np.repeat(starts[:-1], sizes), jnp.int32)
        at_rank = rank[None, :] == lax.broadcasted_iota(jnp.int32, (starts[-1],) * 2, 0)
        sorted_places = jnp.stack(
            [
                jnp.sum(jnp.where(at_rank, field[None, :], 0), axis=1)
                for field in (places, slot_numbers)
            ]
        )
        own_array = array_ids[None, :] == lax.broadcasted_iota(
            jnp.int32, (len(sizes), array_ids.shape[0]), 0
        )
        ends = jnp.stack(
            [
                jnp.sum(jnp.where(own_array & (places < bound // UNIT)[None, :], 1, 0), axis=1)
                for bound in (0, ROW_G, ROWS_ALL)
            ],
            axis=1,
        )
        square = sigmas * sigmas
        data_square = SIGMA_DATA * SIGMA_DATA
        loss_weight = 4.0 * square * data_square / ((square + data_square) * (square + data_square))
        scalars = jnp.concatenate([scales_all, jnp.sqrt(scales_all), mine(loss_weight, images)])
        cosine, sine = rope_tables(mine(positions, images))
        cond = jnp.pad(mine(conditioning, images).astype(BF16), ((0, 16 - images), (0, 0)))

        grad_out = (
            mine(cotangent, toks).astype(F32).reshape(images, SEQ, D)
            * mine(loss_weight, images)[:, None, None]
        ).astype(BF16).reshape(toks, D)
        return (
            sorted_places,
            ends,
            scalars,
            scales_all,
            cosine,
            sine,
            cond,
            grad_out,
            deal_matrix(core),
            mine(tokens, toks),
            mine(cotangent, toks),
        )

    halves_other = swap_mp(halves_here)
    if paired:
        gathered, prepared = gather_slots(
            Moves(ring),
            rounded,
            slots,
            ((halves_other, tokens, conditioning, sigmas, positions, cotangent), prepare),
        )
    else:
        gathered = [lax.all_gather(rounded, ("mp", "dp"), axis=0, tiled=True)]
        prepared = prepare(
            halves_other, tokens, conditioning, sigmas, positions, cotangent
        )
    places, ends, scalars, scales_all, cosine, sine, cond, grad_out, deal, x_own, cot_own = prepared
    (
        outs_low,
        early_keep,
        early_send,
        late_keep,
        late_send,
        normed_two,
        mids,
        grad_gains,
        grad_scale,
    ) = run_layer(
        images, places, ends, scalars, x_own, cot_own, grad_out, cond, cosine, sine, deal, gathered
    )
    outs_other = swap_mp(outs_low)
    outs_both = both_halves(outs_low, outs_other, mp_index, 1)
    output, input_grad = outs_both[0].astype(F32), outs_both[1].astype(F32)
    chunks = FF // CHUNK
    here = chunks // mp_count

    cond_own = mine(conditioning, images).astype(BF16).astype(F32)
    scale_row = jnp.pad(grad_scale[:, 0], (0, D - 16))[None]
    own_rows = jnp.concatenate([cond_own, grad_gains, scale_row], axis=0)
    own_rows = jnp.pad(own_rows, ((0, 16 - own_rows.shape[0]), (0, 0)))
    small = lax.all_gather(own_rows, ("dp", "mp"), axis=0, tiled=True)

    def small_factors():
        rows = small.reshape(-1, 16, D)
        scale_sum = jnp.sum(rows[:, 3 * images, :HEADS], axis=0) / (2.0 * jnp.sqrt(scales_all))
        gains = [
            rows[:, place * images : (place + 1) * images].reshape(-1, D) for place in (1, 2)
        ]
        return (
            rows[:, :images].reshape(-1, D),
            jnp.concatenate(gains, axis=1),
            lax.dynamic_slice_in_dim(scale_sum, mp_index * heads_here, heads_here, 0),
        )

    if paired:
        out_both = (grad_out, ring.twin(grad_out))
        early_both = (early_keep, ring.twin(early_send))
        two_both = (normed_two, ring.twin(normed_two))
        grad_fg = weight_grads(
            ((early_both, out_both, 0, here), (early_both, two_both, chunks, here)), mp_count
        )
        sum_fg = RingSum(ring, (grad_fg,), mp_index)
        hop = sum_fg.step()
        late_both = (after(late_keep, grad_fg), ring.twin(late_send))
        grad_u = weight_grads(((late_both, two_both, 0, here),), mp_count)
        late_both = (after(late_keep, hop, grad_u), late_both[1])
        mids_twin = ring.twin(mids)
        kinds = (((mids, 0), (mids_twin, 0)),) + (((mids, 1), (mids_twin, 1)),) * 3
        grad_at = weight_grads(
            tuple(
                (late_both, rights, chunks + place * mp_count, 1)
                for place, rights in enumerate(kinds)
            ),
            mp_count,
        )
        sum_rest = RingSum(ring, (grad_u, grad_at), mp_index)
        cond_all, gains_all, scale_grad = small_factors()
        hop = sum_fg.step()
        sum_rest.step(hop)
        sum_fg.step()
        sum_rest.step()
        sum_fg.step()
        sum_rest.step(outs_other)
        sum_fg = sum_fg.total()
        sum_rest.step()
        sum_rest = sum_rest.total()
        wanted = lax.broadcasted_iota(jnp.int32, (2 * SPAN, D), 0)
        feature = lax.broadcasted_iota(jnp.int32, (2 * SPAN, D), 1)
        wanted = (mp_index * SPAN + wanted % SPAN) * UNIT + 2 * dp_index + wanted // SPAN
        cond_rows = dot_nt((feature == wanted).astype(F32), cond_all)
        sum_a = jnp.dot(
            cond_rows,
            gains_all,
            precision=lax.Precision.HIGHEST,
            preferred_element_type=F32,
        )
        by_kind = jnp.concatenate(
            [
                sum_a[None, :, :D],
                sum_rest[here + 1 :],
                sum_rest[here : here + 1],
                sum_a[None, :, D:],
                sum_fg[here:],
                sum_rest[:here],
                sum_fg[:here],
            ]
        )
        grad_shards = (
            by_kind.reshape(-1, 2, SPAN, D).transpose(0, 2, 1, 3).reshape(unit_count, 2 * D)
        )
    else:
        def units_of(parts, field, kinds):
            here = parts[0].shape[0] // (kinds * mp_count)
            sides = jnp.stack(
                [
                    jnp.concatenate(
                        [
                            weight_grads(
                                (((part,), (field,), kind * mp_count * here, here),), mp_count
                            )
                            for kind in range(kinds)
                        ],
                        axis=2,
                    )
                    for part in parts
                ]
            )
            sides = sides.reshape(2, mp_count, UNIT // 4, -1, 2, SPAN, D)
            return sides.transpose(1, 3, 5, 2, 0, 4, 6).reshape(mp_count, -1, unit_rows * D)

        summed = lax.psum_scatter(
            jnp.concatenate(
                [
                    units_of((late_keep[chunks + 2 :], late_send[chunks + 2 :]), mids[1], 3),
                    units_of(
                        (late_keep[chunks : chunks + 2], late_send[chunks : chunks + 2]), mids[0], 1
                    ),
                    units_of((early_keep[chunks:], early_send[chunks:]), normed_two, 1),
                    units_of((late_keep[:chunks], late_send[:chunks]), normed_two, 1),
                    units_of((early_keep[:chunks], early_send[:chunks]), grad_out, 1),
                ],
                axis=1,
            ),
            "mp",
            scatter_dimension=0,
            tiled=True,
        )[0]
        summed = lax.psum_scatter(summed, "dp", scatter_dimension=1, tiled=True).astype(F32)
        cond_all, gains_all, scale_grad = small_factors()
        cond_half = lax.dynamic_slice_in_dim(
            cond_all, mp_index * SPAN * unit_rows, SPAN * unit_rows, 1
        )
        sum_a = lax.dot_general(
            cond_half,
            gains_all,
            (((0,), (0,)), ((), ())),
            precision=lax.Precision.HIGHEST,
            preferred_element_type=F32,
        )
        width = unit_rows * D // dp_count

        def piece(field):
            return lax.dynamic_slice_in_dim(
                field.reshape(SPAN, unit_rows * D), dp_index * width, width, 1
            )

        grad_shards = jnp.concatenate(
            [
                piece(sum_a[:, :D]),
                summed[: 4 * SPAN],
                piece(sum_a[:, D:]),
                summed[4 * SPAN :],
            ]
        )

    placed = owners[0] * slots + slots_before(owners[0])
    total_slots = dp_count * slots
    slot_ids = lax.broadcasted_iota(jnp.int32, (total_slots, unit_count), 0)
    unit_ids = lax.broadcasted_iota(jnp.int32, (total_slots, unit_count), 1)
    match_table = slot_ids == placed[None, :]
    source_unit = jnp.sum(jnp.where(match_table, unit_ids, 0), axis=1)
    filled = jnp.any(match_table, axis=1)
    outgoing = jnp.where(
        filled[:, None], jnp.take(grad_shards.astype(BF16), source_unit, axis=0), 0.0
    )
    owned = lax.all_to_all(outgoing, "dp", split_axis=0, concat_axis=1, tiled=True)
    owned_grads = owned.reshape(slots, unit_rows, D).astype(F32)
    first_new = BETA_ONE * moment_one[0] + (1.0 - BETA_ONE) * owned_grads
    second_new = BETA_TWO * moment_two[0] + (1.0 - BETA_TWO) * owned_grads * owned_grads
    master_new = adam_step(master[0], first_new, second_new, LEARN_RATE)
    scale_first = BETA_ONE * scale_state[1] + (1.0 - BETA_ONE) * scale_grad
    scale_second = BETA_TWO * scale_state[2] + (1.0 - BETA_TWO) * scale_grad * scale_grad
    scale_new = adam_step(scale_state[0], scale_first, scale_second, SCALE_RATE)
    scale_update = jnp.stack([scale_first, scale_new])
    return (
        output,
        input_grad,
        grad_shards[None],
        master_new[None],
        first_new[None],
        second_new[None],
        scale_update,
        scale_second,
    )


def solution(mesh):
    in_specs = (
        P("dp", None),
        P("dp", None),
        P("dp"),
        P("dp", None, None),
        P("dp", None),
        P("mp", None),
        P("mp", "dp", None, None),
        P("mp", "dp", None, None),
        P("mp", "dp", None, None),
        P(None, "mp"),
    )
    out_specs = (
        P("dp", None),
        P("dp", None),
        P("mp", None, "dp"),
        P("mp", "dp", None, None),
        P("mp", "dp", None, None),
        P("mp", "dp", None, None),
        P(None, "mp"),
        P("mp"),
    )
    return jax.shard_map(
        on_device, mesh=mesh, in_specs=in_specs, out_specs=out_specs, check_vma=False
    )
```

```python
import math

import jax
import jax.numpy as jnp
import numpy as np
from jax import lax
from jax.experimental import pallas as pl
from jax.experimental.pallas import tpu as pltpu
from jax.sharding import PartitionSpec as P

D = 768
HEADS = 12
HD = 64
FF = 2304
SIDE = 16
STEP = 10
SEQ = 256
UNIT = 32
SPAN = 4
SIDES = 2
CHUNK = SIDES * SPAN * UNIT
HALF_CHUNK = CHUNK // 2

NORM_EPS = 1e-06
COS_EPS = 1e-06
SIGMA_DATA = 0.5
BETA_ONE = 0.5
BETA_TWO = 0.5
ADAM_EPS = 1e-08
WEIGHT_DECAY = 0.01
LEARN_RATE = 0.04
SCALE_RATE = 1.0
ROOT_HALF = 0.7071067811865476
INV_ROOT_TWO_PI = 0.3989422804014327

F32 = jnp.float32
BF16 = jnp.bfloat16
VMEM_BYTES = 60 * 1024 * 1024

STACK = (("A1", D), ("Q", D), ("K", D), ("V", D), ("O", D), ("A2", D), ("G", FF), ("U", FF), ("F", FF))
ROW_A1, ROW_A2, ROW_Q, ROW_K, ROW_V, ROW_O = (D * place for place in range(6))
ROW_G = 6 * D
ROW_U = ROW_G + FF
ROW_F = ROW_U + FF
ROWS_ALL = ROW_F + FF
HELD_ROWS = dict(
    A1=ROW_A1, A2=ROW_A2, Q=ROW_Q, K=ROW_K, V=ROW_V, O=ROW_O, G=ROW_G, U=ROW_U, F=ROW_F
)
HEAD_ORDER = [
    side * (HEADS // SIDES) + chunk * (SPAN * UNIT // HD) + head
    for chunk in range(D // CHUNK)
    for side in range(SIDES)
    for head in range(SPAN * UNIT // HD)
]


def held_units():
    places = []
    for side in range(SIDES):
        for kind, rows in STACK:
            count = rows // SIDES // UNIT
            for unit in range(count):
                if kind in ("A1", "A2"):
                    place = side * count + unit
                else:
                    place = (unit // SPAN * SIDES + side) * SPAN + unit % SPAN
                places.append(HELD_ROWS[kind] // UNIT + place)
    return np.array(places, np.int32)


def dot_nn(left, right):
    return jnp.dot(left, right, preferred_element_type=F32)


def dot_nt(left, right):
    return lax.dot_general(left, right, (((1,), (1,)), ((), ())), preferred_element_type=F32)


def slots_before(owner_list):
    unit_count = owner_list.shape[0]
    same_owner = owner_list[:, None] == owner_list[None, :]
    row_ids = lax.broadcasted_iota(jnp.int32, (unit_count, unit_count), 0)
    col_ids = lax.broadcasted_iota(jnp.int32, (unit_count, unit_count), 1)
    return jnp.sum(jnp.where(same_owner & (col_ids < row_ids), 1, 0), axis=1).astype(jnp.int32)


def rope_tables(positions):
    quarter = HD // 8
    head_ids = jnp.array(HEAD_ORDER, jnp.int32)[:, None]
    column = lax.broadcasted_iota(jnp.int32, (HEADS, quarter), 1)
    flat_index = (column * HEADS + head_ids).astype(F32)
    low_log = math.log(math.pi)
    high_log = math.log(10.0 * math.pi)
    frequency = jnp.exp(low_log + (high_log - low_log) * flat_index / (HEADS * quarter))
    placed = (2.0 * positions.astype(F32) + 1.0) / SIDE - 1.0
    along_rows = placed[:, 0].reshape(1, 1, -1) * frequency[:, :, None]
    along_cols = placed[:, 1].reshape(1, 1, -1) * frequency[:, :, None]
    angles = jnp.concatenate([along_rows, along_cols], axis=1).reshape(HEADS * 2 * quarter, -1)
    return jnp.cos(angles), jnp.sin(angles)


def deal_matrix(core):
    target = lax.broadcasted_iota(jnp.int32, (CHUNK, CHUNK), 0)
    source = lax.broadcasted_iota(jnp.int32, (CHUNK, CHUNK), 1)
    parity = (target // HALF_CHUNK + core) % 2
    inner = target % HALF_CHUNK
    unit = inner % SPAN
    row = inner // SPAN % 2
    piece = inner // (2 * SPAN) % (UNIT // 4)
    side = inner // (2 * SPAN * (UNIT // 4))
    return (source == (side * SPAN + unit) * UNIT + 4 * piece + 2 * parity + row).astype(BF16)


def layer_kernel(
    images,
    slots_refs,
    place_ref,
    ends_ref,
    scal_ref,
    x_ref,
    cot_ref,
    gb_ref,
    cond_ref,
    cos_ref,
    sin_ref,
    deal_ref,
    outs_hbm,
    early_keep,
    early_send,
    late_keep,
    late_send,
    n2_hbm,
    mids_hbm,
    gain_hbm,
    ds_hbm,
    w,
    unit_s,
    coef_s,
    qtok_s,
    p_s,
    qk_s,
    v_s,
    o_s,
    x2_s,
    n1_s,
    n2_s,
    ga_s,
    do_s,
    dot_s,
    ff_s,
    dn2_s,
    dqkv_s,
    early_s,
    late_s,
    outs_s,
    gain_s,
    ds_s,
    dsout_s,
    w_sem,
    o_sem,
):
    toks = images * SEQ
    sends = []

    def send(src, dst):
        copy = pltpu.make_async_copy(src, dst, o_sem.at[len(sends)])
        copy.start()
        sends.append(copy)

    groups = (0, ROW_Q, ROW_O, ROW_G, ROWS_ALL)

    def fetch(low, high):
        first = 0
        for array, slots_ref in enumerate(slots_refs):

            @pl.loop(ends_ref[array, low // 3], ends_ref[array, low // 3 + 1])
            def _(index, slots_ref=slots_ref, first=first):
                unit = place_ref[0, first + index]
                group = jnp.int32(low)
                for bound in groups[low + 1 : high]:
                    group += jnp.where(unit >= bound // UNIT, 1, 0)
                pltpu.make_async_copy(
                    slots_ref.at[place_ref[1, first + index]],
                    w.at[pl.ds(pl.multiple_of(unit * UNIT, UNIT), UNIT)],
                    w_sem.at[group],
                ).start()

            first += slots_ref.shape[0]

    fetch(0, 3)

    def weights_here(index):
        low, high = groups[index : index + 2]
        region = w.at[pl.ds(low, high - low)]
        pltpu.make_async_copy(region, region, w_sem.at[index]).wait()

    def image_rows(image):
        return pl.ds(image * SEQ, SEQ)

    weights_here(0)
    fetch(3, 4)
    gain_one = 1.0 + dot_nn(cond_ref[...], w[ROW_A1 : ROW_A1 + D])
    gain_two = 1.0 + dot_nn(cond_ref[...], w[ROW_A2 : ROW_A2 + D])
    for image in range(images):
        x = x_ref[image_rows(image)]
        inverse = lax.rsqrt(jnp.mean(x * x, axis=-1, keepdims=True) + NORM_EPS)
        n1_s[image_rows(image)] = (x * inverse * gain_one[image : image + 1]).astype(BF16)
    send(n1_s, mids_hbm.at[1])
    weights_here(1)
    unit_s[:D] = dot_nt(w[ROW_Q : ROW_Q + D], n1_s[...])
    unit_s[D:] = dot_nt(w[ROW_K : ROW_K + D], n1_s[...])
    v_s[...] = dot_nt(w[ROW_V : ROW_V + D], n1_s[...]).astype(BF16)

    @pl.loop(0, 2 * HEADS)
    def _(index):
        head = lax.rem(index, HEADS)
        rows = pl.ds(pl.multiple_of(index * HD, HD), HD)
        angle_rows = pl.ds(pl.multiple_of(head * 16, 16), 16)
        raw = unit_s[rows]
        inverse = lax.rsqrt(jnp.sum(raw * raw, axis=0, keepdims=True) + COS_EPS)
        unit = raw * inverse
        root = scal_ref[HEADS + head]
        unit_s[rows] = unit
        coef_s[pl.ds(index, 1)] = root * inverse
        scaled = unit * root
        first, second = scaled[:16], scaled[16:32]
        cosine, sine = cos_ref[angle_rows], sin_ref[angle_rows]
        turned = jnp.concatenate(
            [first * cosine - second * sine, second * cosine + first * sine, scaled[32:]], axis=0
        )
        qk_s[rows] = turned.astype(BF16)

    qtok_s[...] = qk_s[:D].T

    def head_rows(head):
        return pl.ds(pl.multiple_of(head * HD, HD), HD)

    def pair_lanes(pair):
        return pl.ds(pl.multiple_of(pair * 2 * HD, 2 * HD), 2 * HD)

    @pl.loop(0, HEADS // 2)
    def _(pair):
        for image in range(images):
            cols = image_rows(image)
            query = qtok_s[cols, pair_lanes(pair)]
            mixed = []
            for half in range(2):
                head = pair * 2 + half
                scores = dot_nn(
                    query[:, half * HD : (half + 1) * HD], qk_s[head_rows(HEADS + head), cols]
                )
                exp_scores = jnp.exp(scores - scal_ref[head])
                inverse = 1.0 / jnp.sum(exp_scores, axis=-1, keepdims=True)
                probs = (exp_scores * inverse).astype(BF16)
                p_s[head, cols] = probs
                mixed.append(dot_nt(probs, v_s[head_rows(head), cols]))
            o_s[cols, pair_lanes(pair)] = jnp.concatenate(mixed, axis=1)

    weights_here(2)
    x2_s[...] = x_ref[...] + dot_nn(o_s[...].astype(BF16), w[ROW_O : ROW_O + D])
    for image in range(images):
        x2 = x2_s[image_rows(image)]
        inverse = lax.rsqrt(jnp.mean(x2 * x2, axis=-1, keepdims=True) + NORM_EPS)
        n2_s[image_rows(image)] = (x2 * inverse * gain_two[image : image + 1]).astype(BF16)
    send(n2_s, n2_hbm)

    weights_here(3)
    chunks = FF // CHUNK
    width = D

    def deal(field, store, place):
        dealt = dot_nt(deal_ref[...], field).astype(BF16)
        store[0, place] = dealt[:HALF_CHUNK]
        store[1, place] = dealt[HALF_CHUNK:]

    for start in range(0, FF, width):

        def part(base):
            return w[base + start : base + start + width]

        gate = dot_nt(n2_s[...], part(ROW_G))
        up = dot_nt(n2_s[...], part(ROW_U))
        grad_hidden = dot_nt(gb_ref[...], part(ROW_F))
        phi_sum = 0.5 * (1.0 + lax.erf(gate * ROOT_HALF))
        density = INV_ROOT_TWO_PI * jnp.exp(-0.5 * gate * gate)
        gelu = gate * phi_sum
        hidden = (gelu * up).astype(BF16)
        grad_gate = (grad_hidden * up * (phi_sum + gate * density)).astype(BF16)
        grad_up = (grad_hidden * gelu).astype(BF16)
        ff = dot_nn(hidden, part(ROW_F))
        dn2 = dot_nn(grad_gate, part(ROW_G)) + dot_nn(grad_up, part(ROW_U))
        if start == 0:
            ff_s[...] = ff
            dn2_s[...] = dn2
        else:
            ff_s[...] += ff
            dn2_s[...] += dn2
        for at in range(0, width, CHUNK):
            place = (start + at) // CHUNK
            deal(hidden[:, at : at + CHUNK], early_s, place)
            deal(grad_gate[:, at : at + CHUNK], early_s, chunks + place)
            deal(grad_up[:, at : at + CHUNK], late_s, place)

    send(early_s.at[0], early_keep)
    send(early_s.at[1], early_send)
    outs_s[0] = (x2_s[...] + ff_s[...]).astype(BF16)
    send(outs_s.at[0], outs_hbm.at[0])

    def norm_back(x, gain, grad_normed):
        inverse = lax.rsqrt(jnp.mean(x * x, axis=-1, keepdims=True) + NORM_EPS)
        scaled = grad_normed * gain
        inner = jnp.mean(x * scaled, axis=-1, keepdims=True)
        grad_x = inverse * scaled - x * (inverse * inverse * inverse * inner)
        return grad_x, jnp.sum(grad_normed * x * inverse, axis=0, keepdims=True)

    for image in range(images):
        rows = image_rows(image)
        grad_x, grad_gain = norm_back(x2_s[rows], gain_two[image : image + 1], dn2_s[rows])
        grad = cot_ref[rows].astype(F32) * scal_ref[2 * HEADS + image] + grad_x
        x2_s[rows] = grad
        ga_s[rows] = grad.astype(BF16)
        gain_s[pl.ds(images + image, 1)] = grad_gain
    send(ga_s, mids_hbm.at[0])

    do_s[...] = dot_nt(ga_s[...], w[ROW_O : ROW_O + D]).astype(BF16)
    dot_s[...] = dot_nt(w[ROW_O : ROW_O + D], ga_s[...]).astype(BF16)
    ds_s[...] = jnp.zeros_like(ds_s)

    @pl.loop(0, HEADS // 2)
    def _(pair):
        for image in range(images):
            cols = image_rows(image)
            grads_mixed = do_s[cols, pair_lanes(pair)]
            inners = grads_mixed.astype(F32) * o_s[cols, pair_lanes(pair)]
            for half in range(2):
                head = pair * 2 + half
                lanes = slice(half * HD, (half + 1) * HD)
                rows, key_rows = head_rows(head), head_rows(HEADS + head)
                key, value = qk_s[key_rows, cols], v_s[rows, cols]
                probs = p_s[head, cols]
                grad_probs = dot_nn(grads_mixed[:, lanes], value)
                inner = jnp.sum(inners[:, lanes], axis=-1, keepdims=True)
                grad_scores = (probs.astype(F32) * (grad_probs - inner)).astype(BF16)
                grad_query = dot_nt(key, grad_scores)
                grad_key = dot_nn(qk_s[rows, cols], grad_scores)
                grad_value = dot_nn(dot_s[rows, cols], probs)
                angle_rows = pl.ds(pl.multiple_of(head * 16, 16), 16)
                cosine, sine = cos_ref[angle_rows, cols], sin_ref[angle_rows, cols]
                along = jnp.zeros((1, SEQ), F32)
                for grad, own_rows, place in (
                    (grad_query, rows, head),
                    (grad_key, key_rows, HEADS + head),
                ):
                    first, second = grad[:16], grad[16:32]
                    back = jnp.concatenate(
                        [
                            first * cosine + second * sine,
                            second * cosine - first * sine,
                            grad[32:],
                        ],
                        axis=0,
                    )
                    unit = unit_s[own_rows, cols]
                    inner_unit = jnp.sum(unit * back, axis=0, keepdims=True)
                    along += inner_unit
                    dqkv_s[own_rows, cols] = (
                        coef_s[pl.ds(place, 1), cols] * (back - unit * inner_unit)
                    ).astype(BF16)
                value_rows = head_rows(2 * HEADS + head)
                dqkv_s[value_rows, cols] = grad_value.astype(BF16)
                ds_s[pl.ds(head, 1)] += along

    per_kind = D // CHUNK
    for place in range(per_kind):
        deal(o_s[:, place * CHUNK : (place + 1) * CHUNK].astype(BF16), late_s, chunks + place)
    for place in range(3 * per_kind):
        dealt = dot_nn(deal_ref[...], dqkv_s[place * CHUNK : (place + 1) * CHUNK]).astype(BF16)
        late_s[0, chunks + per_kind + place] = dealt[:HALF_CHUNK]
        late_s[1, chunks + per_kind + place] = dealt[HALF_CHUNK:]
    send(late_s.at[0], late_keep)
    send(late_s.at[1], late_send)
    dsout_s[...] = jnp.broadcast_to(jnp.sum(ds_s[...], axis=1, keepdims=True), dsout_s.shape)
    send(dsout_s, ds_hbm)

    dn1 = dot_nn(dqkv_s[:D].T, w[ROW_Q : ROW_Q + D])
    dn1 += dot_nn(dqkv_s[D : 2 * D].T, w[ROW_K : ROW_K + D])
    dn1 += dot_nn(dqkv_s[2 * D :].T, w[ROW_V : ROW_V + D])
    dn2_s[...] = dn1
    for image in range(images):
        rows = image_rows(image)
        grad_x, grad_gain = norm_back(x_ref[rows], gain_one[image : image + 1], dn2_s[rows])
        outs_s[1, rows] = (x2_s[rows] + grad_x).astype(BF16)
        gain_s[pl.ds(image, 1)] = grad_gain
    send(outs_s.at[1], outs_hbm.at[1])
    send(gain_s, gain_hbm)
    for copy in sends:
        copy.wait()


def run_layer(images, places, ends, scalars, x, cotangent, grad_out, cond, cosine, sine, deal, slots):
    toks = images * SEQ
    chunks = FF // CHUNK
    any_spec = pl.BlockSpec(memory_space=pl.ANY)
    vmem = pl.BlockSpec(memory_space=pltpu.VMEM)
    smem = pl.BlockSpec(memory_space=pltpu.SMEM)
    field = jax.ShapeDtypeStruct((toks, D), BF16)

    def dealt(count):
        return jax.ShapeDtypeStruct((count, HALF_CHUNK, toks), BF16)

    pair = jax.ShapeDtypeStruct((2, toks, D), BF16)
    late = chunks + 4 * D // CHUNK
    outs = [pair, dealt(2 * chunks), dealt(2 * chunks), dealt(late), dealt(late), field, pair]
    outs += [
        jax.ShapeDtypeStruct((2 * images, D), F32),
        jax.ShapeDtypeStruct((16, 128), F32),
    ]
    wide = pltpu.VMEM((toks, D), F32)
    low = pltpu.VMEM((toks, D), BF16)
    scratch = [
        pltpu.VMEM((ROWS_ALL, D), BF16),
        pltpu.VMEM((2 * D, toks), F32),
        pltpu.VMEM((2 * HEADS, toks), F32),
        low,
        pltpu.VMEM((HEADS, toks, SEQ), BF16),
        pltpu.VMEM((2 * D, toks), BF16),
        pltpu.VMEM((D, toks), BF16),
        wide,
        wide,
        low,
        low,
        low,
        low,
        pltpu.VMEM((D, toks), BF16),
        wide,
        wide,
        pltpu.VMEM((3 * D, toks), BF16),
        pltpu.VMEM((2, 2 * chunks, HALF_CHUNK, toks), BF16),
        pltpu.VMEM((2, late, HALF_CHUNK, toks), BF16),
        pltpu.VMEM((2, toks, D), BF16),
        pltpu.VMEM((2 * images, D), F32),
        pltpu.VMEM((16, SEQ), F32),
        pltpu.VMEM((16, 128), F32),
        pltpu.SemaphoreType.DMA((4,)),
        pltpu.SemaphoreType.DMA((16,)),
    ]

    operands = [places, ends, scalars, x, cotangent, grad_out, cond, cosine, sine, deal]
    here = len(operands)

    def body(*refs):
        layer_kernel(
            images, refs[here : here + len(slots)], *refs[:here], *refs[here + len(slots) :]
        )

    return pl.pallas_call(
        body,
        out_shape=outs,
        in_specs=[smem] * 3 + [vmem] * 7 + [any_spec] * len(slots),
        out_specs=[any_spec] * len(outs),
        scratch_shapes=scratch,
        compiler_params=pltpu.CompilerParams(vmem_limit_bytes=VMEM_BYTES),
        cost_estimate=pl.CostEstimate(
            flops=2 * 3 * ROWS_ALL * D * toks, bytes_accessed=ROWS_ALL * D * 4, transcendentals=0
        ),
        name="layer",
    )(*operands, *slots)


def weight_grads(lefts, rights, kinds, first=0, here=3):
    rows, toks = lefts[0].shape[1:]
    pieces = rows // (SIDES * 2 * SPAN)
    total = sum(count for count, _ in kinds)
    steps = total // here
    step_rights = [place for count, place in kinds for _ in range(count // here)]
    operands, specs = list(lefts), []
    for left in lefts:
        specs.append(pl.BlockSpec((here, rows, toks), lambda step: (first // here + step, 0, 0)))
    for parts in rights:
        for part in parts:
            field, at = part if isinstance(part, tuple) else (part[None], 0)
            operands.append(field)
            specs.append(pl.BlockSpec((None, toks, D), lambda step, at=at: (at, 0, 0)))

    def body(*refs):
        out_ref, count = refs[-1], len(lefts)
        step = pl.program_id(0)
        for place in range(len(rights)):
            own = refs[count * (place + 1) : count * (place + 2)]
            mine = [index for index, right in enumerate(step_rights) if right == place]

            @pl.when((step >= mine[0]) & (step <= mine[-1]))
            def _(own=own):
                summed = dot_nn(refs[0][...].reshape(here * rows, toks), own[0][...])
                for left, right in zip(refs[1:count], own[1:]):
                    summed += dot_nn(left[...].reshape(here * rows, toks), right[...])
                for chunk in range(here):
                    out_ref[:, :, chunk] = (
                        summed[chunk * rows : (chunk + 1) * rows]
                        .reshape(SIDES, pieces, 2 * SPAN, D)
                        .astype(BF16)
                    )

    return pl.pallas_call(
        body,
        out_shape=jax.ShapeDtypeStruct((SIDES, pieces, total, 2 * SPAN, D), BF16),
        grid=(steps,),
        in_specs=specs,
        out_specs=pl.BlockSpec(
            (SIDES, pieces, here, 2 * SPAN, D), lambda step: (0, 0, step, 0, 0)
        ),
        compiler_params=pltpu.CompilerParams(vmem_limit_bytes=VMEM_BYTES),
        cost_estimate=pl.CostEstimate(
            flops=2 * len(lefts) * total * rows * toks * D,
            bytes_accessed=2 * len(lefts) * (total * rows + len(rights) * D) * toks
            + 2 * total * rows * D,
            transcendentals=0,
        ),
        name="weight_grads",
    )(*operands)


def adam_step(weights, first_new, second_new, rate):
    fix_one = 1.0 - math.pow(BETA_ONE, STEP)
    fix_two = 1.0 - math.pow(BETA_TWO, STEP)
    return weights * (1.0 - rate * WEIGHT_DECAY) - rate * (first_new / fix_one) / (
        jnp.sqrt(second_new / fix_two) + ADAM_EPS
    )


def add(*terms):
    total = terms[0].astype(F32)
    for term in terms[1:]:
        total = total + term.astype(F32)
    return total


class Ring:
    def __init__(self, dp_count):
        self.count = dp_count // 2
        pairs = []
        for place in range(self.count):
            for core in range(2):
                pairs.append(
                    (self.chip(place) * 2 + core, self.chip((place + 1) % self.count) * 2 + core)
                )
        self.onward = pairs
        self.backward = [(b, a) for a, b in pairs]
        self.twins = [(index, index ^ 1) for index in range(dp_count)]

    def chip(self, place):
        column = self.count // 2
        return 2 * place if place < column else 2 * (self.count - 1 - place) + 1

    def here(self):
        chip = lax.axis_index("dp") // 2
        return jnp.where(chip % 2 == 0, chip // 2, self.count - 1 - chip // 2)

    def chip_at(self, offset):
        place = (self.here() + offset + self.count) % self.count
        column = self.count // 2
        return jnp.where(place < column, 2 * place, 2 * (self.count - 1 - place) + 1)

    def on(self, field):
        return lax.ppermute(field, "dp", self.onward)

    def back(self, field):
        return lax.ppermute(field, "dp", self.backward)

    def twin(self, field):
        return lax.ppermute(field, "dp", self.twins)


def after(field, *others):
    return lax.optimization_barrier((field, others))[0]


def swap_mp(field):
    return lax.ppermute(field, "mp", [(0, 1), (1, 0)])


class Labels:
    def __init__(self, rows):
        self.rows = list(rows)

    def __getitem__(self, cut):
        return Labels(self.rows[cut])

    def moved(self, hop, mp, core):
        return Labels((h + hop, m ^ mp, c ^ core, slot) for h, m, c, slot in self.rows)


class LabelMoves:
    def on(self, field):
        return field.moved(-1, 0, 0)

    def back(self, field):
        return field.moved(1, 0, 0)

    def swap(self, field):
        return field.moved(0, 1, 0)

    def twin(self, field):
        return field.moved(0, 0, 1)

    def cat(self, *fields):
        return Labels(row for field in fields for row in field.rows)

    def together(self, *fields):
        return fields


class Moves:
    def __init__(self, ring):
        self.on, self.back, self.twin, self.swap = ring.on, ring.back, ring.twin, swap_mp

    def cat(self, *fields):
        return jnp.concatenate(fields)

    def together(self, *fields):
        return lax.optimization_barrier(fields)


def gather_slots(moves, own, slots, beside):
    cat, on, back, swap, twin = moves.cat, moves.on, moves.back, moves.swap, moves.twin
    cut = slots // 2
    rest = slots - cut
    first, second = own[:cut], own[cut:]
    hop = [on(second), back(second), swap(first), twin(own)]
    f0, b0, y0, c0, second, *soon = moves.together(*hop, second, *beside[0])
    wide = cat(first, y0)
    hop = [on(wide), back(wide), swap(second), twin(cat(y0, f0, b0))]
    f1, b1, y1, c1, f0, b0 = moves.together(*hop, f0, b0)
    hop = [on(cat(f0, f1)), back(cat(b0, b1)), swap(cat(f0, b0)), twin(cat(f1, b1, y1))]
    f2, b2, y2, c2, *later = moves.together(*hop, *beside[1](*soon))
    crossing = cat(f2[:rest], b2[:rest])
    hop = [on(f2), back(b2), swap(crossing), twin(cat(f2, b2, y2))]
    f3, b3, y3, c3 = moves.together(*hop)
    half = (slots + cut) // 2
    crossing = cat(f3[:rest], b3[:rest])
    hop = [on(f3[:half]), back(b3[half:]), swap(crossing), twin(cat(f3, b3, y3))]
    f4, b4, y4, c4 = moves.together(*hop)
    y5 = swap(cat(f4[:rest], b4[: max(0, rest - half)]))
    c5 = [twin(f4), twin(b4), twin(y4)]
    return [own, f0, b0, y0, c0, f1, b1, y1, c1, f2, b2, y2, c2, f3, b3, y3, c3, f4, b4, y4, c4, y5] + c5 + [twin(y5)], later


def both_halves(own, other, half, axis=0):
    return jnp.where(
        half == 0,
        jnp.concatenate([own, other], axis=axis),
        jnp.concatenate([other, own], axis=axis),
    )


def pick(field, *places):
    for place in places:
        field = lax.dynamic_index_in_dim(field, place, 0, keepdims=False)
    return field


class RingSum:
    def __init__(self, ring, fields, half):
        self.ring, self.fields, self.half = ring, fields, half
        self.distance = ring.count // 2
        self.on = self.back = None

    def block(self, offset):
        place = self.ring.chip_at(offset)
        parts = [
            lax.dynamic_index_in_dim(field, place, 1, keepdims=False) for field in self.fields
        ]
        return parts[0] if len(parts) == 1 else jnp.concatenate(parts, axis=1)

    def step(self, *others):
        ring, far, distance = self.ring, self.ring.count // 2, self.distance
        if distance == far:
            block = self.block(far)
            on, back = block[0], block[1]
        else:
            on, back = self.block(distance), self.block(-distance)
            if distance == far - 1:
                on = jnp.stack([add(on[0], self.on).astype(BF16), on[1]])
                back = jnp.stack([back[0], add(back[1], self.back).astype(BF16)])
            else:
                on, back = add(on, self.on).astype(BF16), add(back, self.back).astype(BF16)
        if others:
            on, back = after(on, *others), after(back, *others)
        self.on, self.back = lax.optimization_barrier((ring.on(on), ring.back(back)))
        self.distance -= 1
        return self.on, self.back

    def total(self):
        total = add(self.block(0), self.on, self.back)
        other = swap_mp(pick(total.astype(BF16), 1 - self.half))
        return add(pick(total, self.half), other)


def on_device(
    tokens,
    conditioning,
    sigmas,
    positions,
    cotangent,
    owners,
    master,
    moment_one,
    moment_two,
    scale_state,
):
    dp_count = lax.axis_size("dp")
    mp_count = lax.axis_size("mp")
    dp_index = lax.axis_index("dp")
    mp_index = lax.axis_index("mp")
    images = conditioning.shape[0] // mp_count
    toks = images * SEQ
    slots = master.shape[1]
    unit_rows = master.shape[2]
    unit_count = owners.shape[1]
    heads_here = scale_state.shape[1]
    paired = dp_count * 2 == UNIT
    core = dp_index % 2 if paired else 0

    def mine(field, rows):
        return lax.dynamic_slice_in_dim(field, mp_index * rows, rows, 0)

    rounded = master[0].astype(BF16)
    halves_here = jnp.concatenate([owners[0].astype(F32), scale_state[0]])[None]
    ring = Ring(dp_count) if paired else None
    if paired:
        own_labels = Labels((0, 0, 0, slot) for slot in range(slots))
        arrays, _ = gather_slots(LabelMoves(), own_labels, slots, ((), lambda: ()))
        labels = [row for field in arrays for row in field.rows]
        sizes = [len(field.rows) for field in arrays]
        assert len(set((h % ring.count, m, c, slot) for h, m, c, slot in labels)) == len(labels)
        hops, sides, cores, numbers = (jnp.array(column, jnp.int32) for column in zip(*labels))
        owner = ring.chip_at(hops) * 2 + (dp_index % 2 + cores) % 2
        side = (mp_index + sides) % 2
        slot_ids = (side * dp_count + owner) * slots + numbers
    else:
        sizes = [mp_count * dp_count * slots]
        slot_ids = lax.broadcasted_iota(jnp.int32, (mp_count * dp_count * slots, 1), 0)[:, 0]

    def prepare(halves_other, tokens, conditioning, sigmas, positions, cotangent):
        halves_all = both_halves(halves_here, halves_other, mp_index)
        owners_all = halves_all[:, :unit_count].astype(jnp.int32)
        scales_all = halves_all[:, unit_count:].reshape(-1)
        before = jnp.stack([slots_before(owners_all[half]) for half in range(mp_count)])
        half_ids = lax.broadcasted_iota(jnp.int32, owners_all.shape, 0)
        unit_slots = ((half_ids * dp_count + owners_all) * slots + before).reshape(-1)
        belongs = jnp.array(held_units())
        match = slot_ids[:, None] == unit_slots[None, :]
        places = jnp.where(
            jnp.any(match, axis=1),
            jnp.sum(jnp.where(match, belongs[None, :], 0), axis=1),
            belongs.shape[0],
        )
        starts = np.cumsum([0] + sizes)
        array_ids = jnp.array(np.repeat(np.arange(len(sizes)), sizes), jnp.int32)
        slot_numbers = jnp.array(np.concatenate([np.arange(size) for size in sizes]), jnp.int32)
        key = places * starts[-1] + slot_numbers
        ahead = (array_ids[:, None] == array_ids[None, :]) & (key[None, :] < key[:, None])
        rank = jnp.sum(jnp.where(ahead, 1, 0), axis=1) + jnp.array(np.repeat(starts[:-1], sizes), jnp.int32)
        at_rank = rank[None, :] == lax.broadcasted_iota(jnp.int32, (starts[-1],) * 2, 0)
        sorted_places = jnp.stack(
            [
                jnp.sum(jnp.where(at_rank, field[None, :], 0), axis=1)
                for field in (places, slot_numbers)
            ]
        )
        own_array = array_ids[None, :] == lax.broadcasted_iota(
            jnp.int32, (len(sizes), array_ids.shape[0]), 0
        )
        ends = jnp.stack(
            [
                jnp.sum(jnp.where(own_array & (places < bound // UNIT)[None, :], 1, 0), axis=1)
                for bound in (0, ROW_G, ROWS_ALL)
            ],
            axis=1,
        )
        scales_held = scales_all[jnp.array(HEAD_ORDER)]
        square = sigmas * sigmas
        data_square = SIGMA_DATA * SIGMA_DATA
        loss_weight = 4.0 * square * data_square / ((square + data_square) * (square + data_square))
        scalars = jnp.concatenate([scales_held, jnp.sqrt(scales_held), mine(loss_weight, images)])
        cosine, sine = rope_tables(mine(positions, images))
        cond = jnp.pad(mine(conditioning, images).astype(BF16), ((0, 16 - images), (0, 0)))

        grad_out = (
            mine(cotangent, toks).astype(F32).reshape(images, SEQ, D)
            * mine(loss_weight, images)[:, None, None]
        ).astype(BF16).reshape(toks, D)
        return (
            sorted_places,
            ends,
            scalars,
            scales_all,
            cosine,
            sine,
            cond,
            grad_out,
            deal_matrix(core),
            mine(tokens, toks),
            mine(cotangent, toks),
        )

    halves_other = swap_mp(halves_here)
    if paired:
        gathered, prepared = gather_slots(
            Moves(ring),
            rounded,
            slots,
            ((halves_other, tokens, conditioning, sigmas, positions, cotangent), prepare),
        )
    else:
        gathered = [lax.all_gather(rounded, ("mp", "dp"), axis=0, tiled=True)]
        prepared = prepare(
            halves_other, tokens, conditioning, sigmas, positions, cotangent
        )
    places, ends, scalars, scales_all, cosine, sine, cond, grad_out, deal, x_own, cot_own = prepared
    (
        outs_low,
        early_keep,
        early_send,
        late_keep,
        late_send,
        normed_two,
        mids,
        grad_gains,
        grad_scale,
    ) = run_layer(
        images, places, ends, scalars, x_own, cot_own, grad_out, cond, cosine, sine, deal, gathered
    )
    outs_other = swap_mp(outs_low)
    outs_both = both_halves(outs_low, outs_other, mp_index, 1)
    output, input_grad = outs_both[0].astype(F32), outs_both[1].astype(F32)
    chunks, few = FF // CHUNK, D // CHUNK

    cond_own = mine(conditioning, images).astype(BF16).astype(F32)
    scale_row = jnp.pad(grad_scale[:, 0], (0, D - 16))[None]
    own_rows = jnp.concatenate([cond_own, grad_gains, scale_row], axis=0)
    own_rows = jnp.pad(own_rows, ((0, 16 - own_rows.shape[0]), (0, 0)))
    small = lax.all_gather(own_rows, ("dp", "mp"), axis=0, tiled=True)

    def small_factors():
        rows = small.reshape(-1, 16, D)
        scale_sum = jnp.sum(rows[:, 3 * images, :HEADS], axis=0)[jnp.array(np.argsort(HEAD_ORDER))]
        scale_sum = scale_sum / (2.0 * jnp.sqrt(scales_all))
        gains = [
            rows[:, place * images : (place + 1) * images].reshape(-1, D) for place in (1, 2)
        ]
        return (
            rows[:, :images].reshape(-1, D),
            jnp.concatenate(gains, axis=1),
            lax.dynamic_slice_in_dim(scale_sum, mp_index * heads_here, heads_here, 0),
        )

    if paired:
        out_both = (grad_out, ring.twin(grad_out))
        early_both = (early_keep, ring.twin(early_send))
        two_both = (normed_two, ring.twin(normed_two))
        grad_fg = weight_grads(early_both, (out_both, two_both), ((chunks, 0), (chunks, 1)))
        sum_fg = RingSum(ring, (grad_fg,), mp_index)
        hop = sum_fg.step()
        late_both = (after(late_keep, grad_fg), ring.twin(late_send))
        mids_twin = ring.twin(mids)
        grad_rest = weight_grads(
            late_both,
            (two_both, ((mids, 0), (mids_twin, 0)), ((mids, 1), (mids_twin, 1))),
            ((chunks, 0), (few, 1), (3 * few, 2)),
        )
        sum_rest = RingSum(ring, (grad_rest,), mp_index)
        cond_all, gains_all, scale_grad = small_factors()
        hop = sum_fg.step()
        sum_rest.step(hop)
        sum_fg.step()
        sum_rest.step()
        sum_fg.step()
        sum_rest.step(outs_other)
        sum_fg = sum_fg.total()
        sum_rest.step()
        sum_rest = sum_rest.total()
        own_rows = 2 * (D // mp_count // UNIT)
        row = lax.broadcasted_iota(jnp.int32, (own_rows, D), 0)
        feature = lax.broadcasted_iota(jnp.int32, (own_rows, D), 1)
        unit = row // (2 * SPAN) * SPAN + row % SPAN
        wanted = (mp_index * (own_rows // 2) + unit) * UNIT + 2 * dp_index + row // SPAN % 2
        cond_rows = dot_nt((feature == wanted).astype(F32), cond_all)
        sum_a = jnp.dot(
            cond_rows,
            gains_all,
            precision=lax.Precision.HIGHEST,
            preferred_element_type=F32,
        )
        by_kind = jnp.concatenate(
            [
                sum_a[:, :D].reshape(few, 2 * SPAN, D),
                sum_rest[chunks + few :],
                sum_rest[chunks : chunks + few],
                sum_a[:, D:].reshape(few, 2 * SPAN, D),
                sum_fg[chunks:],
                sum_rest[:chunks],
                sum_fg[:chunks],
            ]
        )
        grad_shards = (
            by_kind.reshape(-1, 2, SPAN, D).transpose(0, 2, 1, 3).reshape(unit_count, 2 * D)
        )
    else:
        def units_of(parts, field, first, count):
            sides = jnp.stack(
                [weight_grads((part,), ((field,),), ((count, 0),), first) for part in parts]
            )
            sides = sides.reshape(2, mp_count, UNIT // 4, -1, 2, SPAN, D)
            return sides.transpose(1, 3, 5, 2, 0, 4, 6).reshape(mp_count, -1, unit_rows * D)

        early, late = (early_keep, early_send), (late_keep, late_send)
        summed = lax.psum_scatter(
            jnp.concatenate(
                [
                    units_of(late, mids[1], chunks + few, few),
                    units_of(late, mids[1], chunks + 2 * few, few),
                    units_of(late, mids[1], chunks + 3 * few, few),
                    units_of(late, mids[0], chunks, few),
                    units_of(early, normed_two, chunks, chunks),
                    units_of(late, normed_two, 0, chunks),
                    units_of(early, grad_out, 0, chunks),
                ],
                axis=1,
            ),
            "mp",
            scatter_dimension=0,
            tiled=True,
        )[0]
        summed = lax.psum_scatter(summed, "dp", scatter_dimension=1, tiled=True).astype(F32)
        cond_all, gains_all, scale_grad = small_factors()
        cond_half = lax.dynamic_slice_in_dim(
            cond_all, mp_index * (D // mp_count), D // mp_count, 1
        )
        sum_a = lax.dot_general(
            cond_half,
            gains_all,
            (((0,), (0,)), ((), ())),
            precision=lax.Precision.HIGHEST,
            preferred_element_type=F32,
        )
        width = unit_rows * D // dp_count

        def piece(field):
            return lax.dynamic_slice_in_dim(
                field.reshape(-1, unit_rows * D), dp_index * width, width, 1
            )

        grad_shards = jnp.concatenate(
            [
                piece(sum_a[:, :D]),
                summed[: 4 * (D // mp_count // unit_rows)],
                piece(sum_a[:, D:]),
                summed[4 * (D // mp_count // unit_rows) :],
            ]
        )

    placed = owners[0] * slots + slots_before(owners[0])
    total_slots = dp_count * slots
    slot_ids = lax.broadcasted_iota(jnp.int32, (total_slots, unit_count), 0)
    unit_ids = lax.broadcasted_iota(jnp.int32, (total_slots, unit_count), 1)
    match_table = slot_ids == placed[None, :]
    source_unit = jnp.sum(jnp.where(match_table, unit_ids, 0), axis=1)
    filled = jnp.any(match_table, axis=1)
    outgoing = jnp.where(
        filled[:, None], jnp.take(grad_shards.astype(BF16), source_unit, axis=0), 0.0
    )
    owned = lax.all_to_all(outgoing, "dp", split_axis=0, concat_axis=1, tiled=True)
    owned_grads = owned.reshape(slots, unit_rows, D).astype(F32)
    first_new = BETA_ONE * moment_one[0] + (1.0 - BETA_ONE) * owned_grads
    second_new = BETA_TWO * moment_two[0] + (1.0 - BETA_TWO) * owned_grads * owned_grads
    master_new = adam_step(master[0], first_new, second_new, LEARN_RATE)
    scale_first = BETA_ONE * scale_state[1] + (1.0 - BETA_ONE) * scale_grad
    scale_second = BETA_TWO * scale_state[2] + (1.0 - BETA_TWO) * scale_grad * scale_grad
    scale_new = adam_step(scale_state[0], scale_first, scale_second, SCALE_RATE)
    scale_update = jnp.stack([scale_first, scale_new])
    return (
        output,
        input_grad,
        grad_shards[None],
        master_new[None],
        first_new[None],
        second_new[None],
        scale_update,
        scale_second,
    )


def solution(mesh):
    in_specs = (
        P("dp", None),
        P("dp", None),
        P("dp"),
        P("dp", None, None),
        P("dp", None),
        P("mp", None),
        P("mp", "dp", None, None),
        P("mp", "dp", None, None),
        P("mp", "dp", None, None),
        P(None, "mp"),
    )
    out_specs = (
        P("dp", None),
        P("dp", None),
        P("mp", None, "dp"),
        P("mp", "dp", None, None),
        P("mp", "dp", None, None),
        P("mp", "dp", None, None),
        P(None, "mp"),
        P("mp"),
    )
    return jax.shard_map(
        on_device, mesh=mesh, in_specs=in_specs, out_specs=out_specs, check_vma=False
    )
```

```python
import math

import jax
import jax.numpy as jnp
import numpy as np
from jax import lax
from jax.experimental import pallas as pl
from jax.experimental.pallas import tpu as pltpu
from jax.sharding import PartitionSpec as P

D = 768
HEADS = 12
HD = 64
FF = 2304
SIDE = 16
STEP = 10
SEQ = 256
UNIT = 32
SPAN = 4
SIDES = 2
CHUNK = SIDES * SPAN * UNIT
HALF_CHUNK = CHUNK // 2

NORM_EPS = 1e-06
COS_EPS = 1e-06
SIGMA_DATA = 0.5
BETA_ONE = 0.5
BETA_TWO = 0.5
ADAM_EPS = 1e-08
WEIGHT_DECAY = 0.01
LEARN_RATE = 0.04
SCALE_RATE = 1.0
ROOT_HALF = 0.7071067811865476
INV_ROOT_TWO_PI = 0.3989422804014327

F32 = jnp.float32
BF16 = jnp.bfloat16
VMEM_BYTES = 60 * 1024 * 1024

STACK = (("A1", D), ("Q", D), ("K", D), ("V", D), ("O", D), ("A2", D), ("G", FF), ("U", FF), ("F", FF))
ROW_A1, ROW_A2, ROW_Q, ROW_K, ROW_V, ROW_O = (D * place for place in range(6))
ROW_G = 6 * D
ROW_U = ROW_G + FF
ROW_F = ROW_U + FF
ROWS_ALL = ROW_F + FF
HELD_ROWS = dict(
    A1=ROW_A1, A2=ROW_A2, Q=ROW_Q, K=ROW_K, V=ROW_V, O=ROW_O, G=ROW_G, U=ROW_U, F=ROW_F
)
HEAD_ORDER = [
    side * (HEADS // SIDES) + chunk * (SPAN * UNIT // HD) + head
    for chunk in range(D // CHUNK)
    for side in range(SIDES)
    for head in range(SPAN * UNIT // HD)
]


def to_held(by_head):
    per_chunk = SPAN * UNIT // HD
    return by_head.reshape(SIDES, -1, per_chunk).transpose(1, 0, 2).reshape(-1)


def from_held(held):
    per_chunk = SPAN * UNIT // HD
    return held.reshape(-1, SIDES, per_chunk).transpose(1, 0, 2).reshape(-1)


def held_units():
    places = []
    for side in range(SIDES):
        for kind, rows in STACK:
            count = rows // SIDES // UNIT
            for unit in range(count):
                if kind in ("A1", "A2"):
                    place = side * count + unit
                else:
                    place = (unit // SPAN * SIDES + side) * SPAN + unit % SPAN
                places.append(HELD_ROWS[kind] // UNIT + place)
    return np.array(places, np.int32)


def dot_nn(left, right):
    return jnp.dot(left, right, preferred_element_type=F32)


def dot_nt(left, right):
    return lax.dot_general(left, right, (((1,), (1,)), ((), ())), preferred_element_type=F32)


def slots_before(owner_list):
    unit_count = owner_list.shape[0]
    same_owner = owner_list[:, None] == owner_list[None, :]
    row_ids = lax.broadcasted_iota(jnp.int32, (unit_count, unit_count), 0)
    col_ids = lax.broadcasted_iota(jnp.int32, (unit_count, unit_count), 1)
    return jnp.sum(jnp.where(same_owner & (col_ids < row_ids), 1, 0), axis=1).astype(jnp.int32)


def rope_tables(positions):
    quarter = HD // 8
    head_ids = jnp.array(HEAD_ORDER, jnp.int32)[:, None]
    column = lax.broadcasted_iota(jnp.int32, (HEADS, quarter), 1)
    flat_index = (column * HEADS + head_ids).astype(F32)
    low_log = math.log(math.pi)
    high_log = math.log(10.0 * math.pi)
    frequency = jnp.exp(low_log + (high_log - low_log) * flat_index / (HEADS * quarter))
    placed = (2.0 * positions.astype(F32) + 1.0) / SIDE - 1.0
    along_rows = placed[:, 0].reshape(1, 1, -1) * frequency[:, :, None]
    along_cols = placed[:, 1].reshape(1, 1, -1) * frequency[:, :, None]
    angles = jnp.concatenate([along_rows, along_cols], axis=1).reshape(HEADS * 2 * quarter, -1)
    return jnp.cos(angles), jnp.sin(angles)


def deal_matrix(core):
    target = lax.broadcasted_iota(jnp.int32, (CHUNK, CHUNK), 0)
    source = lax.broadcasted_iota(jnp.int32, (CHUNK, CHUNK), 1)
    parity = (target // HALF_CHUNK + core) % 2
    inner = target % HALF_CHUNK
    unit = inner % SPAN
    row = inner // SPAN % 2
    piece = inner // (2 * SPAN) % (UNIT // 4)
    side = inner // (2 * SPAN * (UNIT // 4))
    return (source == (side * SPAN + unit) * UNIT + 4 * piece + 2 * parity + row).astype(BF16)


def layer_kernel(
    images,
    slots_refs,
    place_ref,
    ends_ref,
    scal_ref,
    x_ref,
    cot_ref,
    gb_ref,
    cond_ref,
    cos_ref,
    sin_ref,
    deal_ref,
    outs_hbm,
    early_keep,
    early_send,
    late_keep,
    late_send,
    n2_hbm,
    mids_hbm,
    note_hbm,
    w,
    unit_s,
    coef_s,
    qtok_s,
    p_s,
    qk_s,
    v_s,
    o_s,
    x2_s,
    n1_s,
    n2_s,
    ga_s,
    do_s,
    dot_s,
    ff_s,
    dn2_s,
    dqkv_s,
    early_s,
    late_s,
    outs_s,
    note_s,
    ds_s,
    note_low,
    w_sem,
    o_sem,
):
    toks = images * SEQ
    sends = []

    def send(src, dst):
        copy = pltpu.make_async_copy(src, dst, o_sem.at[len(sends)])
        copy.start()
        sends.append(copy)

    groups = (0, ROW_Q, ROW_O, ROW_G, ROWS_ALL)

    def fetch(low, high):
        first = 0
        for array, slots_ref in enumerate(slots_refs):

            @pl.loop(ends_ref[array, low // 3], ends_ref[array, low // 3 + 1])
            def _(index, slots_ref=slots_ref, first=first):
                unit = place_ref[0, first + index]
                group = jnp.int32(low)
                for bound in groups[low + 1 : high]:
                    group += jnp.where(unit >= bound // UNIT, 1, 0)
                pltpu.make_async_copy(
                    slots_ref.at[place_ref[1, first + index]],
                    w.at[pl.ds(pl.multiple_of(unit * UNIT, UNIT), UNIT)],
                    w_sem.at[group],
                ).start()

            first += slots_ref.shape[0]

    fetch(0, 3)

    def weights_here(index):
        low, high = groups[index : index + 2]
        region = w.at[pl.ds(low, high - low)]
        pltpu.make_async_copy(region, region, w_sem.at[index]).wait()

    def image_rows(image):
        return pl.ds(image * SEQ, SEQ)

    note_s[...] = jnp.zeros_like(note_s)
    note_s[:images] = cond_ref[:images].astype(F32)

    def note(place, row):
        high = row.astype(BF16).astype(F32)
        lanes = slice(0, row.shape[1])
        note_s[place : place + 1, lanes] = high
        note_s[place + 2 * images + 1 : place + 2 * images + 2, lanes] = row - high

    weights_here(0)
    fetch(3, 4)
    gain_one = 1.0 + dot_nn(cond_ref[...], w[ROW_A1 : ROW_A1 + D])
    gain_two = 1.0 + dot_nn(cond_ref[...], w[ROW_A2 : ROW_A2 + D])
    for image in range(images):
        x = x_ref[image_rows(image)]
        inverse = lax.rsqrt(jnp.mean(x * x, axis=-1, keepdims=True) + NORM_EPS)
        n1_s[image_rows(image)] = (x * inverse * gain_one[image : image + 1]).astype(BF16)
    send(n1_s, mids_hbm.at[1])
    weights_here(1)
    unit_s[:D] = dot_nt(w[ROW_Q : ROW_Q + D], n1_s[...])
    unit_s[D:] = dot_nt(w[ROW_K : ROW_K + D], n1_s[...])
    v_s[...] = dot_nt(w[ROW_V : ROW_V + D], n1_s[...]).astype(BF16)

    @pl.loop(0, 2 * HEADS)
    def _(index):
        head = lax.rem(index, HEADS)
        rows = pl.ds(pl.multiple_of(index * HD, HD), HD)
        angle_rows = pl.ds(pl.multiple_of(head * 16, 16), 16)
        raw = unit_s[rows]
        inverse = lax.rsqrt(jnp.sum(raw * raw, axis=0, keepdims=True) + COS_EPS)
        unit = raw * inverse
        root = scal_ref[HEADS + head]
        unit_s[rows] = unit
        coef_s[pl.ds(index, 1)] = root * inverse
        scaled = unit * root
        first, second = scaled[:16], scaled[16:32]
        cosine, sine = cos_ref[angle_rows], sin_ref[angle_rows]
        turned = jnp.concatenate(
            [first * cosine - second * sine, second * cosine + first * sine, scaled[32:]], axis=0
        )
        qk_s[rows] = turned.astype(BF16)

    qtok_s[...] = qk_s[:D].T

    def head_rows(head):
        return pl.ds(pl.multiple_of(head * HD, HD), HD)

    def pair_lanes(pair):
        return pl.ds(pl.multiple_of(pair * 2 * HD, 2 * HD), 2 * HD)

    @pl.loop(0, HEADS // 2)
    def _(pair):
        for image in range(images):
            cols = image_rows(image)
            query = qtok_s[cols, pair_lanes(pair)]
            mixed = []
            for half in range(2):
                head = pair * 2 + half
                scores = dot_nn(
                    query[:, half * HD : (half + 1) * HD], qk_s[head_rows(HEADS + head), cols]
                )
                exp_scores = jnp.exp(scores - scal_ref[head])
                inverse = 1.0 / jnp.sum(exp_scores, axis=-1, keepdims=True)
                probs = (exp_scores * inverse).astype(BF16)
                p_s[head, cols] = probs
                mixed.append(dot_nt(probs, v_s[head_rows(head), cols]))
            o_s[cols, pair_lanes(pair)] = jnp.concatenate(mixed, axis=1)

    weights_here(2)
    x2_s[...] = x_ref[...] + dot_nn(o_s[...].astype(BF16), w[ROW_O : ROW_O + D])
    for image in range(images):
        x2 = x2_s[image_rows(image)]
        inverse = lax.rsqrt(jnp.mean(x2 * x2, axis=-1, keepdims=True) + NORM_EPS)
        n2_s[image_rows(image)] = (x2 * inverse * gain_two[image : image + 1]).astype(BF16)
    send(n2_s, n2_hbm)

    weights_here(3)
    chunks = FF // CHUNK
    width = D

    def deal(field, store, place):
        dealt = dot_nt(deal_ref[...], field).astype(BF16)
        store[0, place] = dealt[:HALF_CHUNK]
        store[1, place] = dealt[HALF_CHUNK:]

    for start in range(0, FF, width):

        def part(base):
            return w[base + start : base + start + width]

        gate = dot_nt(n2_s[...], part(ROW_G))
        up = dot_nt(n2_s[...], part(ROW_U))
        grad_hidden = dot_nt(gb_ref[...], part(ROW_F))
        phi_sum = 0.5 * (1.0 + lax.erf(gate * ROOT_HALF))
        density = INV_ROOT_TWO_PI * jnp.exp(-0.5 * gate * gate)
        gelu = gate * phi_sum
        hidden = (gelu * up).astype(BF16)
        grad_gate = (grad_hidden * up * (phi_sum + gate * density)).astype(BF16)
        grad_up = (grad_hidden * gelu).astype(BF16)
        ff = dot_nn(hidden, part(ROW_F))
        dn2 = dot_nn(grad_gate, part(ROW_G)) + dot_nn(grad_up, part(ROW_U))
        if start == 0:
            ff_s[...] = ff
            dn2_s[...] = dn2
        else:
            ff_s[...] += ff
            dn2_s[...] += dn2
        for at in range(0, width, CHUNK):
            place = (start + at) // CHUNK
            deal(hidden[:, at : at + CHUNK], early_s, place)
            deal(grad_gate[:, at : at + CHUNK], early_s, chunks + place)
            deal(grad_up[:, at : at + CHUNK], late_s, place)

    send(early_s.at[0], early_keep)
    send(early_s.at[1], early_send)
    outs_s[0] = (x2_s[...] + ff_s[...]).astype(BF16)
    send(outs_s.at[0], outs_hbm.at[0])

    def norm_back(x, gain, grad_normed):
        inverse = lax.rsqrt(jnp.mean(x * x, axis=-1, keepdims=True) + NORM_EPS)
        scaled = grad_normed * gain
        inner = jnp.mean(x * scaled, axis=-1, keepdims=True)
        grad_x = inverse * scaled - x * (inverse * inverse * inverse * inner)
        return grad_x, jnp.sum(grad_normed * x * inverse, axis=0, keepdims=True)

    for image in range(images):
        rows = image_rows(image)
        grad_x, grad_gain = norm_back(x2_s[rows], gain_two[image : image + 1], dn2_s[rows])
        grad = cot_ref[rows].astype(F32) * scal_ref[2 * HEADS + image] + grad_x
        x2_s[rows] = grad
        ga_s[rows] = grad.astype(BF16)
        note(2 * images + image, grad_gain)
    send(ga_s, mids_hbm.at[0])

    do_s[...] = dot_nt(ga_s[...], w[ROW_O : ROW_O + D]).astype(BF16)
    dot_s[...] = dot_nt(w[ROW_O : ROW_O + D], ga_s[...]).astype(BF16)
    ds_s[...] = jnp.zeros_like(ds_s)

    @pl.loop(0, HEADS // 2)
    def _(pair):
        for image in range(images):
            cols = image_rows(image)
            grads_mixed = do_s[cols, pair_lanes(pair)]
            inners = grads_mixed.astype(F32) * o_s[cols, pair_lanes(pair)]
            for half in range(2):
                head = pair * 2 + half
                lanes = slice(half * HD, (half + 1) * HD)
                rows, key_rows = head_rows(head), head_rows(HEADS + head)
                key, value = qk_s[key_rows, cols], v_s[rows, cols]
                probs = p_s[head, cols]
                grad_probs = dot_nn(grads_mixed[:, lanes], value)
                inner = jnp.sum(inners[:, lanes], axis=-1, keepdims=True)
                grad_scores = (probs.astype(F32) * (grad_probs - inner)).astype(BF16)
                grad_query = dot_nt(key, grad_scores)
                grad_key = dot_nn(qk_s[rows, cols], grad_scores)
                grad_value = dot_nn(dot_s[rows, cols], probs)
                angle_rows = pl.ds(pl.multiple_of(head * 16, 16), 16)
                cosine, sine = cos_ref[angle_rows, cols], sin_ref[angle_rows, cols]
                along = jnp.zeros((1, SEQ), F32)
                for grad, own_rows, place in (
                    (grad_query, rows, head),
                    (grad_key, key_rows, HEADS + head),
                ):
                    first, second = grad[:16], grad[16:32]
                    back = jnp.concatenate(
                        [
                            first * cosine + second * sine,
                            second * cosine - first * sine,
                            grad[32:],
                        ],
                        axis=0,
                    )
                    unit = unit_s[own_rows, cols]
                    inner_unit = jnp.sum(unit * back, axis=0, keepdims=True)
                    along += inner_unit
                    dqkv_s[own_rows, cols] = (
                        coef_s[pl.ds(place, 1), cols] * (back - unit * inner_unit)
                    ).astype(BF16)
                value_rows = head_rows(2 * HEADS + head)
                dqkv_s[value_rows, cols] = grad_value.astype(BF16)
                ds_s[pl.ds(head, 1)] += along

    per_kind = D // CHUNK
    for place in range(per_kind):
        deal(o_s[:, place * CHUNK : (place + 1) * CHUNK].astype(BF16), late_s, chunks + place)
    for place in range(3 * per_kind):
        dealt = dot_nn(deal_ref[...], dqkv_s[place * CHUNK : (place + 1) * CHUNK]).astype(BF16)
        late_s[0, chunks + per_kind + place] = dealt[:HALF_CHUNK]
        late_s[1, chunks + per_kind + place] = dealt[HALF_CHUNK:]
    send(late_s.at[0], late_keep)
    send(late_s.at[1], late_send)
    dn1 = dot_nn(dqkv_s[:D].T, w[ROW_Q : ROW_Q + D])
    dn1 += dot_nn(dqkv_s[D : 2 * D].T, w[ROW_K : ROW_K + D])
    dn1 += dot_nn(dqkv_s[2 * D :].T, w[ROW_V : ROW_V + D])
    dn2_s[...] = dn1
    for image in range(images):
        rows = image_rows(image)
        grad_x, grad_gain = norm_back(x_ref[rows], gain_one[image : image + 1], dn2_s[rows])
        outs_s[1, rows] = (x2_s[rows] + grad_x).astype(BF16)
        note(images + image, grad_gain)
    send(outs_s.at[1], outs_hbm.at[1])
    ones = jnp.ones((8, SEQ), F32)
    scale_row = lax.dot_general(
        ones,
        ds_s[...],
        (((1,), (1,)), ((), ())),
        precision=lax.Precision.HIGHEST,
        preferred_element_type=F32,
    )
    note(3 * images, scale_row[:1])
    note_low[...] = note_s[...].astype(BF16)
    send(note_low, note_hbm)
    for copy in sends:
        copy.wait()


def run_layer(images, places, ends, scalars, x, cotangent, grad_out, cond, cosine, sine, deal, slots):
    toks = images * SEQ
    chunks = FF // CHUNK
    any_spec = pl.BlockSpec(memory_space=pl.ANY)
    vmem = pl.BlockSpec(memory_space=pltpu.VMEM)
    smem = pl.BlockSpec(memory_space=pltpu.SMEM)
    field = jax.ShapeDtypeStruct((toks, D), BF16)

    def dealt(count):
        return jax.ShapeDtypeStruct((count, HALF_CHUNK, toks), BF16)

    pair = jax.ShapeDtypeStruct((2, toks, D), BF16)
    late = chunks + 4 * D // CHUNK
    outs = [pair, dealt(2 * chunks), dealt(2 * chunks), dealt(late), dealt(late), field, pair]
    outs += [jax.ShapeDtypeStruct((16, D), BF16)]
    wide = pltpu.VMEM((toks, D), F32)
    low = pltpu.VMEM((toks, D), BF16)
    scratch = [
        pltpu.VMEM((ROWS_ALL, D), BF16),
        pltpu.VMEM((2 * D, toks), F32),
        pltpu.VMEM((2 * HEADS, toks), F32),
        low,
        pltpu.VMEM((HEADS, toks, SEQ), BF16),
        pltpu.VMEM((2 * D, toks), BF16),
        pltpu.VMEM((D, toks), BF16),
        wide,
        wide,
        low,
        low,
        low,
        low,
        pltpu.VMEM((D, toks), BF16),
        wide,
        wide,
        pltpu.VMEM((3 * D, toks), BF16),
        pltpu.VMEM((2, 2 * chunks, HALF_CHUNK, toks), BF16),
        pltpu.VMEM((2, late, HALF_CHUNK, toks), BF16),
        pltpu.VMEM((2, toks, D), BF16),
        pltpu.VMEM((16, D), F32),
        pltpu.VMEM((16, SEQ), F32),
        pltpu.VMEM((16, D), BF16),
        pltpu.SemaphoreType.DMA((4,)),
        pltpu.SemaphoreType.DMA((16,)),
    ]

    operands = [places, ends, scalars, x, cotangent, grad_out, cond, cosine, sine, deal]
    here = len(operands)

    def body(*refs):
        layer_kernel(
            images, refs[here : here + len(slots)], *refs[:here], *refs[here + len(slots) :]
        )

    return pl.pallas_call(
        body,
        out_shape=outs,
        in_specs=[smem] * 3 + [vmem] * 7 + [any_spec] * len(slots),
        out_specs=[any_spec] * len(outs),
        scratch_shapes=scratch,
        compiler_params=pltpu.CompilerParams(vmem_limit_bytes=VMEM_BYTES),
        cost_estimate=pl.CostEstimate(
            flops=2 * 3 * ROWS_ALL * D * toks, bytes_accessed=ROWS_ALL * D * 4, transcendentals=0
        ),
        name="layer",
    )(*operands, *slots)


def weight_grads(lefts, rights, kinds, first=0, here=3):
    rows, toks = lefts[0].shape[1:]
    pieces = rows // (SIDES * 2 * SPAN)
    total = sum(count for count, _ in kinds)
    steps = total // here
    step_rights = [place for count, place in kinds for _ in range(count // here)]
    operands, specs = list(lefts), []
    for left in lefts:
        specs.append(pl.BlockSpec((here, rows, toks), lambda step: (first // here + step, 0, 0)))
    for parts in rights:
        for part in parts:
            field, at = part if isinstance(part, tuple) else (part[None], 0)
            operands.append(field)
            specs.append(pl.BlockSpec((None, toks, D), lambda step, at=at: (at, 0, 0)))

    def body(*refs):
        out_ref, count = refs[-1], len(lefts)
        step = pl.program_id(0)
        for place in range(len(rights)):
            own = refs[count * (place + 1) : count * (place + 2)]
            mine = [index for index, right in enumerate(step_rights) if right == place]

            @pl.when((step >= mine[0]) & (step <= mine[-1]))
            def _(own=own):
                summed = dot_nn(refs[0][...].reshape(here * rows, toks), own[0][...])
                for left, right in zip(refs[1:count], own[1:]):
                    summed += dot_nn(left[...].reshape(here * rows, toks), right[...])
                for chunk in range(here):
                    out_ref[:, :, chunk] = (
                        summed[chunk * rows : (chunk + 1) * rows]
                        .reshape(SIDES, pieces, 2 * SPAN, D)
                        .astype(BF16)
                    )

    return pl.pallas_call(
        body,
        out_shape=jax.ShapeDtypeStruct((SIDES, pieces, total, 2 * SPAN, D), BF16),
        grid=(steps,),
        in_specs=specs,
        out_specs=pl.BlockSpec(
            (SIDES, pieces, here, 2 * SPAN, D), lambda step: (0, 0, step, 0, 0)
        ),
        compiler_params=pltpu.CompilerParams(vmem_limit_bytes=VMEM_BYTES),
        cost_estimate=pl.CostEstimate(
            flops=2 * len(lefts) * total * rows * toks * D,
            bytes_accessed=2 * len(lefts) * (total * rows + len(rights) * D) * toks
            + 2 * total * rows * D,
            transcendentals=0,
        ),
        name="weight_grads",
    )(*operands)


def adam_step(weights, first_new, second_new, rate):
    fix_one = 1.0 - math.pow(BETA_ONE, STEP)
    fix_two = 1.0 - math.pow(BETA_TWO, STEP)
    return weights * (1.0 - rate * WEIGHT_DECAY) - rate * (first_new / fix_one) / (
        jnp.sqrt(second_new / fix_two) + ADAM_EPS
    )


def moments(first, second, grad):
    return (
        BETA_ONE * first + (1.0 - BETA_ONE) * grad,
        BETA_TWO * second + (1.0 - BETA_TWO) * grad * grad,
    )


def pack(fields):
    def body(*refs):
        for place, ref in enumerate(refs[:-1]):
            refs[-1][place] = ref[...]

    return pl.pallas_call(
        body,
        out_shape=jax.ShapeDtypeStruct((len(fields), *fields[0].shape), fields[0].dtype),
        name="pack",
    )(*fields)


def factor_sums(notes, indices, images, mp_count):
    rows_wanted = 2 * (D // mp_count // UNIT)
    pieces = 2 * images + 1

    def body(*refs):
        index_ref, sums_ref, scale_ref = refs[-3:]
        rows = jnp.concatenate([ref[...].reshape(-1, D) for ref in refs[:-3]])
        row = lax.broadcasted_iota(jnp.int32, (rows_wanted, D), 0)
        feature = lax.broadcasted_iota(jnp.int32, (rows_wanted, D), 1)
        unit = row // (2 * SPAN) * SPAN + row % SPAN
        wanted = (index_ref[0] * (rows_wanted // 2) + unit) * UNIT
        wanted += 2 * index_ref[1] + row // SPAN % 2
        features = (feature == wanted).astype(BF16)
        count = rows.shape[0]
        source = lax.broadcasted_iota(jnp.int32, (count, count), 0)
        target = lax.broadcasted_iota(jnp.int32, (count, count), 1)
        ahead = target - source
        is_cond = source % 16 < images
        cond_rows = dot_nt(features, rows).astype(BF16)
        for place in range(2):
            first = images * (1 + place)
            pick_rows = is_cond & ((ahead == first) | (ahead == first + pieces))
            chosen = dot_nn(cond_rows, pick_rows.astype(BF16)).astype(BF16)
            sums_ref[place] = dot_nn(chosen, rows)
        column = lax.broadcasted_iota(jnp.int32, (8, count), 1) % 16
        last = (column == 3 * images) | (column == 3 * images + pieces)
        scale_ref[...] = dot_nn(last.astype(BF16), rows)

    return pl.pallas_call(
        body,
        out_shape=[
            jax.ShapeDtypeStruct((2, rows_wanted, D), F32),
            jax.ShapeDtypeStruct((8, D), F32),
        ],
        in_specs=[pl.BlockSpec(memory_space=pltpu.VMEM)] * len(notes)
        + [pl.BlockSpec(memory_space=pltpu.SMEM)],
        compiler_params=pltpu.CompilerParams(vmem_limit_bytes=VMEM_BYTES),
        name="factor_sums",
    )(*notes, indices)


def route(sum_a, sum_fg, sum_rest, placed, slots, dp_count):
    chunks, few = FF // CHUNK, D // CHUNK
    rows = 2 * placed.shape[1]
    to_row = np.arange(dp_count * 2 * slots)
    columns = np.stack([to_row // (2 * slots) * slots + to_row % slots, to_row // slots % 2], axis=1)
    placed_rows = jnp.broadcast_to(placed.reshape(-1, 1, SPAN), (rows // (2 * SPAN), 2, SPAN))

    def body(a_ref, fg_ref, rest_ref, placed_ref, columns_ref, pieces_ref, out_ref):
        start = 0
        for field in (
            a_ref[0],
            rest_ref[chunks + few :],
            rest_ref[chunks : chunks + few],
            a_ref[1],
            fg_ref[chunks:],
            rest_ref[:chunks],
            fg_ref[:chunks],
        ):
            field = field.reshape(-1, D)
            pieces_ref[start : start + field.shape[0]] = field
            start += field.shape[0]
        row = lax.broadcasted_iota(jnp.int32, (1, rows), 1) // SPAN % 2
        chosen = (columns_ref[:, :1] == placed_ref[...]) & (columns_ref[:, 1:] == row)
        out_ref[...] = dot_nn(chosen.astype(BF16), pieces_ref[...].astype(BF16)).astype(BF16)

    return pl.pallas_call(
        body,
        out_shape=[
            jax.ShapeDtypeStruct((rows, D), F32),
            jax.ShapeDtypeStruct((dp_count * 2 * slots, D), BF16),
        ],
        compiler_params=pltpu.CompilerParams(vmem_limit_bytes=VMEM_BYTES),
        name="route",
    )(sum_a, sum_fg, sum_rest, placed_rows.reshape(1, rows), jnp.array(columns, jnp.int32))


def add(*terms):
    total = terms[0].astype(F32)
    for term in terms[1:]:
        total = total + term.astype(F32)
    return total


class Ring:
    def __init__(self, dp_count):
        self.count = dp_count // 2
        pairs = []
        for place in range(self.count):
            for core in range(2):
                pairs.append(
                    (self.chip(place) * 2 + core, self.chip((place + 1) % self.count) * 2 + core)
                )
        self.onward = pairs
        self.backward = [(b, a) for a, b in pairs]
        self.twins = [(index, index ^ 1) for index in range(dp_count)]

    def chip(self, place):
        column = self.count // 2
        return 2 * place if place < column else 2 * (self.count - 1 - place) + 1

    def here(self):
        chip = lax.axis_index("dp") // 2
        return jnp.where(chip % 2 == 0, chip // 2, self.count - 1 - chip // 2)

    def chip_at(self, offset):
        place = (self.here() + offset + self.count) % self.count
        column = self.count // 2
        return jnp.where(place < column, 2 * place, 2 * (self.count - 1 - place) + 1)

    def on(self, field):
        return lax.ppermute(field, "dp", self.onward)

    def back(self, field):
        return lax.ppermute(field, "dp", self.backward)

    def twin(self, field):
        return lax.ppermute(field, "dp", self.twins)


def after(field, *others):
    return lax.optimization_barrier((field, others))[0]


def swap_mp(field):
    return lax.ppermute(field, "mp", [(0, 1), (1, 0)])


class Labels:
    def __init__(self, rows):
        self.rows = list(rows)

    def __getitem__(self, cut):
        return Labels(self.rows[cut])

    def moved(self, hop, mp, core):
        return Labels((h + hop, m ^ mp, c ^ core, slot) for h, m, c, slot in self.rows)


class LabelMoves:
    def on(self, field):
        return field.moved(-1, 0, 0)

    def back(self, field):
        return field.moved(1, 0, 0)

    def swap(self, field):
        return field.moved(0, 1, 0)

    def twin(self, field):
        return field.moved(0, 0, 1)

    def cat(self, *fields):
        return Labels(row for field in fields for row in field.rows)

    def together(self, *fields):
        return fields


class Moves:
    def __init__(self, ring):
        self.on, self.back, self.twin, self.swap = ring.on, ring.back, ring.twin, swap_mp

    def cat(self, *fields):
        return jnp.concatenate(fields)

    def together(self, *fields):
        return lax.optimization_barrier(fields)


def gather_slots(moves, own, slots, early=(), use_early=None, late=(), use_late=None):
    cat, on, back, swap, twin = moves.cat, moves.on, moves.back, moves.swap, moves.twin
    cut = slots // 2
    rest = slots - cut
    first, second = own[:cut], own[cut:]
    hop = [on(second), back(second), swap(first), twin(own)]
    f0, b0, y0, c0, second, *early = moves.together(*hop, second, *early)
    wide = cat(first, y0)
    hop = [on(wide), back(wide), swap(second), twin(cat(y0, f0, b0))]
    f1, b1, y1, c1, f0, b0, *late = moves.together(*hop, f0, b0, *late)
    hop = [on(cat(f0, f1)), back(cat(b0, b1)), swap(cat(f0, b0)), twin(cat(f1, b1, y1))]
    done = (*use_early(*early), *use_late(*early, *late)) if early else ()
    f2, b2, y2, c2, *done = moves.together(*hop, *done)
    crossing = cat(f2[:rest], b2[:rest])
    hop = [on(f2), back(b2), swap(crossing), twin(cat(f2, b2, y2))]
    f3, b3, y3, c3 = moves.together(*hop)
    half = (slots + cut) // 2
    crossing = cat(f3[:rest], b3[:rest])
    hop = [on(f3[:half]), back(b3[half:]), swap(crossing), twin(cat(f3, b3, y3))]
    f4, b4, y4, c4 = moves.together(*hop)
    y5 = swap(cat(f4[:rest], b4[: max(0, rest - half)]))
    c5 = [twin(f4), twin(b4), twin(y4)]
    return [own, f0, b0, y0, c0, f1, b1, y1, c1, f2, b2, y2, c2, f3, b3, y3, c3, f4, b4, y4, c4, y5] + c5 + [twin(y5)], done


def both_halves(own, other, half, axis=0):
    return jnp.where(
        half == 0,
        jnp.concatenate([own, other], axis=axis),
        jnp.concatenate([other, own], axis=axis),
    )


def pick(field, *places):
    for place in places:
        field = lax.dynamic_index_in_dim(field, place, 0, keepdims=False)
    return field


class RingSum:
    def __init__(self, ring, field, half, note=None):
        self.ring, self.field, self.half = ring, field, half
        self.distance = ring.count // 2
        self.on = self.back = None
        self.own = self.note_on = self.note_back = note
        self.seen = []

    def block(self, offset):
        return lax.dynamic_index_in_dim(self.field, self.ring.chip_at(offset), 1, keepdims=False)

    def step(self, *others):
        ring, far, distance = self.ring, self.ring.count // 2, self.distance
        chunks = self.field.shape[2]
        if distance == far:
            block = self.block(far)
            on, back = block[0], block[1]
        else:
            on, back = self.block(distance), self.block(-distance)
            if distance == far - 1:
                on = jnp.stack([add(on[0], self.on).astype(BF16), on[1]])
                back = jnp.stack([back[0], add(back[1], self.back).astype(BF16)])
            else:
                on, back = add(on, self.on).astype(BF16), add(back, self.back).astype(BF16)
        if self.own is not None:
            axis = on.ndim - 3
            shape = on.shape[:axis] + (2 // (axis + 1),) + on.shape[axis + 1 :]
            on = jnp.concatenate([on, self.note_on.reshape(shape)], axis=axis)
            back = jnp.concatenate([back, self.note_back.reshape(shape)], axis=axis)
        if others:
            on, back = after(on, *others), after(back, *others)
        on, back = lax.optimization_barrier((ring.on(on), ring.back(back)))
        if self.own is not None:
            self.note_on = on[..., chunks:, :, :].reshape(self.own.shape)
            self.note_back = back[..., chunks:, :, :].reshape(self.own.shape)
            self.seen += [self.note_on, self.note_back]
            on, back = on[..., :chunks, :, :], back[..., :chunks, :, :]
        self.on, self.back = on, back
        self.distance -= 1
        return self.on, self.back

    def total(self):
        total = add(self.block(0), self.on, self.back)
        other = swap_mp(pick(total.astype(BF16), 1 - self.half))
        return add(pick(total, self.half), other)

    def notes(self):
        return [self.own] + self.seen[:-1]


def on_device(
    tokens,
    conditioning,
    sigmas,
    positions,
    cotangent,
    owners,
    master,
    moment_one,
    moment_two,
    scale_state,
):
    dp_count = lax.axis_size("dp")
    mp_count = lax.axis_size("mp")
    dp_index = lax.axis_index("dp")
    mp_index = lax.axis_index("mp")
    images = conditioning.shape[0] // mp_count
    toks = images * SEQ
    slots = master.shape[1]
    unit_rows = master.shape[2]
    unit_count = owners.shape[1]
    heads_here = scale_state.shape[1]
    paired = dp_count * 2 == UNIT
    core = dp_index % 2 if paired else 0

    def mine(field, rows):
        return lax.dynamic_slice_in_dim(field, mp_index * rows, rows, 0)

    rounded = master[0].astype(BF16)
    halves_here = jnp.concatenate([owners[0].astype(F32), scale_state[0]])[None]
    ring = Ring(dp_count) if paired else None
    if paired:
        own_labels = Labels((0, 0, 0, slot) for slot in range(slots))
        arrays, _ = gather_slots(LabelMoves(), own_labels, slots)
        labels = [row for field in arrays for row in field.rows]
        sizes = [len(field.rows) for field in arrays]
        assert len(set((h % ring.count, m, c, slot) for h, m, c, slot in labels)) == len(labels)
        hops, sides, cores, numbers = (jnp.array(column, jnp.int32) for column in zip(*labels))
        owner = ring.chip_at(hops) * 2 + (dp_index % 2 + cores) % 2
        side = (mp_index + sides) % 2
        slot_ids = (side * dp_count + owner) * slots + numbers
    else:
        sizes = [mp_count * dp_count * slots]
        slot_ids = lax.broadcasted_iota(jnp.int32, (mp_count * dp_count * slots, 1), 0)[:, 0]

    def prepare_places(halves_other):
        halves_all = both_halves(halves_here, halves_other, mp_index)
        owners_all = halves_all[:, :unit_count].astype(jnp.int32)
        before = jnp.stack([slots_before(owners_all[half]) for half in range(mp_count)])
        half_ids = lax.broadcasted_iota(jnp.int32, owners_all.shape, 0)
        unit_slots = ((half_ids * dp_count + owners_all) * slots + before).reshape(-1)
        belongs = jnp.array(held_units())
        match = slot_ids[:, None] == unit_slots[None, :]
        places = jnp.where(
            jnp.any(match, axis=1),
            jnp.sum(jnp.where(match, belongs[None, :], 0), axis=1),
            belongs.shape[0],
        )
        starts = np.cumsum([0] + sizes)
        array_ids = jnp.array(np.repeat(np.arange(len(sizes)), sizes), jnp.int32)
        slot_numbers = jnp.array(np.concatenate([np.arange(size) for size in sizes]), jnp.int32)
        key = places * starts[-1] + slot_numbers
        ahead = (array_ids[:, None] == array_ids[None, :]) & (key[None, :] < key[:, None])
        rank = jnp.sum(jnp.where(ahead, 1, 0), axis=1) + jnp.array(np.repeat(starts[:-1], sizes), jnp.int32)
        at_rank = rank[None, :] == lax.broadcasted_iota(jnp.int32, (starts[-1],) * 2, 0)
        sorted_places = jnp.stack(
            [
                jnp.sum(jnp.where(at_rank, field[None, :], 0), axis=1)
                for field in (places, slot_numbers)
            ]
        )
        own_array = array_ids[None, :] == lax.broadcasted_iota(
            jnp.int32, (len(sizes), array_ids.shape[0]), 0
        )
        ends = jnp.stack(
            [
                jnp.sum(jnp.where(own_array & (places < bound // UNIT)[None, :], 1, 0), axis=1)
                for bound in (0, ROW_G, ROWS_ALL)
            ],
            axis=1,
        )
        return sorted_places, ends

    def prepare_fields(halves_other, tokens, conditioning, sigmas, positions, cotangent):
        halves_all = both_halves(halves_here, halves_other, mp_index)
        scales_all = halves_all[:, unit_count:].reshape(-1)
        scales_held = to_held(scales_all)
        square = sigmas * sigmas
        data_square = SIGMA_DATA * SIGMA_DATA
        loss_weight = 4.0 * square * data_square / ((square + data_square) * (square + data_square))
        scalars = jnp.concatenate([scales_held, jnp.sqrt(scales_held), mine(loss_weight, images)])
        cosine, sine = rope_tables(mine(positions, images))
        cond = jnp.pad(mine(conditioning, images).astype(BF16), ((0, 16 - images), (0, 0)))

        grad_out = (
            mine(cotangent, toks).astype(F32).reshape(images, SEQ, D)
            * mine(loss_weight, images)[:, None, None]
        ).astype(BF16).reshape(toks, D)
        return (
            scalars,
            scales_all,
            cosine,
            sine,
            cond,
            grad_out,
            deal_matrix(core),
            mine(tokens, toks),
            mine(cotangent, toks),
        )

    halves_other = swap_mp(halves_here)
    if paired:
        gathered, prepared = gather_slots(
            Moves(ring),
            rounded,
            slots,
            (halves_other,),
            prepare_places,
            (tokens, conditioning, sigmas, positions, cotangent),
            prepare_fields,
        )
    else:
        gathered = [lax.all_gather(rounded, ("mp", "dp"), axis=0, tiled=True)]
        prepared = prepare_places(halves_other)
        prepared += prepare_fields(
            halves_other, tokens, conditioning, sigmas, positions, cotangent
        )
    places, ends, scalars, scales_all, cosine, sine, cond = prepared[:7]
    grad_out, deal, x_own, cot_own = prepared[7:]
    (
        outs_low,
        early_keep,
        early_send,
        late_keep,
        late_send,
        normed_two,
        mids,
        note,
    ) = run_layer(
        images, places, ends, scalars, x_own, cot_own, grad_out, cond, cosine, sine, deal, gathered
    )
    outs_other = swap_mp(outs_low)
    chunks, few = FF // CHUNK, D // CHUNK

    note = note.reshape(2, 8, D)

    def scale_grads(scale_row):
        scale_sum = from_held(scale_row[:HEADS]) / (2.0 * jnp.sqrt(scales_all))
        return lax.dynamic_slice_in_dim(scale_sum, mp_index * heads_here, heads_here, 0)

    if paired:
        out_both = (grad_out, ring.twin(grad_out))
        early_both = (early_keep, ring.twin(early_send))
        two_both = (normed_two, ring.twin(normed_two))
        late_send, mids_send = lax.optimization_barrier(
            (late_send, mids, early_both[1], two_both[1], out_both[1])
        )[:2]
        late_twin, mids_twin = ring.twin(late_send), ring.twin(mids_send)
        grad_fg = weight_grads(
            early_both, (out_both, two_both), ((chunks, 0), (chunks, 1)), here=chunks
        )
        sum_fg = RingSum(ring, grad_fg, mp_index, note)
        hop = sum_fg.step(late_twin, mids_twin)
        grad_rest = weight_grads(
            (after(late_keep, grad_fg), late_twin),
            (two_both, ((mids, 0), (mids_twin, 0)), ((mids, 1), (mids_twin, 1))),
            ((chunks, 0), (few, 1), (3 * few, 2)),
        )
        sum_rest = RingSum(ring, grad_rest, mp_index)
        late_owners = after(owners, grad_rest)[0]
        placed = (late_owners * slots + slots_before(late_owners))[None]
        hop = sum_fg.step(grad_rest)
        sum_rest.step()
        sum_fg.step()
        sum_rest.step()
        sum_fg.step()
        hop = sum_rest.step()
        outs_other = after(outs_other, hop)
        notes = pack(sum_fg.notes())
        sum_fg = sum_fg.total()
        notes = [notes, swap_mp(notes)]
        sum_rest.step()
        notes += [ring.twin(note) for note in notes]
        sum_rest = sum_rest.total()
        indices = jnp.stack([mp_index, dp_index]).astype(jnp.int32)
        sum_a, scale_rows = factor_sums(notes, indices, images, mp_count)
        scale_row = scale_rows[0]
        by_kind, outgoing = route(sum_a, sum_fg, sum_rest, placed, slots, dp_count)
        grad_shards = (
            by_kind.reshape(-1, 2, SPAN, D).transpose(0, 2, 1, 3).reshape(unit_count, 2 * D)
        )
        owned = lax.all_to_all(outgoing, "dp", split_axis=0, concat_axis=0, tiled=True)
        owned = owned.reshape(dp_count, 2, slots, D).transpose(2, 0, 1, 3)
        owned_grads = owned.reshape(slots, unit_rows, D).astype(F32)
    else:
        def units_of(parts, field, first, count):
            sides = jnp.stack(
                [weight_grads((part,), ((field,),), ((count, 0),), first) for part in parts]
            )
            sides = sides.reshape(2, mp_count, UNIT // 4, -1, 2, SPAN, D)
            return sides.transpose(1, 3, 5, 2, 0, 4, 6).reshape(mp_count, -1, unit_rows * D)

        early, late = (early_keep, early_send), (late_keep, late_send)
        summed = lax.psum_scatter(
            jnp.concatenate(
                [
                    units_of(late, mids[1], chunks + few, few),
                    units_of(late, mids[1], chunks + 2 * few, few),
                    units_of(late, mids[1], chunks + 3 * few, few),
                    units_of(late, mids[0], chunks, few),
                    units_of(early, normed_two, chunks, chunks),
                    units_of(late, normed_two, 0, chunks),
                    units_of(early, grad_out, 0, chunks),
                ],
                axis=1,
            ),
            "mp",
            scatter_dimension=0,
            tiled=True,
        )[0]
        summed = lax.psum_scatter(summed, "dp", scatter_dimension=1, tiled=True).astype(F32)
        notes = lax.all_gather(note, ("dp", "mp"), axis=0, tiled=True)
        rows = notes.reshape(-1, 16, D)
        count = 2 * images + 1
        wide = add(rows[:, images : images + count], rows[:, images + count : images + 2 * count])
        scale_row = jnp.sum(wide[:, -1], axis=0)
        cond_all = rows[:, :images].reshape(-1, D).astype(F32)
        gains_all = jnp.concatenate(
            [wide[:, place * images : (place + 1) * images].reshape(-1, D) for place in (0, 1)],
            axis=1,
        )
        cond_half = lax.dynamic_slice_in_dim(
            cond_all, mp_index * (D // mp_count), D // mp_count, 1
        )
        sum_a = lax.dot_general(
            cond_half,
            gains_all,
            (((0,), (0,)), ((), ())),
            precision=lax.Precision.HIGHEST,
            preferred_element_type=F32,
        )
        width = unit_rows * D // dp_count

        def piece(field):
            return lax.dynamic_slice_in_dim(
                field.reshape(-1, unit_rows * D), dp_index * width, width, 1
            )

        grad_shards = jnp.concatenate(
            [
                piece(sum_a[:, :D]),
                summed[: 4 * (D // mp_count // unit_rows)],
                piece(sum_a[:, D:]),
                summed[4 * (D // mp_count // unit_rows) :],
            ]
        )

        placed = owners[0] * slots + slots_before(owners[0])
        slot_rows = lax.broadcasted_iota(jnp.int32, (dp_count * slots, unit_count), 0)
        to_owners = (slot_rows == placed[None, :]).astype(BF16)
        outgoing = dot_nn(to_owners, grad_shards.astype(BF16)).astype(BF16)
        owned = lax.all_to_all(outgoing, "dp", split_axis=0, concat_axis=1, tiled=True)
        owned_grads = owned.reshape(slots, unit_rows, D).astype(F32)

    first_new, second_new = moments(moment_one[0], moment_two[0], owned_grads)
    master_new = adam_step(master[0], first_new, second_new, LEARN_RATE)
    outs_both = both_halves(outs_low, outs_other, mp_index, 1)
    output, input_grad = outs_both[0].astype(F32), outs_both[1].astype(F32)
    scale_grad = scale_grads(scale_row)
    scale_first, scale_second = moments(scale_state[1], scale_state[2], scale_grad)
    scale_new = adam_step(scale_state[0], scale_first, scale_second, SCALE_RATE)
    scale_update = jnp.stack([scale_first, scale_new])
    return (
        output,
        input_grad,
        grad_shards[None],
        master_new[None],
        first_new[None],
        second_new[None],
        scale_update,
        scale_second,
    )


def solution(mesh):
    in_specs = (
        P("dp", None),
        P("dp", None),
        P("dp"),
        P("dp", None, None),
        P("dp", None),
        P("mp", None),
        P("mp", "dp", None, None),
        P("mp", "dp", None, None),
        P("mp", "dp", None, None),
        P(None, "mp"),
    )
    out_specs = (
        P("dp", None),
        P("dp", None),
        P("mp", None, "dp"),
        P("mp", "dp", None, None),
        P("mp", "dp", None, None),
        P("mp", "dp", None, None),
        P(None, "mp"),
        P("mp"),
    )
    return jax.shard_map(
        on_device, mesh=mesh, in_specs=in_specs, out_specs=out_specs, check_vma=False
    )
```

```python
import math

import jax
import jax.numpy as jnp
import numpy as np
from jax import lax
from jax.experimental import pallas as pl
from jax.experimental.pallas import tpu as pltpu
from jax.sharding import PartitionSpec as P

D = 768
HEADS = 12
HD = 64
FF = 2304
SIDE = 16
STEP = 10
SEQ = 256
UNIT = 32
SPAN = 4
SIDES = 2
CHUNK = SIDES * SPAN * UNIT
HALF_CHUNK = CHUNK // 2

NORM_EPS = 1e-06
COS_EPS = 1e-06
SIGMA_DATA = 0.5
BETA_ONE = 0.5
BETA_TWO = 0.5
ADAM_EPS = 1e-08
WEIGHT_DECAY = 0.01
LEARN_RATE = 0.04
SCALE_RATE = 1.0
ROOT_HALF = 0.7071067811865476
INV_ROOT_TWO_PI = 0.3989422804014327

F32 = jnp.float32
BF16 = jnp.bfloat16
VMEM_BYTES = 60 * 1024 * 1024

STACK = (("A1", D), ("Q", D), ("K", D), ("V", D), ("O", D), ("A2", D), ("G", FF), ("U", FF), ("F", FF))
ROW_A1, ROW_A2, ROW_Q, ROW_K, ROW_V, ROW_O = (D * place for place in range(6))
ROW_G = 6 * D
ROW_U = ROW_G + FF
ROW_F = ROW_U + FF
ROWS_ALL = ROW_F + FF
HELD_ROWS = dict(
    A1=ROW_A1, A2=ROW_A2, Q=ROW_Q, K=ROW_K, V=ROW_V, O=ROW_O, G=ROW_G, U=ROW_U, F=ROW_F
)
HEAD_ORDER = [
    side * (HEADS // SIDES) + chunk * (SPAN * UNIT // HD) + head
    for chunk in range(D // CHUNK)
    for side in range(SIDES)
    for head in range(SPAN * UNIT // HD)
]


def to_held(by_head):
    per_chunk = SPAN * UNIT // HD
    return by_head.reshape(SIDES, -1, per_chunk).transpose(1, 0, 2).reshape(-1)


def from_held(held):
    per_chunk = SPAN * UNIT // HD
    return held.reshape(-1, SIDES, per_chunk).transpose(1, 0, 2).reshape(-1)


def held_units():
    places = []
    for side in range(SIDES):
        for kind, rows in STACK:
            count = rows // SIDES // UNIT
            for unit in range(count):
                if kind in ("A1", "A2"):
                    place = side * count + unit
                else:
                    place = (unit // SPAN * SIDES + side) * SPAN + unit % SPAN
                places.append(HELD_ROWS[kind] // UNIT + place)
    return np.array(places, np.int32)


def dot_nn(left, right):
    return jnp.dot(left, right, preferred_element_type=F32)


def dot_nt(left, right):
    return lax.dot_general(left, right, (((1,), (1,)), ((), ())), preferred_element_type=F32)


def slots_before(owner_list):
    unit_count = owner_list.shape[0]
    same_owner = owner_list[:, None] == owner_list[None, :]
    row_ids = lax.broadcasted_iota(jnp.int32, (unit_count, unit_count), 0)
    col_ids = lax.broadcasted_iota(jnp.int32, (unit_count, unit_count), 1)
    return jnp.sum(jnp.where(same_owner & (col_ids < row_ids), 1, 0), axis=1).astype(jnp.int32)


def rope_tables(positions):
    quarter = HD // 8
    head_ids = jnp.array(HEAD_ORDER, jnp.int32)[:, None]
    column = lax.broadcasted_iota(jnp.int32, (HEADS, quarter), 1)
    flat_index = (column * HEADS + head_ids).astype(F32)
    low_log = math.log(math.pi)
    high_log = math.log(10.0 * math.pi)
    frequency = jnp.exp(low_log + (high_log - low_log) * flat_index / (HEADS * quarter))
    placed = (2.0 * positions.astype(F32) + 1.0) / SIDE - 1.0
    along_rows = placed[:, 0].reshape(1, 1, -1) * frequency[:, :, None]
    along_cols = placed[:, 1].reshape(1, 1, -1) * frequency[:, :, None]
    angles = jnp.concatenate([along_rows, along_cols], axis=1).reshape(HEADS * 2 * quarter, -1)
    return jnp.cos(angles), jnp.sin(angles)


def deal_matrix(core):
    target = lax.broadcasted_iota(jnp.int32, (CHUNK, CHUNK), 0)
    source = lax.broadcasted_iota(jnp.int32, (CHUNK, CHUNK), 1)
    parity = (target // HALF_CHUNK + core) % 2
    inner = target % HALF_CHUNK
    unit = inner % SPAN
    row = inner // SPAN % 2
    piece = inner // (2 * SPAN) % (UNIT // 4)
    side = inner // (2 * SPAN * (UNIT // 4))
    return (source == (side * SPAN + unit) * UNIT + 4 * piece + 2 * parity + row).astype(BF16)


def layer_kernel(
    images,
    slots_refs,
    place_ref,
    ends_ref,
    scal_ref,
    x_ref,
    cot_ref,
    gb_ref,
    cond_ref,
    cos_ref,
    sin_ref,
    deal_ref,
    outs_hbm,
    early_keep,
    early_send,
    late_keep,
    late_send,
    n2_hbm,
    mids_hbm,
    note_hbm,
    w,
    unit_s,
    coef_s,
    qtok_s,
    p_s,
    qk_s,
    v_s,
    o_s,
    x2_s,
    n1_s,
    n2_s,
    ga_s,
    do_s,
    dot_s,
    ff_s,
    dn2_s,
    dqkv_s,
    early_s,
    late_s,
    outs_s,
    note_s,
    ds_s,
    note_low,
    w_sem,
    o_sem,
):
    toks = images * SEQ
    sends = []

    def send(src, dst):
        copy = pltpu.make_async_copy(src, dst, o_sem.at[len(sends)])
        copy.start()
        sends.append(copy)

    groups = (0, ROW_Q, ROW_O, ROW_G, ROWS_ALL)

    def fetch(low, high):
        first = 0
        for array, slots_ref in enumerate(slots_refs):

            @pl.loop(ends_ref[array, low // 3], ends_ref[array, low // 3 + 1])
            def _(index, slots_ref=slots_ref, first=first):
                unit = place_ref[0, first + index]
                group = jnp.int32(low)
                for bound in groups[low + 1 : high]:
                    group += jnp.where(unit >= bound // UNIT, 1, 0)
                pltpu.make_async_copy(
                    slots_ref.at[place_ref[1, first + index]],
                    w.at[pl.ds(pl.multiple_of(unit * UNIT, UNIT), UNIT)],
                    w_sem.at[group],
                ).start()

            first += slots_ref.shape[0]

    fetch(0, 3)

    def weights_here(index):
        low, high = groups[index : index + 2]
        region = w.at[pl.ds(low, high - low)]
        pltpu.make_async_copy(region, region, w_sem.at[index]).wait()

    def image_rows(image):
        return pl.ds(image * SEQ, SEQ)

    note_s[...] = jnp.zeros_like(note_s)
    note_s[:images] = cond_ref[:images].astype(F32)

    def note(place, row):
        high = row.astype(BF16).astype(F32)
        lanes = slice(0, row.shape[1])
        note_s[place : place + 1, lanes] = high
        note_s[place + 2 * images + 1 : place + 2 * images + 2, lanes] = row - high

    fetch(3, 4)
    weights_here(0)
    gain_one = 1.0 + dot_nn(cond_ref[...], w[ROW_A1 : ROW_A1 + D])
    gain_two = 1.0 + dot_nn(cond_ref[...], w[ROW_A2 : ROW_A2 + D])
    for image in range(images):
        x = x_ref[image_rows(image)]
        inverse = lax.rsqrt(jnp.mean(x * x, axis=-1, keepdims=True) + NORM_EPS)
        n1_s[image_rows(image)] = (x * inverse * gain_one[image : image + 1]).astype(BF16)
    send(n1_s, mids_hbm.at[1])
    weights_here(1)
    unit_s[:D] = dot_nt(w[ROW_Q : ROW_Q + D], n1_s[...])
    unit_s[D:] = dot_nt(w[ROW_K : ROW_K + D], n1_s[...])
    v_s[...] = dot_nt(w[ROW_V : ROW_V + D], n1_s[...]).astype(BF16)

    @pl.loop(0, 2 * HEADS)
    def _(index):
        head = lax.rem(index, HEADS)
        rows = pl.ds(pl.multiple_of(index * HD, HD), HD)
        angle_rows = pl.ds(pl.multiple_of(head * 16, 16), 16)
        raw = unit_s[rows]
        inverse = lax.rsqrt(jnp.sum(raw * raw, axis=0, keepdims=True) + COS_EPS)
        unit = raw * inverse
        root = scal_ref[HEADS + head]
        unit_s[rows] = unit
        coef_s[pl.ds(index, 1)] = root * inverse
        scaled = unit * root
        first, second = scaled[:16], scaled[16:32]
        cosine, sine = cos_ref[angle_rows], sin_ref[angle_rows]
        turned = jnp.concatenate(
            [first * cosine - second * sine, second * cosine + first * sine, scaled[32:]], axis=0
        )
        qk_s[rows] = turned.astype(BF16)

    qtok_s[...] = qk_s[:D].T

    def head_rows(head):
        return pl.ds(pl.multiple_of(head * HD, HD), HD)

    def pair_lanes(pair):
        return pl.ds(pl.multiple_of(pair * 2 * HD, 2 * HD), 2 * HD)

    @pl.loop(0, HEADS // 2, unroll=2)
    def _(pair):
        for image in range(images):
            cols = image_rows(image)
            query = qtok_s[cols, pair_lanes(pair)]
            mixed = []
            for half in range(2):
                head = pair * 2 + half
                scores = dot_nn(
                    query[:, half * HD : (half + 1) * HD], qk_s[head_rows(HEADS + head), cols]
                )
                exp_scores = jnp.exp(scores - scal_ref[head])
                inverse = 1.0 / jnp.sum(exp_scores, axis=-1, keepdims=True)
                probs = (exp_scores * inverse).astype(BF16)
                p_s[head, cols] = probs
                mixed.append(dot_nt(probs, v_s[head_rows(head), cols]))
            o_s[cols, pair_lanes(pair)] = jnp.concatenate(mixed, axis=1)

    weights_here(2)
    x2_s[...] = x_ref[...] + dot_nn(o_s[...].astype(BF16), w[ROW_O : ROW_O + D])
    for image in range(images):
        x2 = x2_s[image_rows(image)]
        inverse = lax.rsqrt(jnp.mean(x2 * x2, axis=-1, keepdims=True) + NORM_EPS)
        n2_s[image_rows(image)] = (x2 * inverse * gain_two[image : image + 1]).astype(BF16)
    send(n2_s, n2_hbm)

    weights_here(3)
    chunks = FF // CHUNK
    width = D

    def deal(field, store, place):
        dealt = dot_nt(deal_ref[...], field).astype(BF16)
        store[0, place] = dealt[:HALF_CHUNK]
        store[1, place] = dealt[HALF_CHUNK:]

    for start in range(0, FF, width):

        def part(base):
            return w[base + start : base + start + width]

        gate = dot_nt(n2_s[...], part(ROW_G))
        up = dot_nt(n2_s[...], part(ROW_U))
        grad_hidden = dot_nt(gb_ref[...], part(ROW_F))
        phi_sum = 0.5 * (1.0 + lax.erf(gate * ROOT_HALF))
        density = INV_ROOT_TWO_PI * jnp.exp(-0.5 * gate * gate)
        gelu = gate * phi_sum
        hidden = (gelu * up).astype(BF16)
        grad_gate = (grad_hidden * up * (phi_sum + gate * density)).astype(BF16)
        grad_up = (grad_hidden * gelu).astype(BF16)
        ff = dot_nn(hidden, part(ROW_F))
        dn2 = dot_nn(grad_gate, part(ROW_G)) + dot_nn(grad_up, part(ROW_U))
        if start == 0:
            ff_s[...] = ff
            dn2_s[...] = dn2
        else:
            ff_s[...] += ff
            dn2_s[...] += dn2
        for at in range(0, width, CHUNK):
            place = (start + at) // CHUNK
            deal(hidden[:, at : at + CHUNK], early_s, place)
            deal(grad_gate[:, at : at + CHUNK], early_s, chunks + place)
            deal(grad_up[:, at : at + CHUNK], late_s, place)

    send(early_s.at[0], early_keep)
    send(early_s.at[1], early_send)
    outs_s[0] = (x2_s[...] + ff_s[...]).astype(BF16)
    send(outs_s.at[0], outs_hbm.at[0])

    def norm_back(x, gain, grad_normed):
        inverse = lax.rsqrt(jnp.mean(x * x, axis=-1, keepdims=True) + NORM_EPS)
        scaled = grad_normed * gain
        inner = jnp.mean(x * scaled, axis=-1, keepdims=True)
        grad_x = inverse * scaled - x * (inverse * inverse * inverse * inner)
        return grad_x, jnp.sum(grad_normed * x * inverse, axis=0, keepdims=True)

    for image in range(images):
        rows = image_rows(image)
        grad_x, grad_gain = norm_back(x2_s[rows], gain_two[image : image + 1], dn2_s[rows])
        grad = cot_ref[rows].astype(F32) * scal_ref[2 * HEADS + image] + grad_x
        x2_s[rows] = grad
        ga_s[rows] = grad.astype(BF16)
        note(2 * images + image, grad_gain)
    send(ga_s, mids_hbm.at[0])

    do_s[...] = dot_nt(ga_s[...], w[ROW_O : ROW_O + D]).astype(BF16)
    dot_s[...] = dot_nt(w[ROW_O : ROW_O + D], ga_s[...]).astype(BF16)
    ds_s[...] = jnp.zeros_like(ds_s)

    @pl.loop(0, HEADS // 2, unroll=3)
    def _(pair):
        for image in range(images):
            cols = image_rows(image)
            grads_mixed = do_s[cols, pair_lanes(pair)]
            inners = grads_mixed.astype(F32) * o_s[cols, pair_lanes(pair)]
            for half in range(2):
                head = pair * 2 + half
                lanes = slice(half * HD, (half + 1) * HD)
                rows, key_rows = head_rows(head), head_rows(HEADS + head)
                key, value = qk_s[key_rows, cols], v_s[rows, cols]
                probs = p_s[head, cols]
                grad_probs = dot_nn(grads_mixed[:, lanes], value)
                inner = jnp.sum(inners[:, lanes], axis=-1, keepdims=True)
                grad_scores = (probs.astype(F32) * (grad_probs - inner)).astype(BF16)
                grad_query = dot_nt(key, grad_scores)
                grad_key = dot_nn(qk_s[rows, cols], grad_scores)
                grad_value = dot_nn(dot_s[rows, cols], probs)
                angle_rows = pl.ds(pl.multiple_of(head * 16, 16), 16)
                cosine, sine = cos_ref[angle_rows, cols], sin_ref[angle_rows, cols]
                along = jnp.zeros((1, SEQ), F32)
                for grad, own_rows, place in (
                    (grad_query, rows, head),
                    (grad_key, key_rows, HEADS + head),
                ):
                    first, second = grad[:16], grad[16:32]
                    back = jnp.concatenate(
                        [
                            first * cosine + second * sine,
                            second * cosine - first * sine,
                            grad[32:],
                        ],
                        axis=0,
                    )
                    unit = unit_s[own_rows, cols]
                    inner_unit = jnp.sum(unit * back, axis=0, keepdims=True)
                    along += inner_unit
                    dqkv_s[own_rows, cols] = (
                        coef_s[pl.ds(place, 1), cols] * (back - unit * inner_unit)
                    ).astype(BF16)
                value_rows = head_rows(2 * HEADS + head)
                dqkv_s[value_rows, cols] = grad_value.astype(BF16)
                ds_s[pl.ds(head, 1)] += along

    per_kind = D // CHUNK
    for place in range(per_kind):
        deal(o_s[:, place * CHUNK : (place + 1) * CHUNK].astype(BF16), late_s, chunks + place)
    for place in range(3 * per_kind):
        dealt = dot_nn(deal_ref[...], dqkv_s[place * CHUNK : (place + 1) * CHUNK]).astype(BF16)
        late_s[0, chunks + per_kind + place] = dealt[:HALF_CHUNK]
        late_s[1, chunks + per_kind + place] = dealt[HALF_CHUNK:]
    send(late_s.at[0], late_keep)
    send(late_s.at[1], late_send)
    dn1 = dot_nn(dqkv_s[:D].T, w[ROW_Q : ROW_Q + D])
    dn1 += dot_nn(dqkv_s[D : 2 * D].T, w[ROW_K : ROW_K + D])
    dn1 += dot_nn(dqkv_s[2 * D :].T, w[ROW_V : ROW_V + D])
    dn2_s[...] = dn1
    for image in range(images):
        rows = image_rows(image)
        grad_x, grad_gain = norm_back(x_ref[rows], gain_one[image : image + 1], dn2_s[rows])
        outs_s[1, rows] = (x2_s[rows] + grad_x).astype(BF16)
        note(images + image, grad_gain)
    send(outs_s.at[1], outs_hbm.at[1])
    ones = jnp.ones((8, SEQ), F32)
    scale_row = lax.dot_general(
        ones,
        ds_s[...],
        (((1,), (1,)), ((), ())),
        precision=lax.Precision.HIGHEST,
        preferred_element_type=F32,
    )
    note(3 * images, scale_row[:1])
    note_low[...] = note_s[...].astype(BF16)
    send(note_low, note_hbm)
    for copy in sends:
        copy.wait()


def run_layer(images, places, ends, scalars, x, cotangent, grad_out, cond, cosine, sine, deal, slots):
    toks = images * SEQ
    chunks = FF // CHUNK
    any_spec = pl.BlockSpec(memory_space=pl.ANY)
    vmem = pl.BlockSpec(memory_space=pltpu.VMEM)
    smem = pl.BlockSpec(memory_space=pltpu.SMEM)
    field = jax.ShapeDtypeStruct((toks, D), BF16)

    def dealt(count):
        return jax.ShapeDtypeStruct((count, HALF_CHUNK, toks), BF16)

    pair = jax.ShapeDtypeStruct((2, toks, D), BF16)
    late = chunks + 4 * D // CHUNK
    outs = [pair, dealt(2 * chunks), dealt(2 * chunks), dealt(late), dealt(late), field, pair]
    outs += [jax.ShapeDtypeStruct((16, D), BF16)]
    wide = pltpu.VMEM((toks, D), F32)
    low = pltpu.VMEM((toks, D), BF16)
    scratch = [
        pltpu.VMEM((ROWS_ALL, D), BF16),
        pltpu.VMEM((2 * D, toks), F32),
        pltpu.VMEM((2 * HEADS, toks), F32),
        low,
        pltpu.VMEM((HEADS, toks, SEQ), BF16),
        pltpu.VMEM((2 * D, toks), BF16),
        pltpu.VMEM((D, toks), BF16),
        wide,
        wide,
        low,
        low,
        low,
        low,
        pltpu.VMEM((D, toks), BF16),
        wide,
        wide,
        pltpu.VMEM((3 * D, toks), BF16),
        pltpu.VMEM((2, 2 * chunks, HALF_CHUNK, toks), BF16),
        pltpu.VMEM((2, late, HALF_CHUNK, toks), BF16),
        pltpu.VMEM((2, toks, D), BF16),
        pltpu.VMEM((16, D), F32),
        pltpu.VMEM((16, SEQ), F32),
        pltpu.VMEM((16, D), BF16),
        pltpu.SemaphoreType.DMA((4,)),
        pltpu.SemaphoreType.DMA((16,)),
    ]

    operands = [places, ends, scalars, x, cotangent, grad_out, cond, cosine, sine, deal]
    here = len(operands)

    def body(*refs):
        layer_kernel(
            images, refs[here : here + len(slots)], *refs[:here], *refs[here + len(slots) :]
        )

    return pl.pallas_call(
        body,
        out_shape=outs,
        in_specs=[smem] * 3 + [vmem] * 7 + [any_spec] * len(slots),
        out_specs=[any_spec] * len(outs),
        scratch_shapes=scratch,
        compiler_params=pltpu.CompilerParams(vmem_limit_bytes=VMEM_BYTES),
        cost_estimate=pl.CostEstimate(
            flops=2 * 3 * ROWS_ALL * D * toks, bytes_accessed=ROWS_ALL * D * 4, transcendentals=0
        ),
        name="layer",
    )(*operands, *slots)


def weight_grads(lefts, rights, kinds, first=0, here=3):
    rows, toks = lefts[0].shape[1:]
    pieces = rows // (SIDES * 2 * SPAN)
    total = sum(count for count, _ in kinds)
    steps = total // here
    step_rights = [place for count, place in kinds for _ in range(count // here)]
    operands, specs = list(lefts), []
    for left in lefts:
        specs.append(pl.BlockSpec((here, rows, toks), lambda step: (first // here + step, 0, 0)))
    for parts in rights:
        for part in parts:
            field, at = part if isinstance(part, tuple) else (part[None], 0)
            operands.append(field)
            specs.append(pl.BlockSpec((None, toks, D), lambda step, at=at: (at, 0, 0)))

    def body(*refs):
        out_ref, count = refs[-1], len(lefts)
        step = pl.program_id(0)
        for place in range(len(rights)):
            own = refs[count * (place + 1) : count * (place + 2)]
            mine = [index for index, right in enumerate(step_rights) if right == place]

            @pl.when((step >= mine[0]) & (step <= mine[-1]))
            def _(own=own):
                summed = dot_nn(refs[0][...].reshape(here * rows, toks), own[0][...])
                for left, right in zip(refs[1:count], own[1:]):
                    summed += dot_nn(left[...].reshape(here * rows, toks), right[...])
                for chunk in range(here):
                    out_ref[:, :, chunk] = (
                        summed[chunk * rows : (chunk + 1) * rows]
                        .reshape(SIDES, pieces, 2 * SPAN, D)
                        .astype(BF16)
                    )

    return pl.pallas_call(
        body,
        out_shape=jax.ShapeDtypeStruct((SIDES, pieces, total, 2 * SPAN, D), BF16),
        grid=(steps,),
        in_specs=specs,
        out_specs=pl.BlockSpec(
            (SIDES, pieces, here, 2 * SPAN, D), lambda step: (0, 0, step, 0, 0)
        ),
        compiler_params=pltpu.CompilerParams(vmem_limit_bytes=VMEM_BYTES),
        cost_estimate=pl.CostEstimate(
            flops=2 * len(lefts) * total * rows * toks * D,
            bytes_accessed=2 * len(lefts) * (total * rows + len(rights) * D) * toks
            + 2 * total * rows * D,
            transcendentals=0,
        ),
        name="weight_grads",
    )(*operands)


def adam_step(weights, first_new, second_new, rate):
    fix_one = 1.0 - math.pow(BETA_ONE, STEP)
    fix_two = 1.0 - math.pow(BETA_TWO, STEP)
    return weights * (1.0 - rate * WEIGHT_DECAY) - rate * (first_new / fix_one) / (
        jnp.sqrt(second_new / fix_two) + ADAM_EPS
    )


def moments(first, second, grad):
    return (
        BETA_ONE * first + (1.0 - BETA_ONE) * grad,
        BETA_TWO * second + (1.0 - BETA_TWO) * grad * grad,
    )


def pack(fields):
    def body(*refs):
        for place, ref in enumerate(refs[:-1]):
            refs[-1][place] = ref[...]

    return pl.pallas_call(
        body,
        out_shape=jax.ShapeDtypeStruct((len(fields), *fields[0].shape), fields[0].dtype),
        name="pack",
    )(*fields)


def factor_sums(notes, indices, images, mp_count):
    rows_wanted = 2 * (D // mp_count // UNIT)
    pieces = 2 * images + 1

    def body(*refs):
        index_ref, sums_ref, scale_ref = refs[-3:]
        rows = jnp.concatenate([ref[...].reshape(-1, D) for ref in refs[:-3]])
        row = lax.broadcasted_iota(jnp.int32, (rows_wanted, D), 0)
        feature = lax.broadcasted_iota(jnp.int32, (rows_wanted, D), 1)
        unit = row // (2 * SPAN) * SPAN + row % SPAN
        wanted = (index_ref[0] * (rows_wanted // 2) + unit) * UNIT
        wanted += 2 * index_ref[1] + row // SPAN % 2
        features = (feature == wanted).astype(BF16)
        count = rows.shape[0]
        source = lax.broadcasted_iota(jnp.int32, (count, count), 0)
        target = lax.broadcasted_iota(jnp.int32, (count, count), 1)
        ahead = target - source
        is_cond = source % 16 < images
        cond_rows = dot_nt(features, rows).astype(BF16)
        for place in range(2):
            first = images * (1 + place)
            pick_rows = is_cond & ((ahead == first) | (ahead == first + pieces))
            chosen = dot_nn(cond_rows, pick_rows.astype(BF16)).astype(BF16)
            sums_ref[place] = dot_nn(chosen, rows)
        column = lax.broadcasted_iota(jnp.int32, (8, count), 1) % 16
        last = (column == 3 * images) | (column == 3 * images + pieces)
        scale_ref[...] = dot_nn(last.astype(BF16), rows)

    return pl.pallas_call(
        body,
        out_shape=[
            jax.ShapeDtypeStruct((2, rows_wanted, D), F32),
            jax.ShapeDtypeStruct((8, D), F32),
        ],
        in_specs=[pl.BlockSpec(memory_space=pltpu.VMEM)] * len(notes)
        + [pl.BlockSpec(memory_space=pltpu.SMEM)],
        compiler_params=pltpu.CompilerParams(vmem_limit_bytes=VMEM_BYTES),
        name="factor_sums",
    )(*notes, indices)


def route(sum_a, sum_fg, sum_rest, placed, slots, dp_count):
    chunks, few = FF // CHUNK, D // CHUNK
    rows = 2 * placed.shape[1]
    to_row = np.arange(dp_count * 2 * slots)
    columns = np.stack([to_row // (2 * slots) * slots + to_row % slots, to_row // slots % 2], axis=1)
    placed_rows = jnp.broadcast_to(placed.reshape(-1, 1, SPAN), (rows // (2 * SPAN), 2, SPAN))

    def body(a_ref, fg_one, fg_two, rest_one, rest_two, placed_ref, columns_ref, *outs):
        pieces_ref, out_ref = outs
        fg_ref = fg_one[...] + fg_two[...].astype(F32)
        rest_ref = rest_one[...] + rest_two[...].astype(F32)
        start = 0
        for field in (
            a_ref[0],
            rest_ref[chunks + few :],
            rest_ref[chunks : chunks + few],
            a_ref[1],
            fg_ref[chunks:],
            rest_ref[:chunks],
            fg_ref[:chunks],
        ):
            field = field.reshape(-1, D)
            pieces_ref[start : start + field.shape[0]] = field
            start += field.shape[0]
        row = lax.broadcasted_iota(jnp.int32, (1, rows), 1) // SPAN % 2
        chosen = (columns_ref[:, :1] == placed_ref[...]) & (columns_ref[:, 1:] == row)
        out_ref[...] = dot_nn(chosen.astype(BF16), pieces_ref[...].astype(BF16)).astype(BF16)

    return pl.pallas_call(
        body,
        out_shape=[
            jax.ShapeDtypeStruct((rows, D), F32),
            jax.ShapeDtypeStruct((dp_count * 2 * slots, D), BF16),
        ],
        compiler_params=pltpu.CompilerParams(vmem_limit_bytes=VMEM_BYTES),
        name="route",
    )(sum_a, *sum_fg, *sum_rest, placed_rows.reshape(1, rows), jnp.array(columns, jnp.int32))


def add(*terms):
    total = terms[0].astype(F32)
    for term in terms[1:]:
        total = total + term.astype(F32)
    return total


class Ring:
    def __init__(self, dp_count):
        self.count = dp_count // 2
        pairs = []
        for place in range(self.count):
            for core in range(2):
                pairs.append(
                    (self.chip(place) * 2 + core, self.chip((place + 1) % self.count) * 2 + core)
                )
        self.onward = pairs
        self.backward = [(b, a) for a, b in pairs]
        self.twins = [(index, index ^ 1) for index in range(dp_count)]

    def chip(self, place):
        column = self.count // 2
        return 2 * place if place < column else 2 * (self.count - 1 - place) + 1

    def here(self):
        chip = lax.axis_index("dp") // 2
        return jnp.where(chip % 2 == 0, chip // 2, self.count - 1 - chip // 2)

    def chip_at(self, offset):
        place = (self.here() + offset + self.count) % self.count
        column = self.count // 2
        return jnp.where(place < column, 2 * place, 2 * (self.count - 1 - place) + 1)

    def on(self, field):
        return lax.ppermute(field, "dp", self.onward)

    def back(self, field):
        return lax.ppermute(field, "dp", self.backward)

    def twin(self, field):
        return lax.ppermute(field, "dp", self.twins)


def after(field, *others):
    return lax.optimization_barrier((field, others))[0]


def swap_mp(field):
    return lax.ppermute(field, "mp", [(0, 1), (1, 0)])


class Labels:
    def __init__(self, rows):
        self.rows = list(rows)

    def __getitem__(self, cut):
        return Labels(self.rows[cut])

    def moved(self, hop, mp, core):
        return Labels((h + hop, m ^ mp, c ^ core, slot) for h, m, c, slot in self.rows)


class LabelMoves:
    def on(self, field):
        return field.moved(-1, 0, 0)

    def back(self, field):
        return field.moved(1, 0, 0)

    def swap(self, field):
        return field.moved(0, 1, 0)

    def twin(self, field):
        return field.moved(0, 0, 1)

    def cat(self, *fields):
        return Labels(row for field in fields for row in field.rows)

    def together(self, *fields):
        return fields


class Moves:
    def __init__(self, ring):
        self.on, self.back, self.twin, self.swap = ring.on, ring.back, ring.twin, swap_mp

    def cat(self, *fields):
        return jnp.concatenate(fields)

    def together(self, *fields):
        return lax.optimization_barrier(fields)


def gather_slots(moves, own, slots, early=(), use_early=None, late=(), use_late=None):
    cat, on, back, swap, twin = moves.cat, moves.on, moves.back, moves.swap, moves.twin
    cut = slots // 2
    rest = slots - cut
    first, second = own[:cut], own[cut:]
    hop = [on(second), back(second), swap(first), twin(own)]
    f0, b0, y0, c0, second, *early = moves.together(*hop, second, *early)
    wide = cat(first, y0)
    hop = [on(wide), back(wide), swap(second), twin(cat(y0, f0, b0))]
    f1, b1, y1, c1, f0, b0, *late = moves.together(*hop, f0, b0, *late)
    hop = [on(cat(f0, f1)), back(cat(b0, b1)), swap(cat(f0, b0)), twin(cat(f1, b1, y1))]
    done = (*use_early(*early), *use_late(*late)) if early else ()
    f2, b2, y2, c2, *done = moves.together(*hop, *done)
    crossing = cat(f2[:rest], b2[:rest])
    hop = [on(f2), back(b2), swap(crossing), twin(cat(f2, b2, y2))]
    f3, b3, y3, c3 = moves.together(*hop)
    half = (slots + cut) // 2
    crossing = cat(f3[:rest], b3[:rest])
    hop = [on(f3[:half]), back(b3[half:]), swap(crossing), twin(cat(f3, b3, y3))]
    f4, b4, y4, c4 = moves.together(*hop)
    y5 = swap(cat(f4[:rest], b4[: max(0, rest - half)]))
    c5 = [twin(f4), twin(b4), twin(y4)]
    return [own, f0, b0, y0, c0, f1, b1, y1, c1, f2, b2, y2, c2, f3, b3, y3, c3, f4, b4, y4, c4, y5] + c5 + [twin(y5)], done


def both_halves(own, other, half, axis=0):
    return jnp.where(
        half == 0,
        jnp.concatenate([own, other], axis=axis),
        jnp.concatenate([other, own], axis=axis),
    )


def pick(field, *places):
    for place in places:
        field = lax.dynamic_index_in_dim(field, place, 0, keepdims=False)
    return field


def far_packets(field, chip, note):
    sides, _, chunks, rows, cols = field.shape
    dims = (chunks + note.shape[0], rows, cols)

    def body(_, own, note_ref, *outs):
        for way, out in enumerate(outs):
            out[:chunks] = own[way]
            out[chunks:] = note_ref[...]

    def whole(shape):
        return pl.BlockSpec(shape, lambda _, chip: (0,) * len(shape))

    return pl.pallas_call(
        body,
        grid_spec=pltpu.PrefetchScalarGridSpec(
            num_scalar_prefetch=1,
            grid=(1,),
            in_specs=[
                pl.BlockSpec(
                    (sides, None, chunks, rows, cols), lambda _, chip: (0, chip[0], 0, 0, 0)
                ),
                whole(note.shape),
            ],
            out_specs=[whole(dims)] * 2,
        ),
        out_shape=[jax.ShapeDtypeStruct(dims, BF16)] * 2,
        compiler_params=pltpu.CompilerParams(vmem_limit_bytes=VMEM_BYTES),
        name="far_packets",
    )(chip, field, note)


class RingSum:
    def __init__(self, ring, field, half, note=None):
        self.ring, self.field, self.half = ring, field, half
        self.distance = ring.count // 2
        self.on = self.back = None
        self.own = self.note_on = self.note_back = note
        self.seen = []

    def block(self, offset):
        return lax.dynamic_index_in_dim(self.field, self.ring.chip_at(offset), 1, keepdims=False)

    def step(self, *others):
        ring, far, distance = self.ring, self.ring.count // 2, self.distance
        chunks = self.field.shape[2]
        if distance == far:
            block = self.block(far)
            on, back = block[0], block[1]
        else:
            on, back = self.block(distance), self.block(-distance)
            if distance == far - 1:
                on = jnp.stack([add(on[0], self.on).astype(BF16), on[1]])
                back = jnp.stack([back[0], add(back[1], self.back).astype(BF16)])
            else:
                on, back = add(on, self.on).astype(BF16), add(back, self.back).astype(BF16)
        if self.own is not None and distance == far:
            on, back = far_packets(self.field, ring.chip_at(far).reshape(1), self.own)
        elif self.own is not None:
            axis = on.ndim - 3
            shape = on.shape[:axis] + (2 // (axis + 1),) + on.shape[axis + 1 :]
            on = jnp.concatenate([on, self.note_on.reshape(shape)], axis=axis)
            back = jnp.concatenate([back, self.note_back.reshape(shape)], axis=axis)
        if others:
            on, back = after(on, *others), after(back, *others)
        on, back = lax.optimization_barrier((ring.on(on), ring.back(back)))
        if self.own is not None:
            self.note_on = on[..., chunks:, :, :].reshape(self.own.shape)
            self.note_back = back[..., chunks:, :, :].reshape(self.own.shape)
            self.seen += [self.note_on, self.note_back]
            on, back = on[..., :chunks, :, :], back[..., :chunks, :, :]
        self.on, self.back = on, back
        self.distance -= 1
        return self.on, self.back

    def total(self):
        total = add(self.block(0), self.on, self.back)
        other = swap_mp(pick(total.astype(BF16), 1 - self.half))
        return pick(total, self.half), other

    def notes(self):
        return [self.own] + self.seen[:-1]


def on_device(
    tokens,
    conditioning,
    sigmas,
    positions,
    cotangent,
    owners,
    master,
    moment_one,
    moment_two,
    scale_state,
):
    dp_count = lax.axis_size("dp")
    mp_count = lax.axis_size("mp")
    dp_index = lax.axis_index("dp")
    mp_index = lax.axis_index("mp")
    images = conditioning.shape[0] // mp_count
    toks = images * SEQ
    slots = master.shape[1]
    unit_rows = master.shape[2]
    unit_count = owners.shape[1]
    heads_here = scale_state.shape[1]
    paired = dp_count * 2 == UNIT
    core = dp_index % 2 if paired else 0

    def mine(field, rows):
        return lax.dynamic_slice_in_dim(field, mp_index * rows, rows, 0)

    rounded = master[0].astype(BF16)
    halves_here = jnp.concatenate([owners[0].astype(F32), scale_state[0]])[None]
    ring = Ring(dp_count) if paired else None
    if paired:
        own_labels = Labels((0, 0, 0, slot) for slot in range(slots))
        arrays, _ = gather_slots(LabelMoves(), own_labels, slots)
        labels = [row for field in arrays for row in field.rows]
        sizes = [len(field.rows) for field in arrays]
        assert len(set((h % ring.count, m, c, slot) for h, m, c, slot in labels)) == len(labels)
        hops, sides, cores, numbers = (jnp.array(column, jnp.int32) for column in zip(*labels))
        owner = ring.chip_at(hops) * 2 + (dp_index % 2 + cores) % 2
        side = (mp_index + sides) % 2
        slot_ids = (side * dp_count + owner) * slots + numbers
    else:
        sizes = [mp_count * dp_count * slots]
        slot_ids = lax.broadcasted_iota(jnp.int32, (mp_count * dp_count * slots, 1), 0)[:, 0]

    def prepare_places(halves_other):
        halves_all = both_halves(halves_here, halves_other, mp_index)
        owners_all = halves_all[:, :unit_count].astype(jnp.int32)
        before = jnp.stack([slots_before(owners_all[half]) for half in range(mp_count)])
        half_ids = lax.broadcasted_iota(jnp.int32, owners_all.shape, 0)
        unit_slots = ((half_ids * dp_count + owners_all) * slots + before).reshape(-1)
        belongs = jnp.array(held_units())
        match = slot_ids[:, None] == unit_slots[None, :]
        places = jnp.where(
            jnp.any(match, axis=1),
            jnp.sum(jnp.where(match, belongs[None, :], 0), axis=1),
            belongs.shape[0],
        )
        starts = np.cumsum([0] + sizes)
        array_ids = jnp.array(np.repeat(np.arange(len(sizes)), sizes), jnp.int32)
        slot_numbers = jnp.array(np.concatenate([np.arange(size) for size in sizes]), jnp.int32)
        key = places * starts[-1] + slot_numbers
        ahead = (array_ids[:, None] == array_ids[None, :]) & (key[None, :] < key[:, None])
        rank = jnp.sum(jnp.where(ahead, 1, 0), axis=1) + jnp.array(np.repeat(starts[:-1], sizes), jnp.int32)
        at_rank = rank[None, :] == lax.broadcasted_iota(jnp.int32, (starts[-1],) * 2, 0)
        sorted_places = jnp.stack(
            [
                jnp.sum(jnp.where(at_rank, field[None, :], 0), axis=1)
                for field in (places, slot_numbers)
            ]
        )
        own_array = array_ids[None, :] == lax.broadcasted_iota(
            jnp.int32, (len(sizes), array_ids.shape[0]), 0
        )
        ends = jnp.stack(
            [
                jnp.sum(jnp.where(own_array & (places < bound // UNIT)[None, :], 1, 0), axis=1)
                for bound in (0, ROW_G, ROWS_ALL)
            ],
            axis=1,
        )
        return sorted_places, ends

    def prepare_fields(halves_other, tokens, conditioning, sigmas, positions, cotangent):
        halves_all = both_halves(halves_here, halves_other, mp_index)
        scales_all = halves_all[:, unit_count:].reshape(-1)
        scales_held = to_held(scales_all)
        square = sigmas * sigmas
        data_square = SIGMA_DATA * SIGMA_DATA
        loss_weight = 4.0 * square * data_square / ((square + data_square) * (square + data_square))
        scalars = jnp.concatenate([scales_held, jnp.sqrt(scales_held), mine(loss_weight, images)])
        cosine, sine = rope_tables(mine(positions, images))
        cond = jnp.pad(mine(conditioning, images).astype(BF16), ((0, 16 - images), (0, 0)))

        grad_out = (
            mine(cotangent, toks).astype(F32).reshape(images, SEQ, D)
            * mine(loss_weight, images)[:, None, None]
        ).astype(BF16).reshape(toks, D)
        return (
            scalars,
            scales_all,
            cosine,
            sine,
            cond,
            grad_out,
            deal_matrix(core),
            mine(tokens, toks),
            mine(cotangent, toks),
        )

    halves_other = swap_mp(halves_here)
    if paired:
        gathered, prepared = gather_slots(
            Moves(ring),
            rounded,
            slots,
            (halves_other,),
            prepare_places,
            (halves_other, tokens, conditioning, sigmas, positions, cotangent),
            prepare_fields,
        )
    else:
        gathered = [lax.all_gather(rounded, ("mp", "dp"), axis=0, tiled=True)]
        prepared = prepare_places(halves_other)
        prepared += prepare_fields(
            halves_other, tokens, conditioning, sigmas, positions, cotangent
        )
    places, ends, scalars, scales_all, cosine, sine, cond = prepared[:7]
    grad_out, deal, x_own, cot_own = prepared[7:]
    (
        outs_low,
        early_keep,
        early_send,
        late_keep,
        late_send,
        normed_two,
        mids,
        note,
    ) = run_layer(
        images, places, ends, scalars, x_own, cot_own, grad_out, cond, cosine, sine, deal, gathered
    )
    outs_other = swap_mp(outs_low)
    chunks, few = FF // CHUNK, D // CHUNK

    note = note.reshape(2, 8, D)

    def scale_grads(scale_row):
        scale_sum = from_held(scale_row[:HEADS]) / (2.0 * jnp.sqrt(scales_all))
        return lax.dynamic_slice_in_dim(scale_sum, mp_index * heads_here, heads_here, 0)

    if paired:
        out_both = (grad_out, ring.twin(grad_out))
        early_both = (early_keep, ring.twin(early_send))
        two_both = (normed_two, ring.twin(normed_two))
        late_send, mids_send = lax.optimization_barrier(
            (late_send, mids, early_both[1], two_both[1], out_both[1])
        )[:2]
        late_twin, mids_twin = ring.twin(late_send), ring.twin(mids_send)
        grad_fg = weight_grads(
            early_both, (out_both, two_both), ((chunks, 0), (chunks, 1)), here=chunks
        )
        sum_fg = RingSum(ring, grad_fg, mp_index, note)
        hop = sum_fg.step(late_twin, mids_twin)
        grad_rest = weight_grads(
            (after(late_keep, grad_fg), late_twin),
            (two_both, ((mids, 0), (mids_twin, 0)), ((mids, 1), (mids_twin, 1))),
            ((chunks, 0), (few, 1), (3 * few, 2)),
        )
        sum_rest = RingSum(ring, grad_rest, mp_index)
        late_owners = after(owners, grad_fg)[0]
        placed = (late_owners * slots + slots_before(late_owners))[None]
        hop = sum_fg.step(grad_rest)
        sum_rest.step()
        sum_fg.step()
        sum_rest.step()
        sum_fg.step()
        hop = sum_rest.step(outs_other)
        outs_other = after(outs_other, hop)
        notes = pack(sum_fg.notes())
        sum_fg = sum_fg.total()
        notes = [notes, swap_mp(notes)]
        sum_rest.step()
        notes += [ring.twin(note) for note in notes]
        sum_rest = sum_rest.total()
        indices = jnp.stack([mp_index, dp_index]).astype(jnp.int32)
        sum_a, scale_rows = factor_sums(notes, indices, images, mp_count)
        scale_row = scale_rows[0]
        by_kind, outgoing = route(sum_a, sum_fg, sum_rest, placed, slots, dp_count)
        grad_shards = (
            by_kind.reshape(-1, 2, SPAN, D).transpose(0, 2, 1, 3).reshape(unit_count, 2 * D)
        )
        owned = lax.all_to_all(outgoing, "dp", split_axis=0, concat_axis=0, tiled=True)
        owned = owned.reshape(dp_count, 2, slots, D).transpose(2, 0, 1, 3)
        owned_grads = owned.reshape(slots, unit_rows, D).astype(F32)
    else:
        def units_of(parts, field, first, count):
            sides = jnp.stack(
                [weight_grads((part,), ((field,),), ((count, 0),), first) for part in parts]
            )
            sides = sides.reshape(2, mp_count, UNIT // 4, -1, 2, SPAN, D)
            return sides.transpose(1, 3, 5, 2, 0, 4, 6).reshape(mp_count, -1, unit_rows * D)

        early, late = (early_keep, early_send), (late_keep, late_send)
        summed = lax.psum_scatter(
            jnp.concatenate(
                [
                    units_of(late, mids[1], chunks + few, few),
                    units_of(late, mids[1], chunks + 2 * few, few),
                    units_of(late, mids[1], chunks + 3 * few, few),
                    units_of(late, mids[0], chunks, few),
                    units_of(early, normed_two, chunks, chunks),
                    units_of(late, normed_two, 0, chunks),
                    units_of(early, grad_out, 0, chunks),
                ],
                axis=1,
            ),
            "mp",
            scatter_dimension=0,
            tiled=True,
        )[0]
        summed = lax.psum_scatter(summed, "dp", scatter_dimension=1, tiled=True).astype(F32)
        notes = lax.all_gather(note, ("dp", "mp"), axis=0, tiled=True)
        rows = notes.reshape(-1, 16, D)
        count = 2 * images + 1
        wide = add(rows[:, images : images + count], rows[:, images + count : images + 2 * count])
        scale_row = jnp.sum(wide[:, -1], axis=0)
        cond_all = rows[:, :images].reshape(-1, D).astype(F32)
        gains_all = jnp.concatenate(
            [wide[:, place * images : (place + 1) * images].reshape(-1, D) for place in (0, 1)],
            axis=1,
        )
        cond_half = lax.dynamic_slice_in_dim(
            cond_all, mp_index * (D // mp_count), D // mp_count, 1
        )
        sum_a = lax.dot_general(
            cond_half,
            gains_all,
            (((0,), (0,)), ((), ())),
            precision=lax.Precision.HIGHEST,
            preferred_element_type=F32,
        )
        width = unit_rows * D // dp_count

        def piece(field):
            return lax.dynamic_slice_in_dim(
                field.reshape(-1, unit_rows * D), dp_index * width, width, 1
            )

        grad_shards = jnp.concatenate(
            [
                piece(sum_a[:, :D]),
                summed[: 4 * (D // mp_count // unit_rows)],
                piece(sum_a[:, D:]),
                summed[4 * (D // mp_count // unit_rows) :],
            ]
        )

        placed = owners[0] * slots + slots_before(owners[0])
        slot_rows = lax.broadcasted_iota(jnp.int32, (dp_count * slots, unit_count), 0)
        to_owners = (slot_rows == placed[None, :]).astype(BF16)
        outgoing = dot_nn(to_owners, grad_shards.astype(BF16)).astype(BF16)
        owned = lax.all_to_all(outgoing, "dp", split_axis=0, concat_axis=1, tiled=True)
        owned_grads = owned.reshape(slots, unit_rows, D).astype(F32)

    first_new, second_new = moments(moment_one[0], moment_two[0], owned_grads)
    master_new = adam_step(master[0], first_new, second_new, LEARN_RATE)
    outs_both = both_halves(outs_low, outs_other, mp_index, 1)
    output, input_grad = outs_both[0].astype(F32), outs_both[1].astype(F32)
    scale_grad = scale_grads(scale_row)
    scale_first, scale_second = moments(scale_state[1], scale_state[2], scale_grad)
    scale_new = adam_step(scale_state[0], scale_first, scale_second, SCALE_RATE)
    scale_update = jnp.stack([scale_first, scale_new])
    return (
        output,
        input_grad,
        grad_shards[None],
        master_new[None],
        first_new[None],
        second_new[None],
        scale_update,
        scale_second,
    )


def solution(mesh):
    in_specs = (
        P("dp", None),
        P("dp", None),
        P("dp"),
        P("dp", None, None),
        P("dp", None),
        P("mp", None),
        P("mp", "dp", None, None),
        P("mp", "dp", None, None),
        P("mp", "dp", None, None),
        P(None, "mp"),
    )
    out_specs = (
        P("dp", None),
        P("dp", None),
        P("mp", None, "dp"),
        P("mp", "dp", None, None),
        P("mp", "dp", None, None),
        P("mp", "dp", None, None),
        P(None, "mp"),
        P("mp"),
    )
    return jax.shard_map(
        on_device, mesh=mesh, in_specs=in_specs, out_specs=out_specs, check_vma=False
    )
```

```python
import math

import jax
import jax.numpy as jnp
import numpy as np
from jax import lax
from jax.experimental import pallas as pl
from jax.experimental.pallas import tpu as pltpu
from jax.sharding import PartitionSpec as P

D = 768
HEADS = 12
HD = 64
FF = 2304
SIDE = 16
STEP = 10
SEQ = 256
UNIT = 32
SPAN = 4
SIDES = 2
CHUNK = SIDES * SPAN * UNIT
HALF_CHUNK = CHUNK // 2

NORM_EPS = 1e-06
COS_EPS = 1e-06
SIGMA_DATA = 0.5
BETA_ONE = 0.5
BETA_TWO = 0.5
ADAM_EPS = 1e-08
WEIGHT_DECAY = 0.01
LEARN_RATE = 0.04
SCALE_RATE = 1.0
ROOT_HALF = 0.7071067811865476
INV_ROOT_TWO_PI = 0.3989422804014327

F32 = jnp.float32
BF16 = jnp.bfloat16
VMEM_BYTES = 60 * 1024 * 1024

STACK = (("A1", D), ("Q", D), ("K", D), ("V", D), ("O", D), ("A2", D), ("G", FF), ("U", FF), ("F", FF))
ROW_A1, ROW_A2, ROW_Q, ROW_K, ROW_V, ROW_O = (D * place for place in range(6))
ROW_G = 6 * D
ROW_U = ROW_G + FF
ROW_F = ROW_U + FF
ROWS_ALL = ROW_F + FF
HELD_ROWS = dict(
    A1=ROW_A1, A2=ROW_A2, Q=ROW_Q, K=ROW_K, V=ROW_V, O=ROW_O, G=ROW_G, U=ROW_U, F=ROW_F
)
HEAD_ORDER = [
    side * (HEADS // SIDES) + chunk * (SPAN * UNIT // HD) + head
    for chunk in range(D // CHUNK)
    for side in range(SIDES)
    for head in range(SPAN * UNIT // HD)
]


def to_held(by_head):
    per_chunk = SPAN * UNIT // HD
    return by_head.reshape(SIDES, -1, per_chunk).transpose(1, 0, 2).reshape(-1)


def from_held(held):
    per_chunk = SPAN * UNIT // HD
    return held.reshape(-1, SIDES, per_chunk).transpose(1, 0, 2).reshape(-1)


def held_units():
    places = []
    for side in range(SIDES):
        for kind, rows in STACK:
            count = rows // SIDES // UNIT
            for unit in range(count):
                if kind in ("A1", "A2"):
                    place = side * count + unit
                else:
                    place = (unit // SPAN * SIDES + side) * SPAN + unit % SPAN
                places.append(HELD_ROWS[kind] // UNIT + place)
    return np.array(places, np.int32)


def dot_nn(left, right):
    return jnp.dot(left, right, preferred_element_type=F32)


def dot_nt(left, right):
    return lax.dot_general(left, right, (((1,), (1,)), ((), ())), preferred_element_type=F32)


def slots_before(owner_list):
    unit_count = owner_list.shape[0]
    same_owner = owner_list[:, None] == owner_list[None, :]
    row_ids = lax.broadcasted_iota(jnp.int32, (unit_count, unit_count), 0)
    col_ids = lax.broadcasted_iota(jnp.int32, (unit_count, unit_count), 1)
    return jnp.sum(jnp.where(same_owner & (col_ids < row_ids), 1, 0), axis=1).astype(jnp.int32)


def rope_tables(positions):
    quarter = HD // 8
    head_ids = jnp.array(HEAD_ORDER, jnp.int32)[:, None]
    column = lax.broadcasted_iota(jnp.int32, (HEADS, quarter), 1)
    flat_index = (column * HEADS + head_ids).astype(F32)
    low_log = math.log(math.pi)
    high_log = math.log(10.0 * math.pi)
    frequency = jnp.exp(low_log + (high_log - low_log) * flat_index / (HEADS * quarter))
    placed = (2.0 * positions.astype(F32) + 1.0) / SIDE - 1.0
    along_rows = placed[:, 0].reshape(1, 1, -1) * frequency[:, :, None]
    along_cols = placed[:, 1].reshape(1, 1, -1) * frequency[:, :, None]
    angles = jnp.concatenate([along_rows, along_cols], axis=1).reshape(HEADS * 2 * quarter, -1)
    return jnp.cos(angles), jnp.sin(angles)


def deal_matrix(core):
    target = lax.broadcasted_iota(jnp.int32, (CHUNK, CHUNK), 0)
    source = lax.broadcasted_iota(jnp.int32, (CHUNK, CHUNK), 1)
    parity = (target // HALF_CHUNK + core) % 2
    inner = target % HALF_CHUNK
    unit = inner % SPAN
    row = inner // SPAN % 2
    piece = inner // (2 * SPAN) % (UNIT // 4)
    side = inner // (2 * SPAN * (UNIT // 4))
    return (source == (side * SPAN + unit) * UNIT + 4 * piece + 2 * parity + row).astype(BF16)


def layer_kernel(
    images,
    slots_refs,
    place_ref,
    ends_ref,
    scal_ref,
    x_ref,
    cot_ref,
    gb_ref,
    cond_ref,
    cos_ref,
    sin_ref,
    deal_ref,
    outs_hbm,
    early_keep,
    early_send,
    late_keep,
    late_send,
    n2_hbm,
    mids_hbm,
    note_hbm,
    w,
    unit_s,
    coef_s,
    qtok_s,
    p_s,
    qk_s,
    v_s,
    o_s,
    x2_s,
    n1_s,
    n2_s,
    ga_s,
    do_s,
    dot_s,
    ff_s,
    dn2_s,
    dqkv_s,
    early_s,
    late_s,
    outs_s,
    note_s,
    ds_s,
    note_low,
    w_sem,
    o_sem,
):
    toks = images * SEQ
    sends = []

    def send(src, dst):
        copy = pltpu.make_async_copy(src, dst, o_sem.at[len(sends)])
        copy.start()
        sends.append(copy)

    groups = (0, ROW_Q, ROW_O, ROW_G, ROWS_ALL)

    def fetch(low, high):
        first = 0
        for array, slots_ref in enumerate(slots_refs):

            @pl.loop(ends_ref[array, low // 3], ends_ref[array, low // 3 + 1])
            def _(index, slots_ref=slots_ref, first=first):
                unit = place_ref[0, first + index]
                group = jnp.int32(low)
                for bound in groups[low + 1 : high]:
                    group += jnp.where(unit >= bound // UNIT, 1, 0)
                pltpu.make_async_copy(
                    slots_ref.at[place_ref[1, first + index]],
                    w.at[pl.ds(pl.multiple_of(unit * UNIT, UNIT), UNIT)],
                    w_sem.at[group],
                ).start()

            first += slots_ref.shape[0]

    fetch(0, 3)

    def weights_here(index):
        low, high = groups[index : index + 2]
        region = w.at[pl.ds(low, high - low)]
        pltpu.make_async_copy(region, region, w_sem.at[index]).wait()

    def image_rows(image):
        return pl.ds(image * SEQ, SEQ)

    note_s[...] = jnp.zeros_like(note_s)
    note_s[:images] = cond_ref[:images].astype(F32)

    def note(place, row):
        high = row.astype(BF16).astype(F32)
        lanes = slice(0, row.shape[1])
        note_s[place : place + 1, lanes] = high
        note_s[place + 2 * images + 1 : place + 2 * images + 2, lanes] = row - high

    fetch(3, 4)
    weights_here(0)
    gain_one = 1.0 + dot_nn(cond_ref[...], w[ROW_A1 : ROW_A1 + D])
    gain_two = 1.0 + dot_nn(cond_ref[...], w[ROW_A2 : ROW_A2 + D])
    for image in range(images):
        x = x_ref[image_rows(image)]
        inverse = lax.rsqrt(jnp.mean(x * x, axis=-1, keepdims=True) + NORM_EPS)
        n1_s[image_rows(image)] = (x * inverse * gain_one[image : image + 1]).astype(BF16)
    send(n1_s, mids_hbm.at[1])
    weights_here(1)
    unit_s[:D] = dot_nt(w[ROW_Q : ROW_Q + D], n1_s[...])
    unit_s[D:] = dot_nt(w[ROW_K : ROW_K + D], n1_s[...])
    v_s[...] = dot_nt(w[ROW_V : ROW_V + D], n1_s[...]).astype(BF16)

    @pl.loop(0, 2 * HEADS)
    def _(index):
        head = lax.rem(index, HEADS)
        rows = pl.ds(pl.multiple_of(index * HD, HD), HD)
        angle_rows = pl.ds(pl.multiple_of(head * 16, 16), 16)
        raw = unit_s[rows]
        inverse = lax.rsqrt(jnp.sum(raw * raw, axis=0, keepdims=True) + COS_EPS)
        unit = raw * inverse
        root = scal_ref[HEADS + head]
        unit_s[rows] = unit
        coef_s[pl.ds(index, 1)] = root * inverse
        scaled = unit * root
        first, second = scaled[:16], scaled[16:32]
        cosine, sine = cos_ref[angle_rows], sin_ref[angle_rows]
        turned = jnp.concatenate(
            [first * cosine - second * sine, second * cosine + first * sine, scaled[32:]], axis=0
        )
        qk_s[rows] = turned.astype(BF16)

    qtok_s[...] = qk_s[:D].T

    def head_rows(head):
        return pl.ds(pl.multiple_of(head * HD, HD), HD)

    def pair_lanes(pair):
        return pl.ds(pl.multiple_of(pair * 2 * HD, 2 * HD), 2 * HD)

    @pl.loop(0, HEADS // 2, unroll=2)
    def _(pair):
        for image in range(images):
            cols = image_rows(image)
            query = qtok_s[cols, pair_lanes(pair)]
            mixed = []
            for half in range(2):
                head = pair * 2 + half
                scores = dot_nn(
                    query[:, half * HD : (half + 1) * HD], qk_s[head_rows(HEADS + head), cols]
                )
                exp_scores = jnp.exp(scores - scal_ref[head])
                inverse = 1.0 / jnp.sum(exp_scores, axis=-1, keepdims=True)
                probs = (exp_scores * inverse).astype(BF16)
                p_s[head, cols] = probs
                mixed.append(dot_nt(probs, v_s[head_rows(head), cols]))
            o_s[cols, pair_lanes(pair)] = jnp.concatenate(mixed, axis=1)

    weights_here(2)
    x2_s[...] = x_ref[...] + dot_nn(o_s[...].astype(BF16), w[ROW_O : ROW_O + D])
    for image in range(images):
        x2 = x2_s[image_rows(image)]
        inverse = lax.rsqrt(jnp.mean(x2 * x2, axis=-1, keepdims=True) + NORM_EPS)
        n2_s[image_rows(image)] = (x2 * inverse * gain_two[image : image + 1]).astype(BF16)
    send(n2_s, n2_hbm)

    weights_here(3)
    chunks = FF // CHUNK
    width = D

    def deal(field, store, place):
        dealt = dot_nt(deal_ref[...], field).astype(BF16)
        store[0, place] = dealt[:HALF_CHUNK]
        store[1, place] = dealt[HALF_CHUNK:]

    for start in range(0, FF, width):

        def part(base):
            return w[base + start : base + start + width]

        gate = dot_nt(n2_s[...], part(ROW_G))
        up = dot_nt(n2_s[...], part(ROW_U))
        grad_hidden = dot_nt(gb_ref[...], part(ROW_F))
        phi_sum = 0.5 * (1.0 + lax.erf(gate * ROOT_HALF))
        density = INV_ROOT_TWO_PI * jnp.exp(-0.5 * gate * gate)
        gelu = gate * phi_sum
        hidden = (gelu * up).astype(BF16)
        grad_gate = (grad_hidden * up * (phi_sum + gate * density)).astype(BF16)
        grad_up = (grad_hidden * gelu).astype(BF16)
        ff = dot_nn(hidden, part(ROW_F))
        dn2 = dot_nn(grad_gate, part(ROW_G)) + dot_nn(grad_up, part(ROW_U))
        if start == 0:
            ff_s[...] = ff
            dn2_s[...] = dn2
        else:
            ff_s[...] += ff
            dn2_s[...] += dn2
        for at in range(0, width, CHUNK):
            place = (start + at) // CHUNK
            deal(hidden[:, at : at + CHUNK], early_s, place)
            deal(grad_gate[:, at : at + CHUNK], early_s, chunks + place)
            deal(grad_up[:, at : at + CHUNK], late_s, place)

    send(early_s.at[0], early_keep)
    send(early_s.at[1], early_send)
    outs_s[0] = (x2_s[...] + ff_s[...]).astype(BF16)
    send(outs_s.at[0], outs_hbm.at[0])

    def norm_back(x, gain, grad_normed):
        inverse = lax.rsqrt(jnp.mean(x * x, axis=-1, keepdims=True) + NORM_EPS)
        scaled = grad_normed * gain
        inner = jnp.mean(x * scaled, axis=-1, keepdims=True)
        grad_x = inverse * scaled - x * (inverse * inverse * inverse * inner)
        return grad_x, jnp.sum(grad_normed * x * inverse, axis=0, keepdims=True)

    for image in range(images):
        rows = image_rows(image)
        grad_x, grad_gain = norm_back(x2_s[rows], gain_two[image : image + 1], dn2_s[rows])
        grad = cot_ref[rows].astype(F32) * scal_ref[2 * HEADS + image] + grad_x
        x2_s[rows] = grad
        ga_s[rows] = grad.astype(BF16)
        note(2 * images + image, grad_gain)
    send(ga_s, mids_hbm.at[0])

    do_s[...] = dot_nt(ga_s[...], w[ROW_O : ROW_O + D]).astype(BF16)
    dot_s[...] = dot_nt(w[ROW_O : ROW_O + D], ga_s[...]).astype(BF16)
    ds_s[...] = jnp.zeros_like(ds_s)

    @pl.loop(0, HEADS // 2, unroll=3)
    def _(pair):
        for image in range(images):
            cols = image_rows(image)
            grads_mixed = do_s[cols, pair_lanes(pair)]
            inners = grads_mixed.astype(F32) * o_s[cols, pair_lanes(pair)]
            for half in range(2):
                head = pair * 2 + half
                lanes = slice(half * HD, (half + 1) * HD)
                rows, key_rows = head_rows(head), head_rows(HEADS + head)
                key, value = qk_s[key_rows, cols], v_s[rows, cols]
                probs = p_s[head, cols]
                grad_probs = dot_nn(grads_mixed[:, lanes], value)
                inner = jnp.sum(inners[:, lanes], axis=-1, keepdims=True)
                grad_scores = (probs.astype(F32) * (grad_probs - inner)).astype(BF16)
                grad_query = dot_nt(key, grad_scores)
                grad_key = dot_nn(qk_s[rows, cols], grad_scores)
                grad_value = dot_nn(dot_s[rows, cols], probs)
                angle_rows = pl.ds(pl.multiple_of(head * 16, 16), 16)
                cosine, sine = cos_ref[angle_rows, cols], sin_ref[angle_rows, cols]
                along = jnp.zeros((1, SEQ), F32)
                for grad, own_rows, place in (
                    (grad_query, rows, head),
                    (grad_key, key_rows, HEADS + head),
                ):
                    first, second = grad[:16], grad[16:32]
                    back = jnp.concatenate(
                        [
                            first * cosine + second * sine,
                            second * cosine - first * sine,
                            grad[32:],
                        ],
                        axis=0,
                    )
                    unit = unit_s[own_rows, cols]
                    inner_unit = jnp.sum(unit * back, axis=0, keepdims=True)
                    along += inner_unit
                    dqkv_s[own_rows, cols] = (
                        coef_s[pl.ds(place, 1), cols] * (back - unit * inner_unit)
                    ).astype(BF16)
                value_rows = head_rows(2 * HEADS + head)
                dqkv_s[value_rows, cols] = grad_value.astype(BF16)
                ds_s[pl.ds(head, 1)] += along

    per_kind = D // CHUNK
    for place in range(per_kind):
        deal(o_s[:, place * CHUNK : (place + 1) * CHUNK].astype(BF16), late_s, chunks + place)
    for place in range(3 * per_kind):
        dealt = dot_nn(deal_ref[...], dqkv_s[place * CHUNK : (place + 1) * CHUNK]).astype(BF16)
        late_s[0, chunks + per_kind + place] = dealt[:HALF_CHUNK]
        late_s[1, chunks + per_kind + place] = dealt[HALF_CHUNK:]
    send(late_s.at[0], late_keep)
    send(late_s.at[1], late_send)
    dn1 = dot_nn(dqkv_s[:D].T, w[ROW_Q : ROW_Q + D])
    dn1 += dot_nn(dqkv_s[D : 2 * D].T, w[ROW_K : ROW_K + D])
    dn1 += dot_nn(dqkv_s[2 * D :].T, w[ROW_V : ROW_V + D])
    dn2_s[...] = dn1
    for image in range(images):
        rows = image_rows(image)
        grad_x, grad_gain = norm_back(x_ref[rows], gain_one[image : image + 1], dn2_s[rows])
        outs_s[1, rows] = (x2_s[rows] + grad_x).astype(BF16)
        note(images + image, grad_gain)
    send(outs_s.at[1], outs_hbm.at[1])
    ones = jnp.ones((8, SEQ), F32)
    scale_row = lax.dot_general(
        ones,
        ds_s[...],
        (((1,), (1,)), ((), ())),
        precision=lax.Precision.HIGHEST,
        preferred_element_type=F32,
    )
    note(3 * images, scale_row[:1])
    note_low[...] = note_s[...].astype(BF16)
    send(note_low, note_hbm)
    for copy in sends:
        copy.wait()


def run_layer(images, places, ends, scalars, x, cotangent, grad_out, cond, cosine, sine, deal, slots):
    toks = images * SEQ
    chunks = FF // CHUNK
    any_spec = pl.BlockSpec(memory_space=pl.ANY)
    vmem = pl.BlockSpec(memory_space=pltpu.VMEM)
    smem = pl.BlockSpec(memory_space=pltpu.SMEM)
    field = jax.ShapeDtypeStruct((toks, D), BF16)

    def dealt(count):
        return jax.ShapeDtypeStruct((count, HALF_CHUNK, toks), BF16)

    pair = jax.ShapeDtypeStruct((2, toks, D), BF16)
    late = chunks + 4 * D // CHUNK
    outs = [pair, dealt(2 * chunks), dealt(2 * chunks), dealt(late), dealt(late), field, pair]
    outs += [jax.ShapeDtypeStruct((16, D), BF16)]
    wide = pltpu.VMEM((toks, D), F32)
    low = pltpu.VMEM((toks, D), BF16)
    scratch = [
        pltpu.VMEM((ROWS_ALL, D), BF16),
        pltpu.VMEM((2 * D, toks), F32),
        pltpu.VMEM((2 * HEADS, toks), F32),
        low,
        pltpu.VMEM((HEADS, toks, SEQ), BF16),
        pltpu.VMEM((2 * D, toks), BF16),
        pltpu.VMEM((D, toks), BF16),
        wide,
        wide,
        low,
        low,
        low,
        low,
        pltpu.VMEM((D, toks), BF16),
        wide,
        wide,
        pltpu.VMEM((3 * D, toks), BF16),
        pltpu.VMEM((2, 2 * chunks, HALF_CHUNK, toks), BF16),
        pltpu.VMEM((2, late, HALF_CHUNK, toks), BF16),
        pltpu.VMEM((2, toks, D), BF16),
        pltpu.VMEM((16, D), F32),
        pltpu.VMEM((16, SEQ), F32),
        pltpu.VMEM((16, D), BF16),
        pltpu.SemaphoreType.DMA((4,)),
        pltpu.SemaphoreType.DMA((16,)),
    ]

    operands = [places, ends, scalars, x, cotangent, grad_out, cond, cosine, sine, deal]
    here = len(operands)

    def body(*refs):
        layer_kernel(
            images, refs[here : here + len(slots)], *refs[:here], *refs[here + len(slots) :]
        )

    return pl.pallas_call(
        body,
        out_shape=outs,
        in_specs=[smem] * 3 + [vmem] * 7 + [any_spec] * len(slots),
        out_specs=[any_spec] * len(outs),
        scratch_shapes=scratch,
        compiler_params=pltpu.CompilerParams(vmem_limit_bytes=VMEM_BYTES),
        cost_estimate=pl.CostEstimate(
            flops=2 * 3 * ROWS_ALL * D * toks, bytes_accessed=ROWS_ALL * D * 4, transcendentals=0
        ),
        name="layer",
    )(*operands, *slots)


def weight_grads(lefts, rights, kinds, first=0, here=3):
    rows, toks = lefts[0].shape[1:]
    pieces = rows // (SIDES * 2 * SPAN)
    total = sum(count for count, _ in kinds)
    steps = total // here
    step_rights = [place for count, place in kinds for _ in range(count // here)]
    operands, specs = list(lefts), []
    for left in lefts:
        specs.append(pl.BlockSpec((here, rows, toks), lambda step: (first // here + step, 0, 0)))
    for parts in rights:
        for part in parts:
            field, at = part if isinstance(part, tuple) else (part[None], 0)
            operands.append(field)
            specs.append(pl.BlockSpec((None, toks, D), lambda step, at=at: (at, 0, 0)))

    def body(*refs):
        out_ref, count = refs[-1], len(lefts)
        step = pl.program_id(0)
        for place in range(len(rights)):
            own = refs[count * (place + 1) : count * (place + 2)]
            mine = [index for index, right in enumerate(step_rights) if right == place]

            @pl.when((step >= mine[0]) & (step <= mine[-1]))
            def _(own=own):
                summed = dot_nn(refs[0][...].reshape(here * rows, toks), own[0][...])
                for left, right in zip(refs[1:count], own[1:]):
                    summed += dot_nn(left[...].reshape(here * rows, toks), right[...])
                for chunk in range(here):
                    out_ref[:, :, chunk] = (
                        summed[chunk * rows : (chunk + 1) * rows]
                        .reshape(SIDES, pieces, 2 * SPAN, D)
                        .astype(BF16)
                    )

    return pl.pallas_call(
        body,
        out_shape=jax.ShapeDtypeStruct((SIDES, pieces, total, 2 * SPAN, D), BF16),
        grid=(steps,),
        in_specs=specs,
        out_specs=pl.BlockSpec(
            (SIDES, pieces, here, 2 * SPAN, D), lambda step: (0, 0, step, 0, 0)
        ),
        compiler_params=pltpu.CompilerParams(vmem_limit_bytes=VMEM_BYTES),
        cost_estimate=pl.CostEstimate(
            flops=2 * len(lefts) * total * rows * toks * D,
            bytes_accessed=2 * len(lefts) * (total * rows + len(rights) * D) * toks
            + 2 * total * rows * D,
            transcendentals=0,
        ),
        name="weight_grads",
    )(*operands)


def adam_step(weights, first_new, second_new, rate):
    fix_one = 1.0 - math.pow(BETA_ONE, STEP)
    fix_two = 1.0 - math.pow(BETA_TWO, STEP)
    return weights * (1.0 - rate * WEIGHT_DECAY) - rate * (first_new / fix_one) / (
        jnp.sqrt(second_new / fix_two) + ADAM_EPS
    )


def moments(first, second, grad):
    return (
        BETA_ONE * first + (1.0 - BETA_ONE) * grad,
        BETA_TWO * second + (1.0 - BETA_TWO) * grad * grad,
    )


def pack(fields):
    def body(*refs):
        for place, ref in enumerate(refs[:-1]):
            refs[-1][place] = ref[...]

    return pl.pallas_call(
        body,
        out_shape=jax.ShapeDtypeStruct((len(fields), *fields[0].shape), fields[0].dtype),
        name="pack",
    )(*fields)


def factor_sums(notes, indices, images, mp_count):
    rows_wanted = 2 * (D // mp_count // UNIT)
    pieces = 2 * images + 1

    def body(*refs):
        index_ref, sums_ref, scale_ref = refs[-3:]
        rows = jnp.concatenate([ref[...].reshape(-1, D) for ref in refs[:-3]])
        row = lax.broadcasted_iota(jnp.int32, (rows_wanted, D), 0)
        feature = lax.broadcasted_iota(jnp.int32, (rows_wanted, D), 1)
        unit = row // (2 * SPAN) * SPAN + row % SPAN
        wanted = (index_ref[0] * (rows_wanted // 2) + unit) * UNIT
        wanted += 2 * index_ref[1] + row // SPAN % 2
        features = (feature == wanted).astype(BF16)
        count = rows.shape[0]
        source = lax.broadcasted_iota(jnp.int32, (count, count), 0)
        target = lax.broadcasted_iota(jnp.int32, (count, count), 1)
        ahead = target - source
        is_cond = source % 16 < images
        cond_rows = dot_nt(features, rows).astype(BF16)
        for place in range(2):
            first = images * (1 + place)
            pick_rows = is_cond & ((ahead == first) | (ahead == first + pieces))
            chosen = dot_nn(cond_rows, pick_rows.astype(BF16)).astype(BF16)
            sums_ref[place] = dot_nn(chosen, rows)
        column = lax.broadcasted_iota(jnp.int32, (8, count), 1) % 16
        last = (column == 3 * images) | (column == 3 * images + pieces)
        scale_ref[...] = dot_nn(last.astype(BF16), rows)

    return pl.pallas_call(
        body,
        out_shape=[
            jax.ShapeDtypeStruct((2, rows_wanted, D), F32),
            jax.ShapeDtypeStruct((8, D), F32),
        ],
        in_specs=[pl.BlockSpec(memory_space=pltpu.VMEM)] * len(notes)
        + [pl.BlockSpec(memory_space=pltpu.SMEM)],
        compiler_params=pltpu.CompilerParams(vmem_limit_bytes=VMEM_BYTES),
        name="factor_sums",
    )(*notes, indices)


def route(sum_a, sum_fg, sum_rest, placed, slots, dp_count):
    chunks, few = FF // CHUNK, D // CHUNK
    rows = 2 * placed.shape[1]
    to_row = np.arange(dp_count * 2 * slots)
    columns = np.stack([to_row // (2 * slots) * slots + to_row % slots, to_row // slots % 2], axis=1)
    placed_rows = jnp.broadcast_to(placed.reshape(-1, 1, SPAN), (rows // (2 * SPAN), 2, SPAN))

    def body(a_ref, fg_one, fg_two, rest_one, rest_two, placed_ref, columns_ref, *outs):
        pieces_ref, out_ref = outs
        fg_ref = fg_one[...] + fg_two[...].astype(F32)
        rest_ref = rest_one[...] + rest_two[...].astype(F32)
        start = 0
        for field in (
            a_ref[0],
            rest_ref[chunks + few :],
            rest_ref[chunks : chunks + few],
            a_ref[1],
            fg_ref[chunks:],
            rest_ref[:chunks],
            fg_ref[:chunks],
        ):
            field = field.reshape(-1, D)
            pieces_ref[start : start + field.shape[0]] = field
            start += field.shape[0]
        row = lax.broadcasted_iota(jnp.int32, (1, rows), 1) // SPAN % 2
        chosen = (columns_ref[:, :1] == placed_ref[...]) & (columns_ref[:, 1:] == row)
        out_ref[...] = dot_nn(chosen.astype(BF16), pieces_ref[...].astype(BF16)).astype(BF16)

    return pl.pallas_call(
        body,
        out_shape=[
            jax.ShapeDtypeStruct((rows, D), F32),
            jax.ShapeDtypeStruct((dp_count * 2 * slots, D), BF16),
        ],
        compiler_params=pltpu.CompilerParams(vmem_limit_bytes=VMEM_BYTES),
        name="route",
    )(sum_a, *sum_fg, *sum_rest, placed_rows.reshape(1, rows), jnp.array(columns, jnp.int32))


def add(*terms):
    total = terms[0].astype(F32)
    for term in terms[1:]:
        total = total + term.astype(F32)
    return total


class Ring:
    def __init__(self, dp_count):
        self.count = dp_count // 2
        pairs = []
        for place in range(self.count):
            for core in range(2):
                pairs.append(
                    (self.chip(place) * 2 + core, self.chip((place + 1) % self.count) * 2 + core)
                )
        self.onward = pairs
        self.backward = [(b, a) for a, b in pairs]
        self.twins = [(index, index ^ 1) for index in range(dp_count)]

    def chip(self, place):
        column = self.count // 2
        return 2 * place if place < column else 2 * (self.count - 1 - place) + 1

    def here(self):
        chip = lax.axis_index("dp") // 2
        return jnp.where(chip % 2 == 0, chip // 2, self.count - 1 - chip // 2)

    def chip_at(self, offset):
        place = (self.here() + offset + self.count) % self.count
        column = self.count // 2
        return jnp.where(place < column, 2 * place, 2 * (self.count - 1 - place) + 1)

    def on(self, field):
        return lax.ppermute(field, "dp", self.onward)

    def back(self, field):
        return lax.ppermute(field, "dp", self.backward)

    def twin(self, field):
        return lax.ppermute(field, "dp", self.twins)


def after(field, *others):
    return lax.optimization_barrier((field, others))[0]


def swap_mp(field):
    return lax.ppermute(field, "mp", [(0, 1), (1, 0)])


class Labels:
    def __init__(self, rows):
        self.rows = list(rows)

    def __getitem__(self, cut):
        return Labels(self.rows[cut])

    def moved(self, hop, mp, core):
        return Labels((h + hop, m ^ mp, c ^ core, slot) for h, m, c, slot in self.rows)


class LabelMoves:
    def on(self, field):
        return field.moved(-1, 0, 0)

    def back(self, field):
        return field.moved(1, 0, 0)

    def swap(self, field):
        return field.moved(0, 1, 0)

    def twin(self, field):
        return field.moved(0, 0, 1)

    def cat(self, *fields):
        return Labels(row for field in fields for row in field.rows)

    def together(self, *fields):
        return fields


class Moves:
    def __init__(self, ring):
        self.on, self.back, self.twin, self.swap = ring.on, ring.back, ring.twin, swap_mp

    def cat(self, *fields):
        return jnp.concatenate(fields)

    def together(self, *fields):
        return lax.optimization_barrier(fields)


def gather_slots(moves, own, slots, early=(), use_early=None, late=(), use_late=None):
    cat, on, back, swap, twin = moves.cat, moves.on, moves.back, moves.swap, moves.twin
    cut = (slots - 1) // 2
    rest = slots - cut
    first, second = own[:cut], own[cut:]
    hop = [on(second), back(second), swap(first), twin(own)]
    f0, b0, y0, c0, second, *early = moves.together(*hop, second, *early)
    wide = cat(first, y0)
    hop = [on(wide), back(wide), swap(second), twin(cat(y0, f0, b0))]
    f1, b1, y1, c1, f0, b0, *late = moves.together(*hop, f0, b0, *late)
    hop = [on(cat(f0, f1)), back(cat(b0, b1)), swap(cat(f0, b0)), twin(cat(f1, b1, y1))]
    done = (*use_early(*early), *use_late(*late)) if early else ()
    f2, b2, y2, c2, *done = moves.together(*hop, *done)
    crossing = cat(f2[:rest], b2[:rest])
    hop = [on(f2), back(b2), swap(crossing), twin(cat(f2, b2, y2))]
    f3, b3, y3, c3 = moves.together(*hop)
    half = (slots + cut) // 2
    crossing = cat(f3[:rest], b3[:rest])
    hop = [on(f3[:half]), back(b3[half:]), swap(crossing), twin(cat(f3, b3, y3))]
    f4, b4, y4, c4 = moves.together(*hop)
    y5 = swap(cat(f4[:rest], b4[: max(0, rest - half)]))
    c5 = [twin(f4), twin(b4), twin(y4)]
    return [own, f0, b0, y0, c0, f1, b1, y1, c1, f2, b2, y2, c2, f3, b3, y3, c3, f4, b4, y4, c4, y5] + c5 + [twin(y5)], done


def both_halves(own, other, half, axis=0):
    return jnp.where(
        half == 0,
        jnp.concatenate([own, other], axis=axis),
        jnp.concatenate([other, own], axis=axis),
    )


def pick(field, *places):
    for place in places:
        field = lax.dynamic_index_in_dim(field, place, 0, keepdims=False)
    return field


def far_packets(field, chip, note):
    sides, _, chunks, rows, cols = field.shape
    dims = (chunks + note.shape[0], rows, cols)

    def body(_, own, note_ref, *outs):
        for way, out in enumerate(outs):
            out[:chunks] = own[way]
            out[chunks:] = note_ref[...]

    def whole(shape):
        return pl.BlockSpec(shape, lambda _, chip: (0,) * len(shape))

    return pl.pallas_call(
        body,
        grid_spec=pltpu.PrefetchScalarGridSpec(
            num_scalar_prefetch=1,
            grid=(1,),
            in_specs=[
                pl.BlockSpec(
                    (sides, None, chunks, rows, cols), lambda _, chip: (0, chip[0], 0, 0, 0)
                ),
                whole(note.shape),
            ],
            out_specs=[whole(dims)] * 2,
        ),
        out_shape=[jax.ShapeDtypeStruct(dims, BF16)] * 2,
        compiler_params=pltpu.CompilerParams(vmem_limit_bytes=VMEM_BYTES),
        name="far_packets",
    )(chip, field, note)


class RingSum:
    def __init__(self, ring, field, half, note=None):
        self.ring, self.field, self.half = ring, field, half
        self.distance = ring.count // 2
        self.on = self.back = None
        self.own = self.note_on = self.note_back = note
        self.seen = []

    def block(self, offset):
        return lax.dynamic_index_in_dim(self.field, self.ring.chip_at(offset), 1, keepdims=False)

    def step(self, *others):
        ring, far, distance = self.ring, self.ring.count // 2, self.distance
        chunks = self.field.shape[2]
        if distance == far:
            block = self.block(far)
            on, back = block[0], block[1]
        else:
            on, back = self.block(distance), self.block(-distance)
            if distance == far - 1:
                on = jnp.stack([add(on[0], self.on).astype(BF16), on[1]])
                back = jnp.stack([back[0], add(back[1], self.back).astype(BF16)])
            else:
                on, back = add(on, self.on).astype(BF16), add(back, self.back).astype(BF16)
        if self.own is not None and distance == far:
            on, back = far_packets(self.field, ring.chip_at(far).reshape(1), self.own)
        elif self.own is not None:
            axis = on.ndim - 3
            shape = on.shape[:axis] + (2 // (axis + 1),) + on.shape[axis + 1 :]
            on = jnp.concatenate([on, self.note_on.reshape(shape)], axis=axis)
            back = jnp.concatenate([back, self.note_back.reshape(shape)], axis=axis)
        if others:
            on, back = after(on, *others), after(back, *others)
        on, back = lax.optimization_barrier((ring.on(on), ring.back(back)))
        if self.own is not None:
            self.note_on = on[..., chunks:, :, :].reshape(self.own.shape)
            self.note_back = back[..., chunks:, :, :].reshape(self.own.shape)
            self.seen += [self.note_on, self.note_back]
            on, back = on[..., :chunks, :, :], back[..., :chunks, :, :]
        self.on, self.back = on, back
        self.distance -= 1
        return self.on, self.back

    def total(self):
        total = add(self.block(0), self.on, self.back)
        other = swap_mp(pick(total.astype(BF16), 1 - self.half))
        return pick(total, self.half), other

    def notes(self):
        return [self.own] + self.seen[:-1]


def on_device(
    tokens,
    conditioning,
    sigmas,
    positions,
    cotangent,
    owners,
    master,
    moment_one,
    moment_two,
    scale_state,
):
    dp_count = lax.axis_size("dp")
    mp_count = lax.axis_size("mp")
    dp_index = lax.axis_index("dp")
    mp_index = lax.axis_index("mp")
    images = conditioning.shape[0] // mp_count
    toks = images * SEQ
    slots = master.shape[1]
    unit_rows = master.shape[2]
    unit_count = owners.shape[1]
    heads_here = scale_state.shape[1]
    paired = dp_count * 2 == UNIT
    core = dp_index % 2 if paired else 0

    def mine(field, rows):
        return lax.dynamic_slice_in_dim(field, mp_index * rows, rows, 0)

    rounded = master[0].astype(BF16)
    halves_here = jnp.concatenate([owners[0].astype(F32), scale_state[0]])[None]
    ring = Ring(dp_count) if paired else None
    if paired:
        own_labels = Labels((0, 0, 0, slot) for slot in range(slots))
        arrays, _ = gather_slots(LabelMoves(), own_labels, slots)
        labels = [row for field in arrays for row in field.rows]
        sizes = [len(field.rows) for field in arrays]
        assert len(set((h % ring.count, m, c, slot) for h, m, c, slot in labels)) == len(labels)
        hops, sides, cores, numbers = (jnp.array(column, jnp.int32) for column in zip(*labels))
        owner = ring.chip_at(hops) * 2 + (dp_index % 2 + cores) % 2
        side = (mp_index + sides) % 2
        slot_ids = (side * dp_count + owner) * slots + numbers
    else:
        sizes = [mp_count * dp_count * slots]
        slot_ids = lax.broadcasted_iota(jnp.int32, (mp_count * dp_count * slots, 1), 0)[:, 0]

    def prepare_places(halves_other):
        halves_all = both_halves(halves_here, halves_other, mp_index)
        owners_all = halves_all[:, :unit_count].astype(jnp.int32)
        before = jnp.stack([slots_before(owners_all[half]) for half in range(mp_count)])
        half_ids = lax.broadcasted_iota(jnp.int32, owners_all.shape, 0)
        unit_slots = ((half_ids * dp_count + owners_all) * slots + before).reshape(-1)
        belongs = jnp.array(held_units())
        match = slot_ids[:, None] == unit_slots[None, :]
        places = jnp.where(
            jnp.any(match, axis=1),
            jnp.sum(jnp.where(match, belongs[None, :], 0), axis=1),
            belongs.shape[0],
        )
        starts = np.cumsum([0] + sizes)
        array_ids = jnp.array(np.repeat(np.arange(len(sizes)), sizes), jnp.int32)
        slot_numbers = jnp.array(np.concatenate([np.arange(size) for size in sizes]), jnp.int32)
        key = places * starts[-1] + slot_numbers
        ahead = (array_ids[:, None] == array_ids[None, :]) & (key[None, :] < key[:, None])
        rank = jnp.sum(jnp.where(ahead, 1, 0), axis=1) + jnp.array(np.repeat(starts[:-1], sizes), jnp.int32)
        at_rank = rank[None, :] == lax.broadcasted_iota(jnp.int32, (starts[-1],) * 2, 0)
        sorted_places = jnp.stack(
            [
                jnp.sum(jnp.where(at_rank, field[None, :], 0), axis=1)
                for field in (places, slot_numbers)
            ]
        )
        own_array = array_ids[None, :] == lax.broadcasted_iota(
            jnp.int32, (len(sizes), array_ids.shape[0]), 0
        )
        ends = jnp.stack(
            [
                jnp.sum(jnp.where(own_array & (places < bound // UNIT)[None, :], 1, 0), axis=1)
                for bound in (0, ROW_G, ROWS_ALL)
            ],
            axis=1,
        )
        return sorted_places, ends

    def prepare_fields(halves_other, tokens, conditioning, sigmas, positions, cotangent):
        halves_all = both_halves(halves_here, halves_other, mp_index)
        scales_all = halves_all[:, unit_count:].reshape(-1)
        scales_held = to_held(scales_all)
        square = sigmas * sigmas
        data_square = SIGMA_DATA * SIGMA_DATA
        loss_weight = 4.0 * square * data_square / ((square + data_square) * (square + data_square))
        scalars = jnp.concatenate([scales_held, jnp.sqrt(scales_held), mine(loss_weight, images)])
        cosine, sine = rope_tables(mine(positions, images))
        cond = jnp.pad(mine(conditioning, images).astype(BF16), ((0, 16 - images), (0, 0)))

        grad_out = (
            mine(cotangent, toks).astype(F32).reshape(images, SEQ, D)
            * mine(loss_weight, images)[:, None, None]
        ).astype(BF16).reshape(toks, D)
        return (
            scalars,
            scales_all,
            cosine,
            sine,
            cond,
            grad_out,
            deal_matrix(core),
            mine(tokens, toks),
            mine(cotangent, toks),
        )

    halves_other = swap_mp(halves_here)
    if paired:
        gathered, prepared = gather_slots(
            Moves(ring),
            rounded,
            slots,
            (halves_other,),
            prepare_places,
            (halves_other, tokens, conditioning, sigmas, positions, cotangent),
            prepare_fields,
        )
    else:
        gathered = [lax.all_gather(rounded, ("mp", "dp"), axis=0, tiled=True)]
        prepared = prepare_places(halves_other)
        prepared += prepare_fields(
            halves_other, tokens, conditioning, sigmas, positions, cotangent
        )
    places, ends, scalars, scales_all, cosine, sine, cond = prepared[:7]
    grad_out, deal, x_own, cot_own = prepared[7:]
    (
        outs_low,
        early_keep,
        early_send,
        late_keep,
        late_send,
        normed_two,
        mids,
        note,
    ) = run_layer(
        images, places, ends, scalars, x_own, cot_own, grad_out, cond, cosine, sine, deal, gathered
    )
    outs_other = swap_mp(outs_low)
    chunks, few = FF // CHUNK, D // CHUNK

    note = note.reshape(2, 8, D)

    def scale_grads(scale_row):
        scale_sum = from_held(scale_row[:HEADS]) / (2.0 * jnp.sqrt(scales_all))
        return lax.dynamic_slice_in_dim(scale_sum, mp_index * heads_here, heads_here, 0)

    if paired:
        out_both = (grad_out, ring.twin(grad_out))
        early_both = (early_keep, ring.twin(early_send))
        two_both = (normed_two, ring.twin(normed_two))
        late_send, mids_send = lax.optimization_barrier(
            (late_send, mids, early_both[1], two_both[1], out_both[1])
        )[:2]
        late_twin, mids_twin = ring.twin(late_send), ring.twin(mids_send)
        grad_fg = weight_grads(
            early_both, (out_both, two_both), ((chunks, 0), (chunks, 1)), here=chunks
        )
        sum_fg = RingSum(ring, grad_fg, mp_index, note)
        hop = sum_fg.step(late_twin, mids_twin)
        grad_rest = weight_grads(
            (after(late_keep, grad_fg), late_twin),
            (two_both, ((mids, 0), (mids_twin, 0)), ((mids, 1), (mids_twin, 1))),
            ((chunks, 0), (few, 1), (3 * few, 2)),
        )
        sum_rest = RingSum(ring, grad_rest, mp_index)
        late_owners = after(owners, grad_fg)[0]
        placed = (late_owners * slots + slots_before(late_owners))[None]
        hop = sum_fg.step(grad_rest)
        sum_rest.step()
        sum_fg.step()
        sum_rest.step()
        sum_fg.step()
        hop = sum_rest.step(outs_other)
        outs_other = after(outs_other, hop)
        notes = pack(sum_fg.notes())
        sum_fg = sum_fg.total()
        notes = [notes, swap_mp(notes)]
        sum_rest.step()
        notes += [ring.twin(note) for note in notes]
        sum_rest = sum_rest.total()
        indices = jnp.stack([mp_index, dp_index]).astype(jnp.int32)
        sum_a, scale_rows = factor_sums(notes, indices, images, mp_count)
        scale_row = scale_rows[0]
        by_kind, outgoing = route(sum_a, sum_fg, sum_rest, placed, slots, dp_count)
        grad_shards = (
            by_kind.reshape(-1, 2, SPAN, D).transpose(0, 2, 1, 3).reshape(unit_count, 2 * D)
        )
        owned = lax.all_to_all(outgoing, "dp", split_axis=0, concat_axis=0, tiled=True)
        owned = owned.reshape(dp_count, 2, slots, D).transpose(2, 0, 1, 3)
        owned_grads = owned.reshape(slots, unit_rows, D).astype(F32)
    else:
        def units_of(parts, field, first, count):
            sides = jnp.stack(
                [weight_grads((part,), ((field,),), ((count, 0),), first) for part in parts]
            )
            sides = sides.reshape(2, mp_count, UNIT // 4, -1, 2, SPAN, D)
            return sides.transpose(1, 3, 5, 2, 0, 4, 6).reshape(mp_count, -1, unit_rows * D)

        early, late = (early_keep, early_send), (late_keep, late_send)
        summed = lax.psum_scatter(
            jnp.concatenate(
                [
                    units_of(late, mids[1], chunks + few, few),
                    units_of(late, mids[1], chunks + 2 * few, few),
                    units_of(late, mids[1], chunks + 3 * few, few),
                    units_of(late, mids[0], chunks, few),
                    units_of(early, normed_two, chunks, chunks),
                    units_of(late, normed_two, 0, chunks),
                    units_of(early, grad_out, 0, chunks),
                ],
                axis=1,
            ),
            "mp",
            scatter_dimension=0,
            tiled=True,
        )[0]
        summed = lax.psum_scatter(summed, "dp", scatter_dimension=1, tiled=True).astype(F32)
        notes = lax.all_gather(note, ("dp", "mp"), axis=0, tiled=True)
        rows = notes.reshape(-1, 16, D)
        count = 2 * images + 1
        wide = add(rows[:, images : images + count], rows[:, images + count : images + 2 * count])
        scale_row = jnp.sum(wide[:, -1], axis=0)
        cond_all = rows[:, :images].reshape(-1, D).astype(F32)
        gains_all = jnp.concatenate(
            [wide[:, place * images : (place + 1) * images].reshape(-1, D) for place in (0, 1)],
            axis=1,
        )
        cond_half = lax.dynamic_slice_in_dim(
            cond_all, mp_index * (D // mp_count), D // mp_count, 1
        )
        sum_a = lax.dot_general(
            cond_half,
            gains_all,
            (((0,), (0,)), ((), ())),
            precision=lax.Precision.HIGHEST,
            preferred_element_type=F32,
        )
        width = unit_rows * D // dp_count

        def piece(field):
            return lax.dynamic_slice_in_dim(
                field.reshape(-1, unit_rows * D), dp_index * width, width, 1
            )

        grad_shards = jnp.concatenate(
            [
                piece(sum_a[:, :D]),
                summed[: 4 * (D // mp_count // unit_rows)],
                piece(sum_a[:, D:]),
                summed[4 * (D // mp_count // unit_rows) :],
            ]
        )

        placed = owners[0] * slots + slots_before(owners[0])
        slot_rows = lax.broadcasted_iota(jnp.int32, (dp_count * slots, unit_count), 0)
        to_owners = (slot_rows == placed[None, :]).astype(BF16)
        outgoing = dot_nn(to_owners, grad_shards.astype(BF16)).astype(BF16)
        owned = lax.all_to_all(outgoing, "dp", split_axis=0, concat_axis=1, tiled=True)
        owned_grads = owned.reshape(slots, unit_rows, D).astype(F32)

    first_new, second_new = moments(moment_one[0], moment_two[0], owned_grads)
    master_new = adam_step(master[0], first_new, second_new, LEARN_RATE)
    outs_both = both_halves(outs_low, outs_other, mp_index, 1)
    output, input_grad = outs_both[0].astype(F32), outs_both[1].astype(F32)
    scale_grad = scale_grads(scale_row)
    scale_first, scale_second = moments(scale_state[1], scale_state[2], scale_grad)
    scale_new = adam_step(scale_state[0], scale_first, scale_second, SCALE_RATE)
    scale_update = jnp.stack([scale_first, scale_new])
    return (
        output,
        input_grad,
        grad_shards[None],
        master_new[None],
        first_new[None],
        second_new[None],
        scale_update,
        scale_second,
    )


def solution(mesh):
    in_specs = (
        P("dp", None),
        P("dp", None),
        P("dp"),
        P("dp", None, None),
        P("dp", None),
        P("mp", None),
        P("mp", "dp", None, None),
        P("mp", "dp", None, None),
        P("mp", "dp", None, None),
        P(None, "mp"),
    )
    out_specs = (
        P("dp", None),
        P("dp", None),
        P("mp", None, "dp"),
        P("mp", "dp", None, None),
        P("mp", "dp", None, None),
        P("mp", "dp", None, None),
        P(None, "mp"),
        P("mp"),
    )
    return jax.shard_map(
        on_device, mesh=mesh, in_specs=in_specs, out_specs=out_specs, check_vma=False
    )
```
